32 devices in a mesh: stream: 4 (over y, x), span: 8 (over z, core).
Axes of the slice: x: 2, y: 2, z: 4, core: 2. Of those that a mesh axis runs over, the one named last changes fastest.
Arguments:
- right_side: float32 [4, 65536], P(None, ('stream', 'span')), may hold values from -5 to 6
- fine_values: float32 [8, 4, 4, 65536], P(None, None, None, ('stream', 'span')), as said below
- fine_columns: int32 [8, 65536], P(None, ('stream', 'span')), may hold values from 0 to 2303, as said below
- fine_sends: int32 [4, 2048], P(None, ('stream', 'span')), may hold values from 0 to 2047, as said below
- fine_order: int32 [32, 2048], P(('stream', 'span')), may hold values from 0 to 2047, each once within a row
- fine_weights: float32 [4, 4, 65536], P(None, None, ('stream', 'span')), may hold values from -0.6 to 1.2
- middle_values: float32 [8, 4, 4, 16384], P(None, None, None, ('stream', 'span')), as said below
- middle_columns: int32 [8, 16384], P(None, ('stream', 'span')), may hold values from 0 to 767, as said below
- middle_sends: int32 [4, 2048], P(None, ('stream', 'span')), may hold values from 0 to 511, as said below
- middle_order: int32 [32, 512], P(('stream', 'span')), may hold values from 0 to 511, each once within a row
- middle_weights: float32 [4, 4, 16384], P(None, None, ('stream', 'span')), may hold values from -0.6 to 1.2
- coarsest_values: float32 [8, 4, 4, 4096], P(None, None, None, ('stream', 'span')), as said below
- coarsest_columns: int32 [8, 4096], P(None, ('stream', 'span')), may hold values from 0 to 1023, as said below
Outputs:
- solution: float32 [4, 65536], P(None, ('stream', 'span'))
- residual: float32 [4, 65536], P(None, ('stream', 'span'))
The draws below stay inside these ranges and needn't reach their ends.
Inputs may be any that keep to these rules, and one draw needn't show every extreme that they name: `fine_sends`: entry [d, p * 64 + s] is a local row block of device p sent in direction d (0: lower stream index, 1: higher stream index, 2: lower span index, 3: higher span index). Each list has a length of at most 64, which differs between devices and directions and is 64 on some device; rows may repeat within a list, and the slots at or after the length repeat the list's slot 0 as padding. `middle_sends`: as for the first level, with local row blocks of the second level. `fine_columns`: block k = 0 of row block n names its own local row. Entries below 2048 are local row blocks; an entry 2048 + e * 64 + s names slot s of halo block e. Where halo block e has a sending device, s is below the length of that device's list; where it has none (the block is zero), s may be any slot below 64. `middle_columns`: as for the first level with 512 local row blocks. `coarsest_columns`: block k = 0 names the row block itself within its slab; the others name row blocks of the same slab. `fine_values`: each diagonal entry of the k = 0 block is 1 or more, and the other 31 entries of its row over all 8 blocks have absolute values summing to at most 0.9 times it. `middle_values`: as for the first level. `coarsest_values`: as for the first level.
All inputs are finite; a program needn't handle non-finite values.
Results may differ from the reference program's by a relative error of at most 0.0003.
Values sent between devices are 32-bit elements; how exact they have to be, the bound alone decides.
No kernel may reach another device: no remote copies, remote signals or barrier semaphores. Data moves between devices by JAX's collectives and lax.ppermute only.
A program may use at most 64 MiB of HBM per device.

```python
import jax
import jax.numpy as jnp
from jax import lax

NNZ = 8
R1 = 2048
KSM = 3
KC = 4
R2 = 512
R3 = 128
H = 64
SLABS = 4
GROUP = 8
DEVS = 32
N1 = 65536
N2 = 16384
N3 = 4096


def halo_counts(key, salt_value):
    sub_key = jax.random.fold_in(key, 40 + salt_value)
    counts = jax.random.randint(sub_key, (DEVS, 4), H // 2, H + 1)
    chosen = jax.random.randint(jax.random.fold_in(sub_key, 1), (), 0, DEVS)
    return jnp.where(jnp.arange(DEVS)[:, None] == chosen, H, counts)


def received_counts(counts):
    device = jnp.arange(DEVS)
    slab_index = device // GROUP
    member = device % GROUP
    from_prev = (slab_index - 1) % SLABS * GROUP + member
    from_next = (slab_index + 1) % SLABS * GROUP + member
    span_prev = slab_index * GROUP + jnp.maximum(member - 1, 0)
    span_next = slab_index * GROUP + jnp.minimum(member + 1, GROUP - 1)
    return jnp.stack([counts[from_prev, 1], counts[from_next, 0], counts[span_prev, 3], counts[span_next, 2]], axis=1)


def send_lists(key, salt_value, row_count):
    counts = halo_counts(key, salt_value)
    raw_rows = jax.random.randint(jax.random.fold_in(key, 60 + salt_value), (DEVS, 4, H), 0, row_count)
    raw_rows = raw_rows.at[:, 0, 0].set(row_count - 1)
    raw_rows = raw_rows.at[:, 0, 1].set(0)
    slot_index = jnp.arange(H)[None, None, :]
    send_table = jnp.where(slot_index < counts[:, :, None], raw_rows, raw_rows[:, :, :1])
    return jnp.transpose(send_table, (1, 0, 2)).reshape(4, DEVS * H).astype(jnp.int32)


def column_lists(key, salt_value, row_count):
    received = received_counts(halo_counts(key, salt_value))
    draw_shape = (NNZ - 1, DEVS, row_count)
    base_key = jax.random.fold_in(key, 80 + salt_value)
    local_rows = jax.random.randint(jax.random.fold_in(base_key, 0), draw_shape, 0, row_count)
    remote_mask = jax.random.randint(jax.random.fold_in(base_key, 1), draw_shape, 0, 4) == 0
    direction = jax.random.randint(jax.random.fold_in(base_key, 2), draw_shape, 0, 4)
    slot_limit = received[jnp.arange(DEVS)[None, :, None], direction]
    slot_index = jax.random.randint(jax.random.fold_in(base_key, 3), draw_shape, 0, slot_limit)
    others = jnp.where(remote_mask, row_count + direction * H + slot_index, local_rows)
    own_rows = jnp.broadcast_to(jnp.arange(row_count)[None, None, :], (1, DEVS, row_count))
    columns = jnp.concatenate([own_rows, others], axis=0).reshape(NNZ, DEVS * row_count)
    columns = columns.at[NNZ - 1, DEVS * row_count - 1].set(row_count + 4 * H - 1)
    return columns.astype(jnp.int32)


def block_values(key, salt_value, total_rows):
    base_key = jax.random.fold_in(key, salt_value)
    row_scale = jnp.exp(jax.random.uniform(jax.random.fold_in(base_key, 0), (4, total_rows), minval=0.0, maxval=jnp.log(10.0)))
    spread = jax.random.uniform(jax.random.fold_in(base_key, 1), (NNZ, 4, 4, total_rows), minval=0.1, maxval=1.0)
    share = jax.random.uniform(jax.random.fold_in(base_key, 2), (4, total_rows), minval=0.86, maxval=0.89)
    block_index = jnp.arange(NNZ)[:, None, None, None]
    row_index = jnp.arange(4)[None, :, None, None]
    col_index = jnp.arange(4)[None, None, :, None]
    on_diagonal = (block_index == 0) & (row_index == col_index)
    spread = jnp.where(on_diagonal, 0.0, spread)
    row_total = jnp.sum(spread, axis=(0, 2))
    scaled = row_scale[None, :, None, :]
    off_part = -(share / row_total)[None, :, None, :] * spread * scaled
    return jnp.where(on_diagonal, scaled, off_part).astype(jnp.float32)


def prolong_weights(key, salt_value, total_rows):
    base_key = jax.random.fold_in(key, 20 + salt_value)
    on_diagonal = (jnp.arange(4)[:, None] == jnp.arange(4)[None, :])[:, :, None]
    rough_part = jnp.clip(0.2 * jax.random.normal(base_key, (4, 4, total_rows)), -0.6, 0.6)
    return (jnp.where(on_diagonal, 0.6, 0.0) + rough_part).astype(jnp.float32)


def draw_right_side(key, part):
    base_key = jax.random.fold_in(key, 7)
    rough_part = jnp.clip(jax.random.normal(base_key, (4, N1)), -5.5, 5.5)
    return (0.5 + rough_part).astype(jnp.float32)


def draw_fine_weights(key, part):
    return prolong_weights(key, 1, N1)


def draw_middle_weights(key, part):
    return prolong_weights(key, 2, N2)


def draw_fine_values(key, part):
    return block_values(key, 1, N1)


def draw_middle_values(key, part):
    return block_values(key, 2, N2)


def draw_coarsest_values(key, part):
    return block_values(key, 3, N3)


def draw_fine_columns(key, part):
    return column_lists(key, 1, R1)


def draw_middle_columns(key, part):
    return column_lists(key, 2, R2)


def draw_fine_sends(key, part):
    return send_lists(key, 1, R1)


def draw_middle_sends(key, part):
    return send_lists(key, 2, R2)


def draw_coarsest_columns(key, part):
    base_key = jax.random.fold_in(key, 95)
    group_rows = GROUP * R3
    own_rows = jnp.arange(N3) % group_rows
    others = jax.random.randint(base_key, (NNZ - 1, N3), 0, group_rows)
    columns = jnp.concatenate([own_rows[None, :], others], axis=0)
    columns = columns.at[NNZ - 1, 0].set(group_rows - 1)
    return columns.astype(jnp.int32)


def setup_inputs(seed: int = 0) -> dict:
    key_of = jax.random.split(jax.random.key(seed), 14)
    right_side = draw_right_side(jax.random.fold_in(key_of[13], 71), 0)
    fine_values = draw_fine_values(jax.random.fold_in(key_of[13], 71), 0)
    fine_columns = draw_fine_columns(jax.random.fold_in(key_of[13], 71), 0)
    fine_sends = draw_fine_sends(jax.random.fold_in(key_of[13], 71), 0)
    fine_order = jax.vmap(lambda own: jax.random.permutation(own, R1))(jax.random.split(key_of[4], DEVS)).reshape((DEVS, R1)).astype(jnp.int32)
    fine_weights = draw_fine_weights(jax.random.fold_in(key_of[13], 71), 0)
    middle_values = draw_middle_values(jax.random.fold_in(key_of[13], 71), 0)
    middle_columns = draw_middle_columns(jax.random.fold_in(key_of[13], 71), 0)
    middle_sends = draw_middle_sends(jax.random.fold_in(key_of[13], 71), 0)
    middle_order = jax.vmap(lambda own: jax.random.permutation(own, R2))(jax.random.split(key_of[9], DEVS)).reshape((DEVS, R2)).astype(jnp.int32)
    middle_weights = draw_middle_weights(jax.random.fold_in(key_of[13], 71), 0)
    coarsest_values = draw_coarsest_values(jax.random.fold_in(key_of[13], 71), 0)
    coarsest_columns = draw_coarsest_columns(jax.random.fold_in(key_of[13], 71), 0)
    return {"right_side": right_side, "fine_values": fine_values, "fine_columns": fine_columns, "fine_sends": fine_sends, "fine_order": fine_order, "fine_weights": fine_weights, "middle_values": middle_values, "middle_columns": middle_columns, "middle_sends": middle_sends, "middle_order": middle_order, "middle_weights": middle_weights, "coarsest_values": coarsest_values, "coarsest_columns": coarsest_columns}


CHEB_CENTRE = 1.0
CHEB_RADIUS = 0.9


def chebyshev(operate, inverse_diag, target, initial, degree):
    sigma_value = CHEB_CENTRE / CHEB_RADIUS
    rho_prev = 1.0 / sigma_value
    if initial is None:
        iterate = jnp.zeros_like(target)
        current = target
    else:
        iterate = initial
        current = target - operate(initial)
    update = inverse_diag * current / CHEB_CENTRE
    iterate = iterate + update
    for _ in range(degree - 1):
        rho_next = 1.0 / (2.0 * sigma_value - rho_prev)
        current = target - operate(iterate)
        update = (rho_next * rho_prev) * update + (2.0 * rho_next / CHEB_RADIUS) * (inverse_diag * current)
        iterate = iterate + update
        rho_prev = rho_next
    return iterate


def inverse_diagonal(values):
    identity = jnp.eye(4, dtype=values.dtype)
    return 1.0 / jnp.sum(values[0] * identity[:, :, None], axis=1)


def global_columns(columns, row_count):
    position = jnp.arange(columns.shape[1], dtype=jnp.int32)
    device = (position // row_count)[None, :]
    inside = device * row_count + columns
    outside = DEVS * row_count + device * (4 * H) + (columns - row_count)
    return jnp.where(columns < row_count, inside, outside).astype(jnp.int32)


def halo_blocks(vector, send_rows, row_count):
    position = jnp.arange(DEVS * H, dtype=jnp.int32)
    sources = ((position // H)[None, :] * row_count + send_rows).astype(jnp.int32)
    outgoing = vector[:, sources].reshape(4, 4, SLABS, GROUP, H)
    from_prev = jnp.roll(outgoing[:, 1], 1, axis=1)
    from_next = jnp.roll(outgoing[:, 0], -1, axis=1)
    zero_row = jnp.zeros_like(outgoing[:, 2, :, :1])
    span_prev = jnp.concatenate([zero_row, outgoing[:, 3, :, :-1]], axis=2)
    span_next = jnp.concatenate([outgoing[:, 2, :, 1:], zero_row], axis=2)
    stacked = jnp.stack([from_prev, from_next, span_prev, span_next], axis=3)
    return stacked.reshape(4, DEVS * 4 * H)


def apply_level(vector, values, wide_cols, send_rows, row_count):
    extended_vec = jnp.concatenate([vector, halo_blocks(vector, send_rows, row_count)], axis=1)
    gathered = extended_vec[:, wide_cols]
    return jnp.einsum("kijn,jkn->in", values, gathered, precision=lax.Precision.HIGHEST)


def global_order(order_rows, row_count):
    return (jnp.arange(DEVS, dtype=jnp.int32)[:, None] * row_count + order_rows).reshape(-1).astype(jnp.int32)


def restrict(fine_vec, weights, positions):
    moved = fine_vec[:, positions]
    moved_weights = weights[:, :, positions]
    summed = jnp.einsum("ijn,in->jn", moved_weights, moved, precision=lax.Precision.HIGHEST)
    return summed.reshape(4, -1, 4).sum(axis=2)


def prolong(coarse, weights, positions):
    spread = jnp.repeat(coarse, 4, axis=1)
    moved_weights = weights[:, :, positions]
    placed = jnp.einsum("ijn,jn->in", moved_weights, spread, precision=lax.Precision.HIGHEST)
    return jnp.zeros_like(placed).at[:, positions].set(placed)


def reference(right_side, fine_values, fine_columns, fine_sends, fine_order, fine_weights, middle_values, middle_columns, middle_sends, middle_order, middle_weights, coarsest_values, coarsest_columns):
    fine_wide = global_columns(fine_columns, R1)
    middle_wide = global_columns(middle_columns, R2)
    group_rows = GROUP * R3
    slab_of = (jnp.arange(N3, dtype=jnp.int32) // group_rows)[None, :]
    coarse_wide = (slab_of * group_rows + coarsest_columns).astype(jnp.int32)

    def fine_apply(vector):
        return apply_level(vector, fine_values, fine_wide, fine_sends, R1)

    def middle_apply(vector):
        return apply_level(vector, middle_values, middle_wide, middle_sends, R2)

    def coarse_apply(vector):
        return jnp.einsum("kijn,jkn->in", coarsest_values, vector[:, coarse_wide], precision=lax.Precision.HIGHEST)

    fine_inv = inverse_diagonal(fine_values)
    middle_inv = inverse_diagonal(middle_values)
    coarse_inv = inverse_diagonal(coarsest_values)
    fine_pos = global_order(fine_order, R1)
    middle_pos = global_order(middle_order, R2)

    first_iter = chebyshev(fine_apply, fine_inv, right_side, None, KSM)
    fine_resid = right_side - fine_apply(first_iter)
    middle_rhs = restrict(fine_resid, fine_weights, fine_pos)
    middle_iter = chebyshev(middle_apply, middle_inv, middle_rhs, None, KSM)
    middle_resid = middle_rhs - middle_apply(middle_iter)
    coarse_rhs = restrict(middle_resid, middle_weights, middle_pos)
    coarse_iter = chebyshev(coarse_apply, coarse_inv, coarse_rhs, None, KC)
    middle_start = middle_iter + prolong(coarse_iter, middle_weights, middle_pos)
    middle_final = chebyshev(middle_apply, middle_inv, middle_rhs, middle_start, KSM)
    fine_start = first_iter + prolong(middle_final, fine_weights, fine_pos)
    solution = chebyshev(fine_apply, fine_inv, right_side, fine_start, KSM)
    residual = right_side - fine_apply(solution)
    return solution, residual
```

```python
import jax
import jax.numpy as jnp
from jax import lax
from jax.experimental import pallas as pl
from jax.experimental.pallas import tpu as pltpu
from jax.sharding import PartitionSpec as P

KSM = 3
KC = 4
NNZ = 8
LANES = 128
SUBS = 8

CHEB_CENTRE = 1.0
CHEB_RADIUS = 0.9
AXES = ("stream", "span")
F32 = jnp.float32
I32 = jnp.int32


def cheb_factors(degree):
    sigma = CHEB_CENTRE / CHEB_RADIUS
    rho = 1.0 / sigma
    factors = [(0.0, 1.0 / CHEB_CENTRE)]
    for _ in range(degree - 1):
        rho_next = 1.0 / (2.0 * sigma - rho)
        factors.append((rho_next * rho, 2.0 * rho_next / CHEB_RADIUS))
        rho = rho_next
    return factors


def tile_iota(dim):
    return lax.broadcasted_iota(I32, (SUBS, LANES), dim)


def pick(line, lane):
    return jnp.take_along_axis(line, lane, axis=1, mode="promise_in_bounds")


def wide(line):
    return jnp.broadcast_to(line, (SUBS, LANES))


def pick_lines(lines, high, lane, first=0):
    result = jnp.zeros((SUBS, LANES), F32)
    for r, line in enumerate(lines):
        result = jnp.where(high == first + r, pick(line, lane), result)
    return result


def halo_lines(arrivals, edge_ref):
    values = [r[...] for r in arrivals]
    prev_s, next_s, prev_p, next_p = [values[d] + values[4 + d] for d in range(4)]
    left = tile_iota(1) < LANES // 2
    upper = tile_iota(0) < 4
    edge_ref[...] = jnp.where(
        upper, jnp.where(left, prev_s, next_s), jnp.where(left, prev_p, next_p)
    )


def outgoing(lines_of, count, sends):
    high, lane = sends >> 7, sends & (LANES - 1)
    return pick_lines([lines_of(r) for r in range(count)], high, lane)


def duplicate(x):
    return x + pltpu.roll(x, 4, 0)


def fine_start(v_ref, b_ref, s_ref, bo_ref, mo_ref, x_ref, out_ref, pad_ref):
    lines = bo_ref.shape[1]
    for i in range(4):
        for h in range(lines // SUBS):
            rows = pl.ds(h * SUBS, SUBS)
            native = pl.ds(h * SUBS * 4 + i, SUBS, stride=4)
            b = b_ref[native, :]
            m = 1.0 / v_ref[pl.ds((i * lines + h * SUBS) * 4 + i, SUBS, stride=4), :]
            x = m * b
            bo_ref[i, rows, :] = b
            mo_ref[i, rows, :] = m
            x_ref[i, rows, :] = x
            for twice in range(2):
                pad_ref[pl.ds((twice * 4 + i) * lines + h * SUBS, SUBS), :] = x
    out_ref[...] = outgoing(
        lambda r: pad_ref[pl.ds(r, SUBS, stride=lines), :], lines, s_ref[...]
    )


def fine_prepare(v_ref, c_ref, _, vo_ref, co_ref):
    lines = vo_ref.shape[3]
    halves = lines // SUBS

    def body(ki, carry):
        k, i = ki // 4, ki % 4
        for j in range(4):
            for h in range(halves):
                start = ki * (lines * 4) + h * SUBS * 4 + j
                vo_ref[k, i, j, pl.ds(h * SUBS, SUBS), :] = v_ref[
                    pl.ds(start, SUBS, stride=4), :
                ]
        return carry

    lax.fori_loop(0, NNZ * 4, body, 0)
    for k in range(NNZ):
        for h in range(halves):
            co_ref[k, pl.ds(h * SUBS, SUBS), :] = c_ref[
                pl.ds(h * SUBS * NNZ + k, SUBS, stride=NNZ), :
            ]


def fine_local(x_ref, b_ref, v_ref, c_ref, r_ref, line_ref):
    lines = x_ref.shape[1]
    halves = lines // SUBS
    for j in range(4):
        for r in range(lines):
            line_ref[j, r] = wide(x_ref[j, pl.ds(r, 1), :])
    acc = []
    for h in range(halves):
        rows = pl.ds(h * SUBS, SUBS)
        for i in range(4):
            total = b_ref[i, rows, :]
            for j in range(4):
                total = total - v_ref[0, i, j, rows, :] * x_ref[j, rows, :]
            acc.append(total)

    def body(k, acc):
        acc = list(acc)
        for h in range(halves):
            rows = pl.ds(h * SUBS, SUBS)
            col = c_ref[k, rows, :]
            high, lane = col >> 7, col & (LANES - 1)
            for j in range(4):
                got = pick_lines([line_ref[j, r] for r in range(lines)], high, lane)
                for i in range(4):
                    acc[4 * h + i] = acc[4 * h + i] - v_ref[k, i, j, rows, :] * got
        return tuple(acc)

    acc = lax.fori_loop(1, NNZ, body, tuple(acc))
    for h in range(halves):
        for i in range(4):
            r_ref[i, pl.ds(h * SUBS, SUBS), :] = acc[4 * h + i]


def fine_remote(arrivals, r_ref, v_ref, c_ref, edge_ref):
    lines = r_ref.shape[1]
    halves = lines // SUBS
    halo_lines(arrivals, edge_ref)
    edges = [[wide(edge_ref[pl.ds(4 * e + j, 1), :]) for e in range(2)] for j in range(4)]
    result = []
    for h in range(halves):
        rows = pl.ds(h * SUBS, SUBS)
        acc = [r_ref[i, rows, :] for i in range(4)]
        for k in range(1, NNZ):
            col = c_ref[k, rows, :]
            high, lane = col >> 7, col & (LANES - 1)
            for j in range(4):
                got = pick_lines(edges[j], high, lane, lines)
                for i in range(4):
                    acc[i] = acc[i] - v_ref[k, i, j, rows, :] * got
        result.append(acc)
    return result


def fine_step(factors, *refs):
    arrivals = refs[:8]
    (r_ref, v_ref, c_ref, m_ref, x_ref, d_ref, s_ref, xo_ref, do_ref, out_ref, edge_ref, pad_ref) = refs[8:]
    keep, gain = factors
    lines = r_ref.shape[1]
    resid = fine_remote(arrivals, r_ref, v_ref, c_ref, edge_ref)
    for h in range(lines // SUBS):
        rows = pl.ds(h * SUBS, SUBS)
        for i in range(4):
            d = gain * (m_ref[i, rows, :] * resid[h][i])
            if keep:
                d = keep * d_ref[i, rows, :] + d
            x = x_ref[i, rows, :] + d
            do_ref[i, rows, :] = d
            xo_ref[i, rows, :] = x
            for twice in range(2):
                pad_ref[pl.ds((twice * 4 + i) * lines + h * SUBS, SUBS), :] = x
    out_ref[...] = outgoing(
        lambda r: pad_ref[pl.ds(r, SUBS, stride=lines), :], lines, s_ref[...]
    )


def fine_finish(*refs):
    arrivals = refs[:8]
    r_ref, v_ref, c_ref, x_ref, so_ref, ro_ref, edge_ref = refs[8:]
    lines = r_ref.shape[1]
    resid = fine_remote(arrivals, r_ref, v_ref, c_ref, edge_ref)
    for h in range(lines // SUBS):
        for i in range(4):
            native = pl.ds(h * SUBS * 4 + i, SUBS, stride=4)
            so_ref[native, :] = x_ref[i, pl.ds(h * SUBS, SUBS), :]
            ro_ref[native, :] = resid[h][i]


def fine_restrict(*refs):
    arrivals = refs[:8]
    (r_ref, v_ref, c_ref, w_ref, p_ref, m2_ref, s2_ref, b2_ref, x2_ref, out_ref, edge_ref, line_ref, pad_ref) = refs[8:]
    lines = r_ref.shape[1]
    resid = fine_remote(arrivals, r_ref, v_ref, c_ref, edge_ref)
    for h in range(lines // SUBS):
        rows = pl.ds(h * SUBS, SUBS)
        for j in range(4):
            total = w_ref[0, j, rows, :] * resid[h][0]
            for i in range(1, 4):
                total = total + w_ref[i, j, rows, :] * resid[h][i]
            line_ref[j, rows, :] = total
    for j in range(4):
        total = None
        source = [wide(line_ref[j, pl.ds(r, 1), :]) for r in range(lines)]
        for part in range(2):
            place = p_ref[part]
            got = pick_lines(source, place >> 7, place & (LANES - 1))
            total = got if total is None else total + got
        b2 = duplicate(total)
        x2 = m2_ref[j] * b2
        b2_ref[j] = b2
        x2_ref[j] = x2
        middle_pad(pad_ref, j, x2)
    middle_out(out_ref, pad_ref, s2_ref)


def inverse_order(o_row, lines):
    count = lines * LANES
    high, lane = o_row >> 7, o_row & (LANES - 1)
    coarse = lax.broadcasted_iota(I32, (1, count), 1) >> 2
    here = lax.broadcasted_iota(I32, (lines, count), 0) == high
    upper = jnp.where(here, (coarse >> 4).astype(F32), 0.0)
    lower = jnp.where(here, (coarse & 15).astype(F32), 0.0)
    left = jnp.concatenate([upper, lower], axis=0).astype(jnp.bfloat16)
    right = jnp.where(
        lax.broadcasted_iota(I32, (LANES, count), 0) == lane, 1.0, 0.0
    ).astype(jnp.bfloat16)
    found = lax.dot_general(
        left, right, (((1,), (1,)), ((), ())), preferred_element_type=F32
    )
    return (found[:lines] * 16.0 + found[lines:]).astype(I32)


def pick_order(sources, unit):
    lane = tile_iota(1)
    place = 4 * (lane & 31) + unit
    result = jnp.zeros((SUBS, LANES), I32)
    for q, source in enumerate(sources):
        result = jnp.where((lane >> 5) == q, pick(source, place), result)
    return result


def fine_tables(w_ref, row_ref, o_ref, _, wo_ref, agg_ref, place_ref):
    lines = o_ref.shape[0]
    for i in range(4):
        for j in range(4):
            for h in range(lines // SUBS):
                start = (i * lines + h * SUBS) * 4 + j
                wo_ref[i, j, pl.ds(h * SUBS, SUBS), :] = w_ref[pl.ds(start, SUBS, stride=4), :]
    agg_ref[...] = inverse_order(row_ref[...], lines)
    sources = []
    for q in range(4):
        four = o_ref[pl.ds(q, 4, stride=4), :]
        sources.append(jnp.concatenate([four, four], axis=0))
    for part in range(2):
        place_ref[part] = pick_order(sources, (tile_iota(0) >> 2) + 2 * part)


def middle_tables(v_ref, c_ref, w_ref, row_ref, o_ref, _, vo_ref, co_ref, mo_ref, wo_ref, agg_ref, place_ref):
    lines = o_ref.shape[0]

    def body(ki, carry):
        k, i = ki // 4, ki % 4
        kp, i2 = ki // 4, ki % 4
        for j in range(4):
            for odd in range(2):
                start = ((2 * kp + odd) * 4 + i2) * (lines * 4) + j
                vo_ref[k, i, j, pl.ds(4 * odd, 4), :] = v_ref[pl.ds(start, 4, stride=4), :]
        return carry

    lax.fori_loop(0, NNZ // 2 * 4, body, 0)
    for kp in range(NNZ // 2):
        for odd in range(2):
            co_ref[kp, pl.ds(4 * odd, 4), :] = c_ref[pl.ds(2 * kp + odd, 4, stride=NNZ), :]
    for i in range(4):
        four = 1.0 / v_ref[pl.ds(i * lines * 4 + i, 4, stride=4), :]
        mo_ref[i, pl.ds(0, 4), :] = four
        mo_ref[i, pl.ds(4, 4), :] = four
        for j in range(4):
            four = w_ref[pl.ds(i * lines * 4 + j, 4, stride=4), :]
            wo_ref[i, j, pl.ds(0, 4), :] = four
            wo_ref[i, j, pl.ds(4, 4), :] = four
    agg = inverse_order(row_ref[...], lines)
    agg_ref[...] = jnp.concatenate([agg, agg], axis=0)
    sources = [wide(o_ref[pl.ds(q, 1), :]) for q in range(4)]
    place_ref[...] = pick_order(sources, tile_iota(0) & 3)


def middle_pad(pad_ref, j, x):
    for twice in range(2):
        pad_ref[pl.ds((twice * 4 + j) * SUBS, SUBS), :] = x


def middle_out(out_ref, pad_ref, s_ref):
    out_ref[...] = outgoing(
        lambda r: pad_ref[pl.ds(r, SUBS, stride=SUBS), :], 4, s_ref[...]
    )


def middle_residual(arrivals, b_ref, x_ref, v_ref, c_ref, edge_ref):
    halo_lines(arrivals, edge_ref)
    acc = [jnp.zeros((SUBS, LANES), F32) for _ in range(4)]
    for j in range(4):
        source = [wide(x_ref[j, pl.ds(r, 1), :]) for r in range(4)]
        source += [wide(edge_ref[pl.ds(4 * e + j, 1), :]) for e in range(2)]
        for kp in range(NNZ // 2):
            col = c_ref[kp]
            got = pick_lines(source, col >> 7, col & (LANES - 1))
            for i in range(4):
                acc[i] = acc[i] + v_ref[kp, i, j] * got
    return [b_ref[i] - duplicate(acc[i]) for i in range(4)]


def middle_update(factors, resid, m_ref, x_ref, d_ref):
    keep, gain = factors
    xs, ds = [], []
    for i in range(4):
        d = gain * (m_ref[i] * resid[i])
        if keep:
            d = keep * d_ref[i] + d
        ds.append(d)
        xs.append(x_ref[i] + d)
    return xs, ds


def middle_step(factors, *refs):
    arrivals = refs[:8]
    (b_ref, m_ref, x_ref, d_ref, v_ref, c_ref, s_ref, xo_ref, do_ref, out_ref, edge_ref, pad_ref) = refs[8:]
    resid = middle_residual(arrivals, b_ref, x_ref, v_ref, c_ref, edge_ref)
    xs, ds = middle_update(factors, resid, m_ref, x_ref, d_ref)
    for i in range(4):
        xo_ref[i] = xs[i]
        do_ref[i] = ds[i]
        middle_pad(pad_ref, i, xs[i])
    middle_out(out_ref, pad_ref, s_ref)


def middle_restrict(*refs):
    arrivals = refs[:8]
    b_ref, x_ref, v_ref, c_ref, w_ref, p_ref, out_ref, edge_ref, line_ref = refs[8:]
    resid = middle_residual(arrivals, b_ref, x_ref, v_ref, c_ref, edge_ref)
    place = p_ref[...]
    high, lane = place >> 7, place & (LANES - 1)
    for j in range(4):
        total = w_ref[0, j] * resid[0]
        for i in range(1, 4):
            total = total + w_ref[i, j] * resid[i]
        line_ref[j] = total
        source = [wide(line_ref[j, pl.ds(r, 1), :]) for r in range(4)]
        got = pick_lines(source, high, lane)
        got = got + pltpu.roll(got, 2, 0)
        got = got + pltpu.roll(got, 1, 0)
        out_ref[pl.ds(j, 1), :] = got[0:1]
        out_ref[pl.ds(4 + j, 1), :] = got[0:1]


def middle_prolong(factors, *refs):
    arrivals = refs[:8]
    (b_ref, m_ref, x_ref, d_ref, v_ref, c_ref, x1_ref, w_ref, agg_ref, s_ref, xo_ref, out_ref, edge_ref, line_ref, pad_ref) = refs[8:]
    lines = x1_ref.shape[1]
    resid = middle_residual(arrivals, b_ref, x_ref, v_ref, c_ref, edge_ref)
    xs, _ = middle_update(factors, resid, m_ref, x_ref, d_ref)
    for j in range(4):
        line_ref[j] = xs[j]
    for h in range(lines // SUBS):
        rows = pl.ds(h * SUBS, SUBS)
        agg = agg_ref[rows, :]
        high, lane = agg >> 7, agg & (LANES - 1)
        spread = [
            pick_lines([wide(line_ref[j, pl.ds(r, 1), :]) for r in range(4)], high, lane)
            for j in range(4)
        ]
        for i in range(4):
            placed = w_ref[i, 0, rows, :] * spread[0]
            for j in range(1, 4):
                placed = placed + w_ref[i, j, rows, :] * spread[j]
            x = x1_ref[i, rows, :] + placed
            xo_ref[i, rows, :] = x
            for twice in range(2):
                pad_ref[pl.ds((twice * 4 + i) * lines + h * SUBS, SUBS), :] = x
    out_ref[...] = outgoing(
        lambda r: pad_ref[pl.ds(r, SUBS, stride=lines), :], lines, s_ref[...]
    )


def coarse_half(half, *refs):
    for t in range(half):
        refs[2 * half + 1][t] = refs[t][...] + refs[half + t][...]
    for t in range(1, half):
        refs[2 * half + 2][t - 1] = refs[t][...] + refs[half + t][...]


def coarse_tables(group, *refs):
    half = group // 2
    own_ref, me_ref = refs[0], refs[1]
    odd = refs[2]
    even = refs[3:5]
    vo_ref, co_ref, mo_ref, pad_ref = refs[6:]
    pad_ref[0] = own_ref[...]
    for t in range(half):
        pad_ref[2 * t + 1] = odd[t]
    for t in range(half - 1):
        pad_ref[2 * t + 2] = even[0][t] + even[1][t]
    me = me_ref[0]
    for h in range(group // SUBS):
        rows = pl.ds(h * SUBS, SUBS)
        for ki in range(NNZ * 4):
            k, i = ki // 4, ki % 4
            for j in range(4):
                tile = pad_ref[rows, ki * 4 + j, :]
                vo_ref[k, i, j, rows, :] = tile
                if k == 0 and i == j:
                    mo_ref[i, rows, :] = 1.0 / tile
        for k in range(NNZ):
            col = pad_ref[rows, NNZ * 16 + k, :].astype(I32)
            co_ref[k, rows, :] = ((col >> 7) ^ me) * LANES + (col & (LANES - 1))


def coarse_solve(group, *refs):
    half = group // 2
    own_ref = refs[0]
    odd = refs[1 : 1 + 2 * half]
    even = refs[1 + 2 * half : 3 + 2 * half]
    (v_ref, c_ref, m_ref, x2_ref, w_ref, agg_ref, s_ref, xo_ref, out_ref, b_ref, x_ref, d_ref, tmp_ref, pad_ref) = refs[3 + 2 * half :]
    for j in range(4):
        b_ref[j, pl.ds(0, 1), :] = own_ref[pl.ds(j, 1), :]
    for t in range(half):
        tmp_ref[...] = odd[t][...] + odd[half + t][...]
        for j in range(4):
            b_ref[j, pl.ds(2 * t + 1, 1), :] = tmp_ref[pl.ds(j, 1), :]
    for t in range(half - 1):
        tmp_ref[...] = even[0][t] + even[1][t]
        for j in range(4):
            b_ref[j, pl.ds(2 * t + 2, 1), :] = tmp_ref[pl.ds(j, 1), :]
    blocks = group // SUBS
    for j in range(4):
        first = m_ref[j] * b_ref[j]
        x_ref[j] = first
        d_ref[j] = first
    for keep, gain in cheb_factors(KC)[1:]:
        resid = []
        for h in range(blocks):
            rows = pl.ds(h * SUBS, SUBS)
            acc = [b_ref[i, rows, :] for i in range(4)]
            for k in range(NNZ):
                col = c_ref[k, rows, :]
                high, lane = col >> 7, col & (LANES - 1)
                for j in range(4):
                    if k:
                        got = pick_lines(
                            [wide(x_ref[j, pl.ds(r, 1), :]) for r in range(group)], high, lane
                        )
                    else:
                        got = x_ref[j, rows, :]
                    for i in range(4):
                        acc[i] = acc[i] - v_ref[k, i, j, rows, :] * got
            resid.append(acc)
        for h in range(blocks):
            rows = pl.ds(h * SUBS, SUBS)
            for i in range(4):
                d = keep * d_ref[i, rows, :] + gain * (m_ref[i, rows, :] * resid[h][i])
                d_ref[i, rows, :] = d
                x_ref[i, rows, :] = x_ref[i, rows, :] + d
    lane = agg_ref[...]
    spread = [pick(wide(x_ref[j, pl.ds(0, 1), :]), lane) for j in range(4)]
    for i in range(4):
        x = x2_ref[i]
        for j in range(4):
            x = x + w_ref[i, j] * spread[j]
        xo_ref[i] = x
        middle_pad(pad_ref, i, x)
    middle_out(out_ref, pad_ref, s_ref)


def call(body, outs, args, scratch=(), free=(), smem=()):
    specs = []
    for index in range(len(args)):
        if index in free:
            specs.append(pl.BlockSpec(memory_space=pl.ANY))
        elif index in smem:
            specs.append(pl.BlockSpec(memory_space=pltpu.SMEM))
        else:
            specs.append(pl.BlockSpec(memory_space=pltpu.VMEM))
    single = not isinstance(outs, (list, tuple))
    shapes = [outs] if single else list(outs)
    result = pl.pallas_call(
        body,
        out_shape=shapes,
        in_specs=specs,
        out_specs=[pl.BlockSpec(memory_space=pltpu.VMEM) for _ in shapes],
        scratch_shapes=list(scratch),
        compiler_params=pltpu.CompilerParams(vmem_limit_bytes=16 * 2**20),
    )(*args)
    return result[0] if single else result


def shape(*dims, dtype=F32):
    return jax.ShapeDtypeStruct(dims, dtype)


def vmem(*dims, dtype=F32):
    return pltpu.VMEM(dims, dtype)


def native_rows(x):
    lines = x.shape[-1] // LANES
    split = x.reshape(x.shape[:-1] + (lines, LANES))
    return jnp.swapaxes(split, -2, -3).reshape(-1, LANES)


def from_native(rows, lines):
    return jnp.swapaxes(rows.reshape(lines, 4, LANES), 0, 1).reshape(4, lines * LANES)


def send_table(sends):
    stream = jnp.concatenate([sends[1], sends[0]])[None]
    span = jnp.concatenate([sends[3], sends[2]])[None]
    return jnp.concatenate([stream] * 4 + [span] * 4, axis=0)


def colour_of(mesh):
    count = mesh.shape["span"]
    return lambda p: (p // count + p % count) % 2


def exchange(mesh, out):
    slabs, count = mesh.shape["stream"], mesh.shape["span"]
    colour = colour_of(mesh)
    places = [(a, b) for a in range(slabs) for b in range(count)]
    moves = []
    for da, db in ((1, 0), (-1, 0), (0, 1), (0, -1)):
        moves.append(
            [
                (a * count + b, (a + da) % slabs * count + b + db)
                for a, b in places
                if 0 <= b + db < count
            ]
        )
    return [
        lax.ppermute(out, AXES, [pair for pair in move if colour(pair[0]) == side])
        for side in range(2)
        for move in moves
    ]


def span_swaps(mesh, value, masks, in_turn=False):
    slabs, count = mesh.shape["stream"], mesh.shape["span"]
    colour = colour_of(mesh)
    places = [(a, b) for a in range(slabs) for b in range(count)]

    def one_side(value, side):
        return [
            lax.ppermute(
                value,
                AXES,
                [
                    (a * count + b, a * count + (b ^ mask))
                    for a, b in places
                    if colour(a * count + b) == side
                ],
            )
            for mask in masks
        ]

    first = one_side(value, 1)
    if in_turn:
        value, first = lax.optimization_barrier((value, first))
    return one_side(value, 0) + first


def span_gather(mesh, value):
    half = mesh.shape["span"] // 2
    odd = span_swaps(mesh, value, range(1, 2 * half, 2), True)
    held = jnp.stack([odd[t] + odd[half + t] for t in range(1, half)])
    even = span_swaps(mesh, held, (1,))
    return odd, even


def per_device(mesh, right_side, fine_values, fine_columns, fine_sends, fine_order, fine_weights, middle_values, middle_columns, middle_sends, middle_order, middle_weights, coarsest_values, coarsest_columns):
    group = mesh.shape["span"]
    lines = right_side.shape[1] // LANES
    tile = shape(SUBS, LANES)
    vec1 = shape(4, lines, LANES)
    vec2 = shape(4, SUBS, LANES)
    edge = vmem(SUBS, LANES)
    pad1 = vmem(SUBS * lines, LANES)
    pad2 = vmem(SUBS * SUBS, LANES)
    factors = cheb_factors(KSM)
    send1, send2 = send_table(fine_sends), send_table(middle_sends)
    values1 = native_rows(fine_values)
    values2 = native_rows(middle_values)

    b1, m1, x1, out = call(
        fine_start,
        [vec1, vec1, vec1, tile],
        [native_rows(fine_values[0]), native_rows(right_side), send1],
        [pad1],
    )
    d1 = x1

    own3 = jnp.concatenate(
        [coarsest_values.reshape(NNZ * 16, LANES), coarsest_columns.astype(F32)], axis=0
    )
    v1, c1 = call(
        fine_prepare,
        [shape(NNZ, 4, 4, lines, LANES), shape(NNZ, lines, LANES, dtype=I32)],
        [values1, native_columns(fine_columns), out],
        free=(2,),
    )

    def fine_part(x):
        return call(fine_local, vec1, [x, b1, v1, c1], [vmem(4, lines, SUBS, LANES)])

    def fine_next(which, arrived, resid, x, d, after=()):
        args = arrived + [resid, v1, c1, m1, x, d, send1]
        return call(
            lambda *refs: fine_step(factors[which], *(refs[: len(args)] + refs[len(args) + len(after) :])),
            [vec1, vec1, tile],
            args + list(after),
            [edge, pad1],
            free=range(len(args), len(args) + len(after)),
        )

    arrived = exchange(mesh, out)
    own3, _ = lax.optimization_barrier((own3, out))
    swapped3 = span_swaps(mesh, own3, range(1, group, 2))
    resid = fine_part(x1)
    x1, d1, out = fine_next(1, arrived, resid, x1, d1)

    arrived = exchange(mesh, out)
    half = group // 2
    odd3, held3 = call(
        lambda *refs: coarse_half(half, *refs),
        [shape(half, NNZ * 17, LANES), shape(half - 1, NNZ * 17, LANES)],
        swapped3 + [out],
        free=(group,),
    )
    even3 = span_swaps(mesh, held3, (1,))
    resid = fine_part(x1)
    w1, agg1, place1 = call(
        fine_tables,
        [shape(4, 4, lines, LANES), shape(lines, LANES, dtype=I32), shape(2, SUBS, LANES, dtype=I32)],
        [native_rows(fine_weights), fine_order, fine_order.reshape(lines, LANES), out],
        free=(3,),
    )
    x1, d1, out = fine_next(2, arrived, resid, x1, d1, [held3])

    arrived = exchange(mesh, out)
    resid = fine_part(x1)
    v2, c2, m2, w2, agg2, place2 = call(
        middle_tables,
        [
            shape(NNZ // 2, 4, 4, SUBS, LANES),
            shape(NNZ // 2, SUBS, LANES, dtype=I32),
            vec2,
            shape(4, 4, SUBS, LANES),
            shape(SUBS, LANES, dtype=I32),
            shape(SUBS, LANES, dtype=I32),
        ],
        [values2, native_columns(middle_columns), native_rows(middle_weights), middle_order, middle_order.reshape(-1, LANES), out],
        free=(5,),
    )
    b2, x2, out = call(
        fine_restrict,
        [vec2, vec2, tile],
        arrived + [resid, v1, c1, w1, place1, m2, send2],
        [edge, vmem(4, lines, LANES), pad2],
    )
    d2 = x2

    def middle_next(which, arrived, x, d, after=()):
        args = arrived + [b2, m2, x, d, v2, c2, send2]
        return call(
            lambda *refs: middle_step(factors[which], *(refs[: len(args)] + refs[len(args) + len(after) :])),
            [vec2, vec2, tile],
            args + list(after),
            [edge, pad2],
            free=range(len(args), len(args) + len(after)),
        )

    arrived = exchange(mesh, out)
    me = lax.axis_index("span").astype(I32).reshape(1)
    v3, c3, m3 = call(
        lambda *refs: coarse_tables(group, *refs),
        [shape(NNZ, 4, 4, group, LANES), shape(NNZ, group, LANES, dtype=I32), shape(4, group, LANES)],
        [own3, me, odd3] + even3 + [out],
        [vmem(group, NNZ * 17, LANES)],
        free=(5,),
        smem=(1,),
    )
    x2, d2, out = middle_next(1, arrived, x2, d2, [m3])
    arrived = exchange(mesh, out)
    x2, d2, out = middle_next(2, arrived, x2, d2)
    arrived = exchange(mesh, out)
    rhs3 = call(
        middle_restrict,
        tile,
        arrived + [b2, x2, v2, c2, w2, place2],
        [edge, vmem(4, SUBS, LANES)],
    )
    odd, even = span_gather(mesh, rhs3)
    vec3 = vmem(4, group, LANES)
    x2, out = call(
        lambda *refs: coarse_solve(group, *refs),
        [vec2, tile],
        [rhs3] + odd + even + [v3, c3, m3, x2, w2, agg2, send2],
        [vec3, vec3, vec3, edge, pad2],
    )
    arrived = exchange(mesh, out)
    x2, d2, out = middle_next(0, arrived, x2, x2)
    arrived = exchange(mesh, out)
    x2, d2, out = middle_next(1, arrived, x2, d2)
    arrived = exchange(mesh, out)
    x1, out = call(
        lambda *refs: middle_prolong(factors[2], *refs),
        [vec1, tile],
        arrived + [b2, m2, x2, d2, v2, c2, x1, w1, agg1, send1],
        [edge, vmem(4, SUBS, LANES), pad1],
    )
    for which in range(KSM):
        arrived = exchange(mesh, out)
        resid = fine_part(x1)
        x1, d1, out = fine_next(which, arrived, resid, x1, d1)
    arrived = exchange(mesh, out)
    resid = fine_part(x1)
    rows = shape(4 * lines, LANES)
    solved, left = call(fine_finish, [rows, rows], arrived + [resid, v1, c1, x1], [edge])
    return from_native(solved, lines), from_native(left, lines)


def native_columns(columns):
    lines = columns.shape[1] // LANES
    return jnp.swapaxes(columns.reshape(NNZ, lines, LANES), 0, 1).reshape(-1, LANES)


def solution(mesh):
    both = ("stream", "span")
    in_specs = (
        P(None, both),
        P(None, None, None, both),
        P(None, both),
        P(None, both),
        P(both, None),
        P(None, None, both),
        P(None, None, None, both),
        P(None, both),
        P(None, both),
        P(both, None),
        P(None, None, both),
        P(None, None, None, both),
        P(None, both),
    )
    return jax.shard_map(
        lambda *args: per_device(mesh, *args),
        mesh=mesh,
        in_specs=in_specs,
        out_specs=(P(None, both), P(None, both)),
        check_vma=False,
    )
```

```python
import jax
import jax.numpy as jnp
from jax import lax
from jax.experimental import pallas as pl
from jax.experimental.pallas import tpu as pltpu
from jax.sharding import PartitionSpec as P

KSM = 3
KC = 4
NNZ = 8
LANES = 128
SUBS = 8

CHEB_CENTRE = 1.0
CHEB_RADIUS = 0.9
AXES = ("stream", "span")
F32 = jnp.float32
I32 = jnp.int32


def cheb_factors(degree):
    sigma = CHEB_CENTRE / CHEB_RADIUS
    rho = 1.0 / sigma
    factors = [(0.0, 1.0 / CHEB_CENTRE)]
    for _ in range(degree - 1):
        rho_next = 1.0 / (2.0 * sigma - rho)
        factors.append((rho_next * rho, 2.0 * rho_next / CHEB_RADIUS))
        rho = rho_next
    return factors


def tile_iota(dim):
    return lax.broadcasted_iota(I32, (SUBS, LANES), dim)


def pick(line, lane):
    return jnp.take_along_axis(line, lane, axis=1, mode="promise_in_bounds")


def wide(line):
    return jnp.broadcast_to(line, (SUBS, LANES))


def pick_lines(lines, high, lane, first=0):
    result = jnp.zeros((SUBS, LANES), F32)
    for r, line in enumerate(lines):
        result = jnp.where(high == first + r, pick(line, lane), result)
    return result


def halo_lines(arrivals, edge_ref):
    prev_s, next_s, prev_p, next_p, inside = [r[...] for r in arrivals]
    left = tile_iota(1) < LANES // 2
    upper = tile_iota(0) < 4
    values = jnp.where(
        upper, jnp.where(left, prev_s, next_s), jnp.where(left, prev_p, next_p)
    )
    edge_ref[...] = jnp.where(inside > 0.0, values, 0.0)


def outgoing(lines_of, count, sends):
    high, lane = sends >> 7, sends & (LANES - 1)
    return pick_lines([lines_of(r) for r in range(count)], high, lane)


def duplicate(x):
    return x + pltpu.roll(x, 4, 0)


def fine_start(v_ref, b_ref, s_ref, bo_ref, mo_ref, x_ref, out_ref, pad_ref):
    lines = bo_ref.shape[1]
    for i in range(4):
        for h in range(lines // SUBS):
            rows = pl.ds(h * SUBS, SUBS)
            native = pl.ds(h * SUBS * 4 + i, SUBS, stride=4)
            b = b_ref[native, :]
            m = 1.0 / v_ref[pl.ds((i * lines + h * SUBS) * 4 + i, SUBS, stride=4), :]
            x = m * b
            bo_ref[i, rows, :] = b
            mo_ref[i, rows, :] = m
            x_ref[i, rows, :] = x
            for twice in range(2):
                pad_ref[pl.ds((twice * 4 + i) * lines + h * SUBS, SUBS), :] = x
    out_ref[...] = outgoing(
        lambda r: pad_ref[pl.ds(r, SUBS, stride=lines), :], lines, s_ref[...]
    )


def fine_prepare(v_ref, c_ref, _, vo_ref, co_ref):
    lines = vo_ref.shape[3]
    halves = lines // SUBS

    def body(ki, carry):
        k, i = ki // 4, ki % 4
        for j in range(4):
            for h in range(halves):
                start = ki * (lines * 4) + h * SUBS * 4 + j
                vo_ref[k, i, j, pl.ds(h * SUBS, SUBS), :] = v_ref[
                    pl.ds(start, SUBS, stride=4), :
                ]
        return carry

    lax.fori_loop(0, NNZ * 4, body, 0)
    for k in range(NNZ):
        for h in range(halves):
            co_ref[k, pl.ds(h * SUBS, SUBS), :] = c_ref[
                pl.ds(h * SUBS * NNZ + k, SUBS, stride=NNZ), :
            ]


def fine_local(x_ref, b_ref, v_ref, c_ref, r_ref, line_ref):
    lines = x_ref.shape[1]
    halves = lines // SUBS
    for j in range(4):
        for r in range(lines):
            line_ref[j, r] = wide(x_ref[j, pl.ds(r, 1), :])
    acc = []
    for h in range(halves):
        rows = pl.ds(h * SUBS, SUBS)
        for i in range(4):
            total = b_ref[i, rows, :]
            for j in range(4):
                total = total - v_ref[0, i, j, rows, :] * x_ref[j, rows, :]
            acc.append(total)

    def body(k, acc):
        acc = list(acc)
        for h in range(halves):
            rows = pl.ds(h * SUBS, SUBS)
            col = c_ref[k, rows, :]
            high, lane = col >> 7, col & (LANES - 1)
            for j in range(4):
                got = pick_lines([line_ref[j, r] for r in range(lines)], high, lane)
                for i in range(4):
                    acc[4 * h + i] = acc[4 * h + i] - v_ref[k, i, j, rows, :] * got
        return tuple(acc)

    acc = lax.fori_loop(1, NNZ, body, tuple(acc))
    for h in range(halves):
        for i in range(4):
            r_ref[i, pl.ds(h * SUBS, SUBS), :] = acc[4 * h + i]


def fine_remote(arrivals, r_ref, v_ref, c_ref, edge_ref):
    lines = r_ref.shape[1]
    halves = lines // SUBS
    halo_lines(arrivals, edge_ref)
    edges = [[wide(edge_ref[pl.ds(4 * e + j, 1), :]) for e in range(2)] for j in range(4)]
    result = []
    for h in range(halves):
        rows = pl.ds(h * SUBS, SUBS)
        acc = [r_ref[i, rows, :] for i in range(4)]
        for k in range(1, NNZ):
            col = c_ref[k, rows, :]
            high, lane = col >> 7, col & (LANES - 1)
            for j in range(4):
                got = pick_lines(edges[j], high, lane, lines)
                for i in range(4):
                    acc[i] = acc[i] - v_ref[k, i, j, rows, :] * got
        result.append(acc)
    return result


def fine_step(factors, *refs):
    arrivals = refs[:5]
    (r_ref, v_ref, c_ref, m_ref, x_ref, d_ref, s_ref, xo_ref, do_ref, out_ref, edge_ref, pad_ref) = refs[5:]
    keep, gain = factors
    lines = r_ref.shape[1]
    resid = fine_remote(arrivals, r_ref, v_ref, c_ref, edge_ref)
    for h in range(lines // SUBS):
        rows = pl.ds(h * SUBS, SUBS)
        for i in range(4):
            d = gain * (m_ref[i, rows, :] * resid[h][i])
            if keep:
                d = keep * d_ref[i, rows, :] + d
            x = x_ref[i, rows, :] + d
            do_ref[i, rows, :] = d
            xo_ref[i, rows, :] = x
            for twice in range(2):
                pad_ref[pl.ds((twice * 4 + i) * lines + h * SUBS, SUBS), :] = x
    out_ref[...] = outgoing(
        lambda r: pad_ref[pl.ds(r, SUBS, stride=lines), :], lines, s_ref[...]
    )


def fine_finish(*refs):
    arrivals = refs[:5]
    r_ref, v_ref, c_ref, x_ref, so_ref, ro_ref, edge_ref = refs[5:]
    lines = r_ref.shape[1]
    resid = fine_remote(arrivals, r_ref, v_ref, c_ref, edge_ref)
    for h in range(lines // SUBS):
        for i in range(4):
            native = pl.ds(h * SUBS * 4 + i, SUBS, stride=4)
            so_ref[native, :] = x_ref[i, pl.ds(h * SUBS, SUBS), :]
            ro_ref[native, :] = resid[h][i]


def fine_restrict(*refs):
    arrivals = refs[:5]
    (r_ref, v_ref, c_ref, w_ref, p_ref, m2_ref, s2_ref, b2_ref, x2_ref, out_ref, edge_ref, line_ref, pad_ref) = refs[5:]
    lines = r_ref.shape[1]
    resid = fine_remote(arrivals, r_ref, v_ref, c_ref, edge_ref)
    for h in range(lines // SUBS):
        rows = pl.ds(h * SUBS, SUBS)
        for j in range(4):
            total = w_ref[0, j, rows, :] * resid[h][0]
            for i in range(1, 4):
                total = total + w_ref[i, j, rows, :] * resid[h][i]
            line_ref[j, rows, :] = total
    for j in range(4):
        total = None
        source = [wide(line_ref[j, pl.ds(r, 1), :]) for r in range(lines)]
        for part in range(2):
            place = p_ref[part]
            got = pick_lines(source, place >> 7, place & (LANES - 1))
            total = got if total is None else total + got
        b2 = duplicate(total)
        x2 = m2_ref[j] * b2
        b2_ref[j] = b2
        x2_ref[j] = x2
        middle_pad(pad_ref, j, x2)
    middle_out(out_ref, pad_ref, s2_ref)


def inverse_order(o_row, lines):
    count = lines * LANES
    high, lane = o_row >> 7, o_row & (LANES - 1)
    coarse = lax.broadcasted_iota(I32, (1, count), 1) >> 2
    here = lax.broadcasted_iota(I32, (lines, count), 0) == high
    upper = jnp.where(here, (coarse >> 4).astype(F32), 0.0)
    lower = jnp.where(here, (coarse & 15).astype(F32), 0.0)
    left = jnp.concatenate([upper, lower], axis=0).astype(jnp.bfloat16)
    right = jnp.where(
        lax.broadcasted_iota(I32, (LANES, count), 0) == lane, 1.0, 0.0
    ).astype(jnp.bfloat16)
    found = lax.dot_general(
        left, right, (((1,), (1,)), ((), ())), preferred_element_type=F32
    )
    return (found[:lines] * 16.0 + found[lines:]).astype(I32)


def pick_order(sources, unit):
    lane = tile_iota(1)
    place = 4 * (lane & 31) + unit
    result = jnp.zeros((SUBS, LANES), I32)
    for q, source in enumerate(sources):
        result = jnp.where((lane >> 5) == q, pick(source, place), result)
    return result


def fine_tables(w_ref, row_ref, o_ref, _, wo_ref, agg_ref, place_ref):
    lines = o_ref.shape[0]
    for i in range(4):
        for j in range(4):
            for h in range(lines // SUBS):
                start = (i * lines + h * SUBS) * 4 + j
                wo_ref[i, j, pl.ds(h * SUBS, SUBS), :] = w_ref[pl.ds(start, SUBS, stride=4), :]
    agg_ref[...] = inverse_order(row_ref[...], lines)
    sources = []
    for q in range(4):
        four = o_ref[pl.ds(q, 4, stride=4), :]
        sources.append(jnp.concatenate([four, four], axis=0))
    for part in range(2):
        place_ref[part] = pick_order(sources, (tile_iota(0) >> 2) + 2 * part)


def middle_tables(v_ref, c_ref, w_ref, row_ref, o_ref, _, vo_ref, co_ref, mo_ref, wo_ref, agg_ref, place_ref):
    lines = o_ref.shape[0]

    def body(ki, carry):
        k, i = ki // 4, ki % 4
        kp, i2 = ki // 4, ki % 4
        for j in range(4):
            for odd in range(2):
                start = ((2 * kp + odd) * 4 + i2) * (lines * 4) + j
                vo_ref[k, i, j, pl.ds(4 * odd, 4), :] = v_ref[pl.ds(start, 4, stride=4), :]
        return carry

    lax.fori_loop(0, NNZ // 2 * 4, body, 0)
    for kp in range(NNZ // 2):
        for odd in range(2):
            co_ref[kp, pl.ds(4 * odd, 4), :] = c_ref[pl.ds(2 * kp + odd, 4, stride=NNZ), :]
    for i in range(4):
        four = 1.0 / v_ref[pl.ds(i * lines * 4 + i, 4, stride=4), :]
        mo_ref[i, pl.ds(0, 4), :] = four
        mo_ref[i, pl.ds(4, 4), :] = four
        for j in range(4):
            four = w_ref[pl.ds(i * lines * 4 + j, 4, stride=4), :]
            wo_ref[i, j, pl.ds(0, 4), :] = four
            wo_ref[i, j, pl.ds(4, 4), :] = four
    agg = inverse_order(row_ref[...], lines)
    agg_ref[...] = jnp.concatenate([agg, agg], axis=0)
    sources = [wide(o_ref[pl.ds(q, 1), :]) for q in range(4)]
    place_ref[...] = pick_order(sources, tile_iota(0) & 3)


def middle_pad(pad_ref, j, x):
    for twice in range(2):
        pad_ref[pl.ds((twice * 4 + j) * SUBS, SUBS), :] = x


def middle_out(out_ref, pad_ref, s_ref):
    out_ref[...] = outgoing(
        lambda r: pad_ref[pl.ds(r, SUBS, stride=SUBS), :], 4, s_ref[...]
    )


def middle_residual(arrivals, b_ref, x_ref, v_ref, c_ref, edge_ref):
    halo_lines(arrivals, edge_ref)
    acc = [jnp.zeros((SUBS, LANES), F32) for _ in range(4)]
    for j in range(4):
        source = [wide(x_ref[j, pl.ds(r, 1), :]) for r in range(4)]
        source += [wide(edge_ref[pl.ds(4 * e + j, 1), :]) for e in range(2)]
        for kp in range(NNZ // 2):
            col = c_ref[kp]
            got = pick_lines(source, col >> 7, col & (LANES - 1))
            for i in range(4):
                acc[i] = acc[i] + v_ref[kp, i, j] * got
    return [b_ref[i] - duplicate(acc[i]) for i in range(4)]


def middle_update(factors, resid, m_ref, x_ref, d_ref):
    keep, gain = factors
    xs, ds = [], []
    for i in range(4):
        d = gain * (m_ref[i] * resid[i])
        if keep:
            d = keep * d_ref[i] + d
        ds.append(d)
        xs.append(x_ref[i] + d)
    return xs, ds


def middle_step(factors, *refs):
    arrivals = refs[:5]
    (b_ref, m_ref, x_ref, d_ref, v_ref, c_ref, s_ref, xo_ref, do_ref, out_ref, edge_ref, pad_ref) = refs[5:]
    resid = middle_residual(arrivals, b_ref, x_ref, v_ref, c_ref, edge_ref)
    xs, ds = middle_update(factors, resid, m_ref, x_ref, d_ref)
    for i in range(4):
        xo_ref[i] = xs[i]
        do_ref[i] = ds[i]
        middle_pad(pad_ref, i, xs[i])
    middle_out(out_ref, pad_ref, s_ref)


def middle_restrict(*refs):
    arrivals = refs[:5]
    b_ref, x_ref, v_ref, c_ref, w_ref, p_ref, out_ref, edge_ref, line_ref = refs[5:]
    resid = middle_residual(arrivals, b_ref, x_ref, v_ref, c_ref, edge_ref)
    place = p_ref[...]
    high, lane = place >> 7, place & (LANES - 1)
    for j in range(4):
        total = w_ref[0, j] * resid[0]
        for i in range(1, 4):
            total = total + w_ref[i, j] * resid[i]
        line_ref[j] = total
        source = [wide(line_ref[j, pl.ds(r, 1), :]) for r in range(4)]
        got = pick_lines(source, high, lane)
        got = got + pltpu.roll(got, 2, 0)
        got = got + pltpu.roll(got, 1, 0)
        out_ref[pl.ds(j, 1), :] = got[0:1]
        out_ref[pl.ds(4 + j, 1), :] = got[0:1]


def middle_prolong(factors, *refs):
    arrivals = refs[:5]
    (b_ref, m_ref, x_ref, d_ref, v_ref, c_ref, x1_ref, w_ref, agg_ref, s_ref, xo_ref, out_ref, edge_ref, line_ref, pad_ref) = refs[5:]
    lines = x1_ref.shape[1]
    resid = middle_residual(arrivals, b_ref, x_ref, v_ref, c_ref, edge_ref)
    xs, _ = middle_update(factors, resid, m_ref, x_ref, d_ref)
    for j in range(4):
        line_ref[j] = xs[j]
    for h in range(lines // SUBS):
        rows = pl.ds(h * SUBS, SUBS)
        agg = agg_ref[rows, :]
        high, lane = agg >> 7, agg & (LANES - 1)
        spread = [
            pick_lines([wide(line_ref[j, pl.ds(r, 1), :]) for r in range(4)], high, lane)
            for j in range(4)
        ]
        for i in range(4):
            placed = w_ref[i, 0, rows, :] * spread[0]
            for j in range(1, 4):
                placed = placed + w_ref[i, j, rows, :] * spread[j]
            x = x1_ref[i, rows, :] + placed
            xo_ref[i, rows, :] = x
            for twice in range(2):
                pad_ref[pl.ds((twice * 4 + i) * lines + h * SUBS, SUBS), :] = x
    out_ref[...] = outgoing(
        lambda r: pad_ref[pl.ds(r, SUBS, stride=lines), :], lines, s_ref[...]
    )


def coarse_tables(group, *refs):
    vo_ref, co_ref, mo_ref, pad_ref = refs[-4:]
    me = refs[0][0]
    place = 0
    for piece in refs[1:-5]:
        for t in range(piece.shape[0]):
            pad_ref[place] = piece[t]
            place += 1
    for h in range(group // SUBS):
        rows = pl.ds(h * SUBS, SUBS)
        for ki in range(NNZ * 4):
            k, i = ki // 4, ki % 4
            for j in range(4):
                tile = pad_ref[rows, ki * 4 + j, :]
                vo_ref[k, i, j, rows, :] = tile
                if k == 0 and i == j:
                    mo_ref[i, rows, :] = 1.0 / tile
        for k in range(NNZ):
            col = pad_ref[rows, NNZ * 16 + k, :].astype(I32)
            back = me - (col >> 7)
            back = jnp.where(back < 0, back + group, back)
            co_ref[k, rows, :] = back * LANES + (col & (LANES - 1))


def coarse_solve(group, *refs):
    (v_ref, c_ref, m_ref, x2_ref, w_ref, agg_ref, s_ref, xo_ref, out_ref, b_ref, x_ref, d_ref, pad_ref) = refs[-13:]
    place = 0
    for piece in refs[:-13]:
        for t in range(piece.shape[0]):
            for j in range(4):
                b_ref[j, pl.ds(place, 1), :] = piece[t, pl.ds(j, 1), :]
            place += 1
    blocks = group // SUBS
    for j in range(4):
        first = m_ref[j] * b_ref[j]
        x_ref[j] = first
        d_ref[j] = first
    for keep, gain in cheb_factors(KC)[1:]:
        resid = []
        for h in range(blocks):
            rows = pl.ds(h * SUBS, SUBS)
            acc = [b_ref[i, rows, :] for i in range(4)]
            for k in range(NNZ):
                col = c_ref[k, rows, :]
                high, lane = col >> 7, col & (LANES - 1)
                for j in range(4):
                    if k:
                        got = pick_lines(
                            [wide(x_ref[j, pl.ds(r, 1), :]) for r in range(group)], high, lane
                        )
                    else:
                        got = x_ref[j, rows, :]
                    for i in range(4):
                        acc[i] = acc[i] - v_ref[k, i, j, rows, :] * got
            resid.append(acc)
        for h in range(blocks):
            rows = pl.ds(h * SUBS, SUBS)
            for i in range(4):
                d = keep * d_ref[i, rows, :] + gain * (m_ref[i, rows, :] * resid[h][i])
                d_ref[i, rows, :] = d
                x_ref[i, rows, :] = x_ref[i, rows, :] + d
    lane = agg_ref[...]
    spread = [pick(wide(x_ref[j, pl.ds(0, 1), :]), lane) for j in range(4)]
    for i in range(4):
        x = x2_ref[i]
        for j in range(4):
            x = x + w_ref[i, j] * spread[j]
        xo_ref[i] = x
        middle_pad(pad_ref, i, x)
    middle_out(out_ref, pad_ref, s_ref)


def call(body, outs, args, scratch=(), free=(), smem=()):
    specs = []
    for index in range(len(args)):
        if index in free:
            specs.append(pl.BlockSpec(memory_space=pl.ANY))
        elif index in smem:
            specs.append(pl.BlockSpec(memory_space=pltpu.SMEM))
        else:
            specs.append(pl.BlockSpec(memory_space=pltpu.VMEM))
    single = not isinstance(outs, (list, tuple))
    shapes = [outs] if single else list(outs)
    result = pl.pallas_call(
        body,
        out_shape=shapes,
        in_specs=specs,
        out_specs=[pl.BlockSpec(memory_space=pltpu.VMEM) for _ in shapes],
        scratch_shapes=list(scratch),
        compiler_params=pltpu.CompilerParams(vmem_limit_bytes=16 * 2**20),
    )(*args)
    return result[0] if single else result


def shape(*dims, dtype=F32):
    return jax.ShapeDtypeStruct(dims, dtype)


def vmem(*dims, dtype=F32):
    return pltpu.VMEM(dims, dtype)


def native_rows(x):
    lines = x.shape[-1] // LANES
    split = x.reshape(x.shape[:-1] + (lines, LANES))
    return jnp.swapaxes(split, -2, -3).reshape(-1, LANES)


def from_native(rows, lines):
    return jnp.swapaxes(rows.reshape(lines, 4, LANES), 0, 1).reshape(4, lines * LANES)


def send_table(sends):
    stream = jnp.concatenate([sends[1], sends[0]])[None]
    span = jnp.concatenate([sends[3], sends[2]])[None]
    return jnp.concatenate([stream] * 4 + [span] * 4, axis=0)


def exchange(mesh, out, inside):
    count = mesh.shape["span"]
    total = mesh.shape["stream"] * count
    moved = [
        lax.ppermute(out, AXES, [(p, (p + shift) % total) for p in range(total)])
        for shift in (count, -count, 1, -1)
    ]
    return moved + [inside]


def span_shift(mesh, value, shift):
    slabs, count = mesh.shape["stream"], mesh.shape["span"]
    pairs = [
        (a * count + b, a * count + (b + shift) % count)
        for a in range(slabs)
        for b in range(count)
    ]
    return lax.ppermute(value, AXES, pairs)


def span_stage(mesh, pieces):
    group = mesh.shape["span"]
    have = sum(piece.shape[0] for piece in pieces)
    held = jnp.concatenate(pieces)[: min(have, group - have)]
    return pieces + [span_shift(mesh, held, have)]


def per_device(mesh, right_side, fine_values, fine_columns, fine_sends, fine_order, fine_weights, middle_values, middle_columns, middle_sends, middle_order, middle_weights, coarsest_values, coarsest_columns):
    group = mesh.shape["span"]
    lines = right_side.shape[1] // LANES
    tile = shape(SUBS, LANES)
    vec1 = shape(4, lines, LANES)
    vec2 = shape(4, SUBS, LANES)
    edge = vmem(SUBS, LANES)
    pad1 = vmem(SUBS * lines, LANES)
    pad2 = vmem(SUBS * SUBS, LANES)
    factors = cheb_factors(KSM)
    me = lax.axis_index("span").astype(I32)
    row, lane = (lax.broadcasted_iota(I32, (SUBS, LANES), d) for d in range(2))
    outside = (row >= 4) & jnp.where(lane < LANES // 2, me == 0, me == group - 1)
    inside = jnp.where(outside, 0.0, 1.0).astype(F32)
    send1, send2 = send_table(fine_sends), send_table(middle_sends)
    values1 = native_rows(fine_values)
    values2 = native_rows(middle_values)

    b1, m1, x1, out = call(
        fine_start,
        [vec1, vec1, vec1, tile],
        [native_rows(fine_values[0]), native_rows(right_side), send1],
        [pad1],
    )
    d1 = x1

    own3 = jnp.concatenate(
        [coarsest_values.reshape(NNZ * 16, LANES), coarsest_columns.astype(F32)], axis=0
    )
    v1, c1 = call(
        fine_prepare,
        [shape(NNZ, 4, 4, lines, LANES), shape(NNZ, lines, LANES, dtype=I32)],
        [values1, native_columns(fine_columns), out],
        free=(2,),
    )

    def fine_part(x):
        return call(fine_local, vec1, [x, b1, v1, c1], [vmem(4, lines, SUBS, LANES)])

    def fine_next(which, arrived, resid, x, d, after=()):
        args = arrived + [resid, v1, c1, m1, x, d, send1]
        return call(
            lambda *refs: fine_step(factors[which], *(refs[: len(args)] + refs[len(args) + len(after) :])),
            [vec1, vec1, tile],
            args + list(after),
            [edge, pad1],
            free=range(len(args), len(args) + len(after)),
        )

    arrived = exchange(mesh, out, inside)
    own3, _ = lax.optimization_barrier((own3, out))
    pieces3 = span_stage(mesh, [own3[None]])
    resid = fine_part(x1)
    x1, d1, out = fine_next(1, arrived, resid, x1, d1)

    arrived = exchange(mesh, out, inside)
    pieces3, _ = lax.optimization_barrier((pieces3, out))
    pieces3 = span_stage(mesh, pieces3)
    resid = fine_part(x1)
    w1, agg1, place1 = call(
        fine_tables,
        [shape(4, 4, lines, LANES), shape(lines, LANES, dtype=I32), shape(2, SUBS, LANES, dtype=I32)],
        [native_rows(fine_weights), fine_order, fine_order.reshape(lines, LANES), out],
        free=(3,),
    )
    x1, d1, out = fine_next(2, arrived, resid, x1, d1, [pieces3[1]])

    arrived = exchange(mesh, out, inside)
    pieces3, _ = lax.optimization_barrier((pieces3, out))
    while sum(piece.shape[0] for piece in pieces3) < group:
        pieces3 = span_stage(mesh, pieces3)
    resid = fine_part(x1)
    v2, c2, m2, w2, agg2, place2 = call(
        middle_tables,
        [
            shape(NNZ // 2, 4, 4, SUBS, LANES),
            shape(NNZ // 2, SUBS, LANES, dtype=I32),
            vec2,
            shape(4, 4, SUBS, LANES),
            shape(SUBS, LANES, dtype=I32),
            shape(SUBS, LANES, dtype=I32),
        ],
        [values2, native_columns(middle_columns), native_rows(middle_weights), middle_order, middle_order.reshape(-1, LANES), out],
        free=(5,),
    )
    b2, x2, out = call(
        fine_restrict,
        [vec2, vec2, tile],
        arrived + [resid, v1, c1, w1, place1, m2, send2],
        [edge, vmem(4, lines, LANES), pad2],
    )
    d2 = x2

    def middle_next(which, arrived, x, d, after=()):
        args = arrived + [b2, m2, x, d, v2, c2, send2]
        return call(
            lambda *refs: middle_step(factors[which], *(refs[: len(args)] + refs[len(args) + len(after) :])),
            [vec2, vec2, tile],
            args + list(after),
            [edge, pad2],
            free=range(len(args), len(args) + len(after)),
        )

    arrived = exchange(mesh, out, inside)
    v3, c3, m3 = call(
        lambda *refs: coarse_tables(group, *refs),
        [shape(NNZ, 4, 4, group, LANES), shape(NNZ, group, LANES, dtype=I32), shape(4, group, LANES)],
        [me.reshape(1)] + pieces3 + [out],
        [vmem(group, NNZ * 17, LANES)],
        free=(1 + len(pieces3),),
        smem=(0,),
    )
    x2, d2, out = middle_next(1, arrived, x2, d2, [m3])
    arrived = exchange(mesh, out, inside)
    x2, d2, out = middle_next(2, arrived, x2, d2)
    arrived = exchange(mesh, out, inside)
    rhs3 = call(
        middle_restrict,
        tile,
        arrived + [b2, x2, v2, c2, w2, place2],
        [edge, vmem(4, SUBS, LANES)],
    )
    pieces = [rhs3[None]]
    while sum(piece.shape[0] for piece in pieces) < group:
        pieces = span_stage(mesh, pieces)
    vec3 = vmem(4, group, LANES)
    x2, out = call(
        lambda *refs: coarse_solve(group, *refs),
        [vec2, tile],
        pieces + [v3, c3, m3, x2, w2, agg2, send2],
        [vec3, vec3, vec3, pad2],
    )
    arrived = exchange(mesh, out, inside)
    x2, d2, out = middle_next(0, arrived, x2, x2)
    arrived = exchange(mesh, out, inside)
    x2, d2, out = middle_next(1, arrived, x2, d2)
    arrived = exchange(mesh, out, inside)
    x1, out = call(
        lambda *refs: middle_prolong(factors[2], *refs),
        [vec1, tile],
        arrived + [b2, m2, x2, d2, v2, c2, x1, w1, agg1, send1],
        [edge, vmem(4, SUBS, LANES), pad1],
    )
    for which in range(KSM):
        arrived = exchange(mesh, out, inside)
        resid = fine_part(x1)
        x1, d1, out = fine_next(which, arrived, resid, x1, d1)
    arrived = exchange(mesh, out, inside)
    resid = fine_part(x1)
    rows = shape(4 * lines, LANES)
    solved, left = call(fine_finish, [rows, rows], arrived + [resid, v1, c1, x1], [edge])
    return from_native(solved, lines), from_native(left, lines)


def native_columns(columns):
    lines = columns.shape[1] // LANES
    return jnp.swapaxes(columns.reshape(NNZ, lines, LANES), 0, 1).reshape(-1, LANES)


def solution(mesh):
    both = ("stream", "span")
    in_specs = (
        P(None, both),
        P(None, None, None, both),
        P(None, both),
        P(None, both),
        P(both, None),
        P(None, None, both),
        P(None, None, None, both),
        P(None, both),
        P(None, both),
        P(both, None),
        P(None, None, both),
        P(None, None, None, both),
        P(None, both),
    )
    return jax.shard_map(
        lambda *args: per_device(mesh, *args),
        mesh=mesh,
        in_specs=in_specs,
        out_specs=(P(None, both), P(None, both)),
        check_vma=False,
    )
```

```python
import jax
import jax.numpy as jnp
from jax import lax
from jax.experimental import pallas as pl
from jax.experimental.pallas import tpu as pltpu
from jax.sharding import PartitionSpec as P

KSM = 3
KC = 4
NNZ = 8
LANES = 128
SUBS = 8

CHEB_CENTRE = 1.0
CHEB_RADIUS = 0.9
AXES = ("stream", "span")
F32 = jnp.float32
I32 = jnp.int32


def cheb_factors(degree):
    sigma = CHEB_CENTRE / CHEB_RADIUS
    rho = 1.0 / sigma
    factors = [(0.0, 1.0 / CHEB_CENTRE)]
    for _ in range(degree - 1):
        rho_next = 1.0 / (2.0 * sigma - rho)
        factors.append((rho_next * rho, 2.0 * rho_next / CHEB_RADIUS))
        rho = rho_next
    return factors


def tile_iota(dim):
    return lax.broadcasted_iota(I32, (SUBS, LANES), dim)


def pick(line, lane):
    return jnp.take_along_axis(line, lane, axis=1, mode="promise_in_bounds")


def wide(line):
    return jnp.broadcast_to(line, (SUBS, LANES))


def pick_lines(lines, high, lane, first=0):
    result = jnp.zeros((SUBS, LANES), F32)
    for r, line in enumerate(lines):
        result = jnp.where(high == first + r, pick(line, lane), result)
    return result


def halo_lines(arrivals, edge_ref):
    all_ref, place_ref, inside_ref = arrivals
    prev_s, next_s, prev_p, next_p = [all_ref[place_ref[d]] for d in range(4)]
    inside = inside_ref[...]
    left = tile_iota(1) < LANES // 2
    upper = tile_iota(0) < 4
    values = jnp.where(
        upper, jnp.where(left, prev_s, next_s), jnp.where(left, prev_p, next_p)
    )
    edge_ref[...] = jnp.where(inside > 0.0, values, 0.0)


def outgoing(lines_of, count, sends):
    high, lane = sends >> 7, sends & (LANES - 1)
    return pick_lines([lines_of(r) for r in range(count)], high, lane)


def duplicate(x):
    return x + pltpu.roll(x, 4, 0)


def fine_start(v_ref, b_ref, s_ref, bo_ref, mo_ref, x_ref, out_ref, pad_ref):
    lines = bo_ref.shape[1]
    for i in range(4):
        for h in range(lines // SUBS):
            rows = pl.ds(h * SUBS, SUBS)
            native = pl.ds(h * SUBS * 4 + i, SUBS, stride=4)
            b = b_ref[native, :]
            m = 1.0 / v_ref[pl.ds((i * lines + h * SUBS) * 4 + i, SUBS, stride=4), :]
            x = m * b
            bo_ref[i, rows, :] = b
            mo_ref[i, rows, :] = m
            x_ref[i, rows, :] = x
            for twice in range(2):
                pad_ref[pl.ds((twice * 4 + i) * lines + h * SUBS, SUBS), :] = x
    out_ref[...] = outgoing(
        lambda r: pad_ref[pl.ds(r, SUBS, stride=lines), :], lines, s_ref[...]
    )


def fine_prepare(v_ref, c_ref, _, vo_ref, co_ref):
    lines = vo_ref.shape[3]
    halves = lines // SUBS

    def body(ki, carry):
        k, i = ki // 4, ki % 4
        for j in range(4):
            for h in range(halves):
                start = ki * (lines * 4) + h * SUBS * 4 + j
                vo_ref[k, i, j, pl.ds(h * SUBS, SUBS), :] = v_ref[
                    pl.ds(start, SUBS, stride=4), :
                ]
        return carry

    lax.fori_loop(0, NNZ * 4, body, 0)
    for k in range(NNZ):
        for h in range(halves):
            co_ref[k, pl.ds(h * SUBS, SUBS), :] = c_ref[
                pl.ds(h * SUBS * NNZ + k, SUBS, stride=NNZ), :
            ]


def fine_local(x_ref, b_ref, v_ref, c_ref, r_ref, line_ref):
    lines = x_ref.shape[1]
    halves = lines // SUBS
    for j in range(4):
        for r in range(lines):
            line_ref[j, r] = wide(x_ref[j, pl.ds(r, 1), :])
    acc = []
    for h in range(halves):
        rows = pl.ds(h * SUBS, SUBS)
        for i in range(4):
            total = b_ref[i, rows, :]
            for j in range(4):
                total = total - v_ref[0, i, j, rows, :] * x_ref[j, rows, :]
            acc.append(total)

    def body(k, acc):
        acc = list(acc)
        for h in range(halves):
            rows = pl.ds(h * SUBS, SUBS)
            col = c_ref[k, rows, :]
            high, lane = col >> 7, col & (LANES - 1)
            for j in range(4):
                got = pick_lines([line_ref[j, r] for r in range(lines)], high, lane)
                for i in range(4):
                    acc[4 * h + i] = acc[4 * h + i] - v_ref[k, i, j, rows, :] * got
        return tuple(acc)

    acc = lax.fori_loop(1, NNZ, body, tuple(acc))
    for h in range(halves):
        for i in range(4):
            r_ref[i, pl.ds(h * SUBS, SUBS), :] = acc[4 * h + i]


def fine_remote(arrivals, r_ref, v_ref, c_ref, edge_ref):
    lines = r_ref.shape[1]
    halves = lines // SUBS
    halo_lines(arrivals, edge_ref)
    edges = [[wide(edge_ref[pl.ds(4 * e + j, 1), :]) for e in range(2)] for j in range(4)]
    result = []
    for h in range(halves):
        rows = pl.ds(h * SUBS, SUBS)
        acc = [r_ref[i, rows, :] for i in range(4)]
        for k in range(1, NNZ):
            col = c_ref[k, rows, :]
            high, lane = col >> 7, col & (LANES - 1)
            for j in range(4):
                got = pick_lines(edges[j], high, lane, lines)
                for i in range(4):
                    acc[i] = acc[i] - v_ref[k, i, j, rows, :] * got
        result.append(acc)
    return result


def fine_step(factors, *refs):
    arrivals = refs[:3]
    (r_ref, v_ref, c_ref, m_ref, x_ref, d_ref, s_ref, xo_ref, do_ref, out_ref, edge_ref, pad_ref) = refs[3:]
    keep, gain = factors
    lines = r_ref.shape[1]
    resid = fine_remote(arrivals, r_ref, v_ref, c_ref, edge_ref)
    for h in range(lines // SUBS):
        rows = pl.ds(h * SUBS, SUBS)
        for i in range(4):
            d = gain * (m_ref[i, rows, :] * resid[h][i])
            if keep:
                d = keep * d_ref[i, rows, :] + d
            x = x_ref[i, rows, :] + d
            do_ref[i, rows, :] = d
            xo_ref[i, rows, :] = x
            for twice in range(2):
                pad_ref[pl.ds((twice * 4 + i) * lines + h * SUBS, SUBS), :] = x
    out_ref[...] = outgoing(
        lambda r: pad_ref[pl.ds(r, SUBS, stride=lines), :], lines, s_ref[...]
    )


def fine_finish(*refs):
    arrivals = refs[:3]
    r_ref, v_ref, c_ref, x_ref, so_ref, ro_ref, edge_ref = refs[3:]
    lines = r_ref.shape[1]
    resid = fine_remote(arrivals, r_ref, v_ref, c_ref, edge_ref)
    for h in range(lines // SUBS):
        for i in range(4):
            native = pl.ds(h * SUBS * 4 + i, SUBS, stride=4)
            so_ref[native, :] = x_ref[i, pl.ds(h * SUBS, SUBS), :]
            ro_ref[native, :] = resid[h][i]


def fine_restrict(*refs):
    arrivals = refs[:3]
    (r_ref, v_ref, c_ref, w_ref, p_ref, m2_ref, s2_ref, b2_ref, x2_ref, out_ref, edge_ref, line_ref, pad_ref) = refs[3:]
    lines = r_ref.shape[1]
    resid = fine_remote(arrivals, r_ref, v_ref, c_ref, edge_ref)
    for h in range(lines // SUBS):
        rows = pl.ds(h * SUBS, SUBS)
        for j in range(4):
            total = w_ref[0, j, rows, :] * resid[h][0]
            for i in range(1, 4):
                total = total + w_ref[i, j, rows, :] * resid[h][i]
            line_ref[j, rows, :] = total
    for j in range(4):
        total = None
        source = [wide(line_ref[j, pl.ds(r, 1), :]) for r in range(lines)]
        for part in range(2):
            place = p_ref[part]
            got = pick_lines(source, place >> 7, place & (LANES - 1))
            total = got if total is None else total + got
        b2 = duplicate(total)
        x2 = m2_ref[j] * b2
        b2_ref[j] = b2
        x2_ref[j] = x2
        middle_pad(pad_ref, j, x2)
    middle_out(out_ref, pad_ref, s2_ref)


def inverse_order(o_row, lines):
    count = lines * LANES
    high, lane = o_row >> 7, o_row & (LANES - 1)
    coarse = lax.broadcasted_iota(I32, (1, count), 1) >> 2
    here = lax.broadcasted_iota(I32, (lines, count), 0) == high
    upper = jnp.where(here, (coarse >> 4).astype(F32), 0.0)
    lower = jnp.where(here, (coarse & 15).astype(F32), 0.0)
    left = jnp.concatenate([upper, lower], axis=0).astype(jnp.bfloat16)
    right = jnp.where(
        lax.broadcasted_iota(I32, (LANES, count), 0) == lane, 1.0, 0.0
    ).astype(jnp.bfloat16)
    found = lax.dot_general(
        left, right, (((1,), (1,)), ((), ())), preferred_element_type=F32
    )
    return (found[:lines] * 16.0 + found[lines:]).astype(I32)


def pick_order(sources, unit):
    lane = tile_iota(1)
    place = 4 * (lane & 31) + unit
    result = jnp.zeros((SUBS, LANES), I32)
    for q, source in enumerate(sources):
        result = jnp.where((lane >> 5) == q, pick(source, place), result)
    return result


def fine_tables(w_ref, row_ref, o_ref, _, wo_ref, agg_ref, place_ref):
    lines = o_ref.shape[0]
    for i in range(4):
        for j in range(4):
            for h in range(lines // SUBS):
                start = (i * lines + h * SUBS) * 4 + j
                wo_ref[i, j, pl.ds(h * SUBS, SUBS), :] = w_ref[pl.ds(start, SUBS, stride=4), :]
    agg_ref[...] = inverse_order(row_ref[...], lines)
    sources = []
    for q in range(4):
        four = o_ref[pl.ds(q, 4, stride=4), :]
        sources.append(jnp.concatenate([four, four], axis=0))
    for part in range(2):
        place_ref[part] = pick_order(sources, (tile_iota(0) >> 2) + 2 * part)


def middle_tables(v_ref, c_ref, w_ref, row_ref, o_ref, _, vo_ref, co_ref, mo_ref, wo_ref, agg_ref, place_ref):
    lines = o_ref.shape[0]

    def body(ki, carry):
        k, i = ki // 4, ki % 4
        kp, i2 = ki // 4, ki % 4
        for j in range(4):
            for odd in range(2):
                start = ((2 * kp + odd) * 4 + i2) * (lines * 4) + j
                vo_ref[k, i, j, pl.ds(4 * odd, 4), :] = v_ref[pl.ds(start, 4, stride=4), :]
        return carry

    lax.fori_loop(0, NNZ // 2 * 4, body, 0)
    for kp in range(NNZ // 2):
        for odd in range(2):
            co_ref[kp, pl.ds(4 * odd, 4), :] = c_ref[pl.ds(2 * kp + odd, 4, stride=NNZ), :]
    for i in range(4):
        four = 1.0 / v_ref[pl.ds(i * lines * 4 + i, 4, stride=4), :]
        mo_ref[i, pl.ds(0, 4), :] = four
        mo_ref[i, pl.ds(4, 4), :] = four
        for j in range(4):
            four = w_ref[pl.ds(i * lines * 4 + j, 4, stride=4), :]
            wo_ref[i, j, pl.ds(0, 4), :] = four
            wo_ref[i, j, pl.ds(4, 4), :] = four
    agg = inverse_order(row_ref[...], lines)
    agg_ref[...] = jnp.concatenate([agg, agg], axis=0)
    sources = [wide(o_ref[pl.ds(q, 1), :]) for q in range(4)]
    place_ref[...] = pick_order(sources, tile_iota(0) & 3)


def middle_pad(pad_ref, j, x):
    for twice in range(2):
        pad_ref[pl.ds((twice * 4 + j) * SUBS, SUBS), :] = x


def middle_out(out_ref, pad_ref, s_ref):
    out_ref[...] = outgoing(
        lambda r: pad_ref[pl.ds(r, SUBS, stride=SUBS), :], 4, s_ref[...]
    )


def middle_residual(arrivals, b_ref, x_ref, v_ref, c_ref, edge_ref):
    halo_lines(arrivals, edge_ref)
    acc = [jnp.zeros((SUBS, LANES), F32) for _ in range(4)]
    for j in range(4):
        source = [wide(x_ref[j, pl.ds(r, 1), :]) for r in range(4)]
        source += [wide(edge_ref[pl.ds(4 * e + j, 1), :]) for e in range(2)]
        for kp in range(NNZ // 2):
            col = c_ref[kp]
            got = pick_lines(source, col >> 7, col & (LANES - 1))
            for i in range(4):
                acc[i] = acc[i] + v_ref[kp, i, j] * got
    return [b_ref[i] - duplicate(acc[i]) for i in range(4)]


def middle_update(factors, resid, m_ref, x_ref, d_ref):
    keep, gain = factors
    xs, ds = [], []
    for i in range(4):
        d = gain * (m_ref[i] * resid[i])
        if keep:
            d = keep * d_ref[i] + d
        ds.append(d)
        xs.append(x_ref[i] + d)
    return xs, ds


def middle_step(factors, *refs):
    arrivals = refs[:3]
    (b_ref, m_ref, x_ref, d_ref, v_ref, c_ref, s_ref, xo_ref, do_ref, out_ref, edge_ref, pad_ref) = refs[3:]
    resid = middle_residual(arrivals, b_ref, x_ref, v_ref, c_ref, edge_ref)
    xs, ds = middle_update(factors, resid, m_ref, x_ref, d_ref)
    for i in range(4):
        xo_ref[i] = xs[i]
        do_ref[i] = ds[i]
        middle_pad(pad_ref, i, xs[i])
    middle_out(out_ref, pad_ref, s_ref)


def middle_restrict(*refs):
    arrivals = refs[:3]
    b_ref, x_ref, v_ref, c_ref, w_ref, p_ref, out_ref, edge_ref, line_ref = refs[3:]
    resid = middle_residual(arrivals, b_ref, x_ref, v_ref, c_ref, edge_ref)
    place = p_ref[...]
    high, lane = place >> 7, place & (LANES - 1)
    for j in range(4):
        total = w_ref[0, j] * resid[0]
        for i in range(1, 4):
            total = total + w_ref[i, j] * resid[i]
        line_ref[j] = total
        source = [wide(line_ref[j, pl.ds(r, 1), :]) for r in range(4)]
        got = pick_lines(source, high, lane)
        got = got + pltpu.roll(got, 2, 0)
        got = got + pltpu.roll(got, 1, 0)
        out_ref[pl.ds(j, 1), :] = got[0:1]
        out_ref[pl.ds(4 + j, 1), :] = got[0:1]


def middle_prolong(factors, *refs):
    arrivals = refs[:3]
    (b_ref, m_ref, x_ref, d_ref, v_ref, c_ref, x1_ref, w_ref, agg_ref, s_ref, xo_ref, out_ref, edge_ref, line_ref, pad_ref) = refs[3:]
    lines = x1_ref.shape[1]
    resid = middle_residual(arrivals, b_ref, x_ref, v_ref, c_ref, edge_ref)
    xs, _ = middle_update(factors, resid, m_ref, x_ref, d_ref)
    for j in range(4):
        line_ref[j] = xs[j]
    for h in range(lines // SUBS):
        rows = pl.ds(h * SUBS, SUBS)
        agg = agg_ref[rows, :]
        high, lane = agg >> 7, agg & (LANES - 1)
        spread = [
            pick_lines([wide(line_ref[j, pl.ds(r, 1), :]) for r in range(4)], high, lane)
            for j in range(4)
        ]
        for i in range(4):
            placed = w_ref[i, 0, rows, :] * spread[0]
            for j in range(1, 4):
                placed = placed + w_ref[i, j, rows, :] * spread[j]
            x = x1_ref[i, rows, :] + placed
            xo_ref[i, rows, :] = x
            for twice in range(2):
                pad_ref[pl.ds((twice * 4 + i) * lines + h * SUBS, SUBS), :] = x
    out_ref[...] = outgoing(
        lambda r: pad_ref[pl.ds(r, SUBS, stride=lines), :], lines, s_ref[...]
    )


def coarse_tables(group, *refs):
    vo_ref, co_ref, mo_ref, pad_ref = refs[-4:]
    me = refs[0][0]
    place = 0
    for piece in refs[1:-5]:
        for t in range(piece.shape[0]):
            pad_ref[place] = piece[t]
            place += 1
    for h in range(group // SUBS):
        rows = pl.ds(h * SUBS, SUBS)
        for ki in range(NNZ * 4):
            k, i = ki // 4, ki % 4
            for j in range(4):
                tile = pad_ref[rows, ki * 4 + j, :]
                vo_ref[k, i, j, rows, :] = tile
                if k == 0 and i == j:
                    mo_ref[i, rows, :] = 1.0 / tile
        for k in range(NNZ):
            col = pad_ref[rows, NNZ * 16 + k, :].astype(I32)
            back = me - (col >> 7)
            back = jnp.where(back < 0, back + group, back)
            co_ref[k, rows, :] = back * LANES + (col & (LANES - 1))


def coarse_solve(group, *refs):
    (v_ref, c_ref, m_ref, x2_ref, w_ref, agg_ref, s_ref, xo_ref, out_ref, b_ref, x_ref, d_ref, pad_ref) = refs[-13:]
    place = 0
    for piece in refs[:-13]:
        for t in range(piece.shape[0]):
            for j in range(4):
                b_ref[j, pl.ds(place, 1), :] = piece[t, pl.ds(j, 1), :]
            place += 1
    blocks = group // SUBS
    for j in range(4):
        first = m_ref[j] * b_ref[j]
        x_ref[j] = first
        d_ref[j] = first
    for keep, gain in cheb_factors(KC)[1:]:
        resid = []
        for h in range(blocks):
            rows = pl.ds(h * SUBS, SUBS)
            acc = [b_ref[i, rows, :] for i in range(4)]
            for k in range(NNZ):
                col = c_ref[k, rows, :]
                high, lane = col >> 7, col & (LANES - 1)
                for j in range(4):
                    if k:
                        got = pick_lines(
                            [wide(x_ref[j, pl.ds(r, 1), :]) for r in range(group)], high, lane
                        )
                    else:
                        got = x_ref[j, rows, :]
                    for i in range(4):
                        acc[i] = acc[i] - v_ref[k, i, j, rows, :] * got
            resid.append(acc)
        for h in range(blocks):
            rows = pl.ds(h * SUBS, SUBS)
            for i in range(4):
                d = keep * d_ref[i, rows, :] + gain * (m_ref[i, rows, :] * resid[h][i])
                d_ref[i, rows, :] = d
                x_ref[i, rows, :] = x_ref[i, rows, :] + d
    lane = agg_ref[...]
    spread = [pick(wide(x_ref[j, pl.ds(0, 1), :]), lane) for j in range(4)]
    for i in range(4):
        x = x2_ref[i]
        for j in range(4):
            x = x + w_ref[i, j] * spread[j]
        xo_ref[i] = x
        middle_pad(pad_ref, i, x)
    middle_out(out_ref, pad_ref, s_ref)


def call(body, outs, args, scratch=(), free=(), smem=()):
    specs = []
    smem = tuple(smem) + tuple(t for t, arg in enumerate(args) if arg.shape == (4,))
    for index in range(len(args)):
        if index in free:
            specs.append(pl.BlockSpec(memory_space=pl.ANY))
        elif index in smem:
            specs.append(pl.BlockSpec(memory_space=pltpu.SMEM))
        else:
            specs.append(pl.BlockSpec(memory_space=pltpu.VMEM))
    single = not isinstance(outs, (list, tuple))
    shapes = [outs] if single else list(outs)
    result = pl.pallas_call(
        body,
        out_shape=shapes,
        in_specs=specs,
        out_specs=[pl.BlockSpec(memory_space=pltpu.VMEM) for _ in shapes],
        scratch_shapes=list(scratch),
        compiler_params=pltpu.CompilerParams(vmem_limit_bytes=16 * 2**20),
    )(*args)
    return result[0] if single else result


def shape(*dims, dtype=F32):
    return jax.ShapeDtypeStruct(dims, dtype)


def vmem(*dims, dtype=F32):
    return pltpu.VMEM(dims, dtype)


def native_rows(x):
    lines = x.shape[-1] // LANES
    split = x.reshape(x.shape[:-1] + (lines, LANES))
    return jnp.swapaxes(split, -2, -3).reshape(-1, LANES)


def from_native(rows, lines):
    return jnp.swapaxes(rows.reshape(lines, 4, LANES), 0, 1).reshape(4, lines * LANES)


def send_table(sends):
    stream = jnp.concatenate([sends[1], sends[0]])[None]
    span = jnp.concatenate([sends[3], sends[2]])[None]
    return jnp.concatenate([stream] * 4 + [span] * 4, axis=0)


def exchange(mesh, out, near):
    total = mesh.shape["stream"] * mesh.shape["span"]
    copies = jnp.broadcast_to(out[None], (total, SUBS, LANES))
    return [lax.all_to_all(copies, AXES, 0, 0, tiled=True)] + near


def span_shift(mesh, value, shift):
    slabs, count = mesh.shape["stream"], mesh.shape["span"]
    pairs = [
        (a * count + b, a * count + (b + shift) % count)
        for a in range(slabs)
        for b in range(count)
    ]
    return lax.ppermute(value, AXES, pairs)


def span_stage(mesh, pieces):
    group = mesh.shape["span"]
    have = sum(piece.shape[0] for piece in pieces)
    held = jnp.concatenate(pieces)[: min(have, group - have)]
    return pieces + [span_shift(mesh, held, have)]


def per_device(mesh, right_side, fine_values, fine_columns, fine_sends, fine_order, fine_weights, middle_values, middle_columns, middle_sends, middle_order, middle_weights, coarsest_values, coarsest_columns):
    group = mesh.shape["span"]
    lines = right_side.shape[1] // LANES
    tile = shape(SUBS, LANES)
    vec1 = shape(4, lines, LANES)
    vec2 = shape(4, SUBS, LANES)
    edge = vmem(SUBS, LANES)
    pad1 = vmem(SUBS * lines, LANES)
    pad2 = vmem(SUBS * SUBS, LANES)
    factors = cheb_factors(KSM)
    me = lax.axis_index("span").astype(I32)
    row, lane = (lax.broadcasted_iota(I32, (SUBS, LANES), d) for d in range(2))
    outside = (row >= 4) & jnp.where(lane < LANES // 2, me == 0, me == group - 1)
    inside = jnp.where(outside, 0.0, 1.0).astype(F32)
    total = mesh.shape["stream"] * group
    here = lax.axis_index("stream").astype(I32) * group + me
    place = jnp.stack([here - group, here + group, here - 1, here + 1])
    near = [jnp.where(place < 0, place + total, jnp.where(place >= total, place - total, place)), inside]
    send1, send2 = send_table(fine_sends), send_table(middle_sends)
    values1 = native_rows(fine_values)
    values2 = native_rows(middle_values)

    b1, m1, x1, out = call(
        fine_start,
        [vec1, vec1, vec1, tile],
        [native_rows(fine_values[0]), native_rows(right_side), send1],
        [pad1],
    )
    d1 = x1

    own3 = jnp.concatenate(
        [coarsest_values.reshape(NNZ * 16, LANES), coarsest_columns.astype(F32)], axis=0
    )
    v1, c1 = call(
        fine_prepare,
        [shape(NNZ, 4, 4, lines, LANES), shape(NNZ, lines, LANES, dtype=I32)],
        [values1, native_columns(fine_columns), out],
        free=(2,),
    )

    def fine_part(x):
        return call(fine_local, vec1, [x, b1, v1, c1], [vmem(4, lines, SUBS, LANES)])

    def fine_next(which, arrived, resid, x, d, after=()):
        args = arrived + [resid, v1, c1, m1, x, d, send1]
        return call(
            lambda *refs: fine_step(factors[which], *(refs[: len(args)] + refs[len(args) + len(after) :])),
            [vec1, vec1, tile],
            args + list(after),
            [edge, pad1],
            free=range(len(args), len(args) + len(after)),
        )

    arrived = exchange(mesh, out, near)
    own3, _ = lax.optimization_barrier((own3, out))
    pieces3 = span_stage(mesh, [own3[None]])
    resid = fine_part(x1)
    x1, d1, out = fine_next(1, arrived, resid, x1, d1)

    arrived = exchange(mesh, out, near)
    pieces3, _ = lax.optimization_barrier((pieces3, out))
    pieces3 = span_stage(mesh, pieces3)
    resid = fine_part(x1)
    w1, agg1, place1 = call(
        fine_tables,
        [shape(4, 4, lines, LANES), shape(lines, LANES, dtype=I32), shape(2, SUBS, LANES, dtype=I32)],
        [native_rows(fine_weights), fine_order, fine_order.reshape(lines, LANES), out],
        free=(3,),
    )
    x1, d1, out = fine_next(2, arrived, resid, x1, d1, [pieces3[1]])

    arrived = exchange(mesh, out, near)
    pieces3, _ = lax.optimization_barrier((pieces3, out))
    while sum(piece.shape[0] for piece in pieces3) < group:
        pieces3 = span_stage(mesh, pieces3)
    resid = fine_part(x1)
    v2, c2, m2, w2, agg2, place2 = call(
        middle_tables,
        [
            shape(NNZ // 2, 4, 4, SUBS, LANES),
            shape(NNZ // 2, SUBS, LANES, dtype=I32),
            vec2,
            shape(4, 4, SUBS, LANES),
            shape(SUBS, LANES, dtype=I32),
            shape(SUBS, LANES, dtype=I32),
        ],
        [values2, native_columns(middle_columns), native_rows(middle_weights), middle_order, middle_order.reshape(-1, LANES), out],
        free=(5,),
    )
    b2, x2, out = call(
        fine_restrict,
        [vec2, vec2, tile],
        arrived + [resid, v1, c1, w1, place1, m2, send2],
        [edge, vmem(4, lines, LANES), pad2],
    )
    d2 = x2

    def middle_next(which, arrived, x, d, after=()):
        args = arrived + [b2, m2, x, d, v2, c2, send2]
        return call(
            lambda *refs: middle_step(factors[which], *(refs[: len(args)] + refs[len(args) + len(after) :])),
            [vec2, vec2, tile],
            args + list(after),
            [edge, pad2],
            free=range(len(args), len(args) + len(after)),
        )

    arrived = exchange(mesh, out, near)
    v3, c3, m3 = call(
        lambda *refs: coarse_tables(group, *refs),
        [shape(NNZ, 4, 4, group, LANES), shape(NNZ, group, LANES, dtype=I32), shape(4, group, LANES)],
        [me.reshape(1)] + pieces3 + [out],
        [vmem(group, NNZ * 17, LANES)],
        free=(1 + len(pieces3),),
        smem=(0,),
    )
    x2, d2, out = middle_next(1, arrived, x2, d2, [m3])
    arrived = exchange(mesh, out, near)
    x2, d2, out = middle_next(2, arrived, x2, d2)
    arrived = exchange(mesh, out, near)
    rhs3 = call(
        middle_restrict,
        tile,
        arrived + [b2, x2, v2, c2, w2, place2],
        [edge, vmem(4, SUBS, LANES)],
    )
    pieces = [rhs3[None]]
    while sum(piece.shape[0] for piece in pieces) < group:
        pieces = span_stage(mesh, pieces)
    vec3 = vmem(4, group, LANES)
    x2, out = call(
        lambda *refs: coarse_solve(group, *refs),
        [vec2, tile],
        pieces + [v3, c3, m3, x2, w2, agg2, send2],
        [vec3, vec3, vec3, pad2],
    )
    arrived = exchange(mesh, out, near)
    x2, d2, out = middle_next(0, arrived, x2, x2)
    arrived = exchange(mesh, out, near)
    x2, d2, out = middle_next(1, arrived, x2, d2)
    arrived = exchange(mesh, out, near)
    x1, out = call(
        lambda *refs: middle_prolong(factors[2], *refs),
        [vec1, tile],
        arrived + [b2, m2, x2, d2, v2, c2, x1, w1, agg1, send1],
        [edge, vmem(4, SUBS, LANES), pad1],
    )
    for which in range(KSM):
        arrived = exchange(mesh, out, near)
        resid = fine_part(x1)
        x1, d1, out = fine_next(which, arrived, resid, x1, d1)
    arrived = exchange(mesh, out, near)
    resid = fine_part(x1)
    rows = shape(4 * lines, LANES)
    solved, left = call(fine_finish, [rows, rows], arrived + [resid, v1, c1, x1], [edge])
    return from_native(solved, lines), from_native(left, lines)


def native_columns(columns):
    lines = columns.shape[1] // LANES
    return jnp.swapaxes(columns.reshape(NNZ, lines, LANES), 0, 1).reshape(-1, LANES)


def solution(mesh):
    both = ("stream", "span")
    in_specs = (
        P(None, both),
        P(None, None, None, both),
        P(None, both),
        P(None, both),
        P(both, None),
        P(None, None, both),
        P(None, None, None, both),
        P(None, both),
        P(None, both),
        P(both, None),
        P(None, None, both),
        P(None, None, None, both),
        P(None, both),
    )
    return jax.shard_map(
        lambda *args: per_device(mesh, *args),
        mesh=mesh,
        in_specs=in_specs,
        out_specs=(P(None, both), P(None, both)),
        check_vma=False,
    )
```

```python
import jax
import jax.numpy as jnp
from jax import lax
from jax.experimental import pallas as pl
from jax.experimental.pallas import tpu as pltpu
from jax.sharding import PartitionSpec as P

KSM = 3
KC = 4
NNZ = 8
LANES = 128
SUBS = 8

CHEB_CENTRE = 1.0
CHEB_RADIUS = 0.9
AXES = ("stream", "span")
F32 = jnp.float32
I32 = jnp.int32


def cheb_factors(degree):
    sigma = CHEB_CENTRE / CHEB_RADIUS
    rho = 1.0 / sigma
    factors = [(0.0, 1.0 / CHEB_CENTRE)]
    for _ in range(degree - 1):
        rho_next = 1.0 / (2.0 * sigma - rho)
        factors.append((rho_next * rho, 2.0 * rho_next / CHEB_RADIUS))
        rho = rho_next
    return factors


def tile_iota(dim):
    return lax.broadcasted_iota(I32, (SUBS, LANES), dim)


def pick(line, lane):
    return jnp.take_along_axis(line, lane, axis=1, mode="promise_in_bounds")


def wide(line):
    return jnp.broadcast_to(line, (SUBS, LANES))


def pick_lines(lines, high, lane, first=0):
    result = jnp.zeros((SUBS, LANES), F32)
    for r, line in enumerate(lines):
        result = jnp.where(high == first + r, pick(line, lane), result)
    return result


def halo_lines(arrivals, edge_ref):
    s_odd, p_odd, s_even, p_even, which = [r[...] for r in arrivals]
    upper = tile_iota(0) < 4
    even = jnp.where(upper, s_even, p_even)
    odd = jnp.where(upper, s_odd, p_odd)
    edge_ref[...] = jnp.where(which == 1, even, jnp.where(which == 2, odd, 0.0))


def outgoing(lines_of, count, sends):
    high, lane = sends >> 7, sends & (LANES - 1)
    return pick_lines([lines_of(r) for r in range(count)], high, lane)


def send_table(s_ref):
    stream = jnp.concatenate([s_ref[pl.ds(1, 1), :], s_ref[pl.ds(0, 1), :]], axis=1)
    span = jnp.concatenate([s_ref[pl.ds(3, 1), :], s_ref[pl.ds(2, 1), :]], axis=1)
    return jnp.where(tile_iota(0) < 4, stream, span)


def duplicate(x):
    return x + pltpu.roll(x, 4, 0)


def fine_start(v_ref, b_ref, s_ref, bo_ref, mo_ref, x_ref, so_ref, out_ref, pad_ref):
    sends = send_table(s_ref)
    so_ref[...] = sends
    lines = bo_ref.shape[1]
    for i in range(4):
        for h in range(lines // SUBS):
            rows = pl.ds(h * SUBS, SUBS)
            native = pl.ds(h * SUBS * 4 + i, SUBS, stride=4)
            b = b_ref[native, :]
            m = 1.0 / v_ref[pl.ds((i * lines + h * SUBS) * 4 + i, SUBS, stride=4), :]
            x = m * b
            bo_ref[i, rows, :] = b
            mo_ref[i, rows, :] = m
            x_ref[i, rows, :] = x
            for twice in range(2):
                pad_ref[pl.ds((twice * 4 + i) * lines + h * SUBS, SUBS), :] = x
    out_ref[...] = outgoing(
        lambda r: pad_ref[pl.ds(r, SUBS, stride=lines), :], lines, sends
    )


def fine_prepare(v_ref, c_ref, _, vo_ref, co_ref):
    lines = vo_ref.shape[3]
    halves = lines // SUBS

    def body(ki, carry):
        k, i = ki // 4, ki % 4
        for j in range(4):
            for h in range(halves):
                start = ki * (lines * 4) + h * SUBS * 4 + j
                vo_ref[k, i, j, pl.ds(h * SUBS, SUBS), :] = v_ref[
                    pl.ds(start, SUBS, stride=4), :
                ]
        return carry

    lax.fori_loop(0, NNZ * 4, body, 0)
    for k in range(NNZ):
        for h in range(halves):
            co_ref[k, pl.ds(h * SUBS, SUBS), :] = c_ref[
                pl.ds(h * SUBS * NNZ + k, SUBS, stride=NNZ), :
            ]


def fine_local(x_ref, b_ref, v_ref, c_ref, r_ref, line_ref):
    lines = x_ref.shape[1]
    halves = lines // SUBS
    for j in range(4):
        for r in range(lines):
            line_ref[j, r] = wide(x_ref[j, pl.ds(r, 1), :])
    acc = []
    for h in range(halves):
        rows = pl.ds(h * SUBS, SUBS)
        for i in range(4):
            total = b_ref[i, rows, :]
            for j in range(4):
                total = total - v_ref[0, i, j, rows, :] * x_ref[j, rows, :]
            acc.append(total)

    def body(k, acc):
        acc = list(acc)
        for h in range(halves):
            rows = pl.ds(h * SUBS, SUBS)
            col = c_ref[k, rows, :]
            high, lane = col >> 7, col & (LANES - 1)
            for j in range(4):
                got = pick_lines([line_ref[j, r] for r in range(lines)], high, lane)
                for i in range(4):
                    acc[4 * h + i] = acc[4 * h + i] - v_ref[k, i, j, rows, :] * got
        return tuple(acc)

    acc = lax.fori_loop(1, NNZ, body, tuple(acc))
    for h in range(halves):
        for i in range(4):
            r_ref[i, pl.ds(h * SUBS, SUBS), :] = acc[4 * h + i]


def fine_remote(arrivals, r_ref, v_ref, c_ref, edge_ref):
    lines = r_ref.shape[1]
    halves = lines // SUBS
    halo_lines(arrivals, edge_ref)
    edges = [[wide(edge_ref[pl.ds(4 * e + j, 1), :]) for e in range(2)] for j in range(4)]
    result = []
    for h in range(halves):
        rows = pl.ds(h * SUBS, SUBS)
        acc = [r_ref[i, rows, :] for i in range(4)]
        for k in range(1, NNZ):
            col = c_ref[k, rows, :]
            high, lane = col >> 7, col & (LANES - 1)
            for j in range(4):
                got = pick_lines(edges[j], high, lane, lines)
                for i in range(4):
                    acc[i] = acc[i] - v_ref[k, i, j, rows, :] * got
        result.append(acc)
    return result


def fine_step(factors, *refs):
    arrivals = refs[:5]
    (r_ref, v_ref, c_ref, m_ref, x_ref, d_ref, s_ref, xo_ref, do_ref, out_ref, edge_ref, pad_ref) = refs[5:]
    keep, gain = factors
    lines = r_ref.shape[1]
    resid = fine_remote(arrivals, r_ref, v_ref, c_ref, edge_ref)
    for h in range(lines // SUBS):
        rows = pl.ds(h * SUBS, SUBS)
        for i in range(4):
            d = gain * (m_ref[i, rows, :] * resid[h][i])
            if keep:
                d = keep * d_ref[i, rows, :] + d
            x = x_ref[i, rows, :] + d
            do_ref[i, rows, :] = d
            xo_ref[i, rows, :] = x
            for twice in range(2):
                pad_ref[pl.ds((twice * 4 + i) * lines + h * SUBS, SUBS), :] = x
    out_ref[...] = outgoing(
        lambda r: pad_ref[pl.ds(r, SUBS, stride=lines), :], lines, s_ref[...]
    )


def fine_finish(*refs):
    arrivals = refs[:5]
    r_ref, v_ref, c_ref, x_ref, so_ref, ro_ref, edge_ref = refs[5:]
    lines = r_ref.shape[1]
    resid = fine_remote(arrivals, r_ref, v_ref, c_ref, edge_ref)
    for h in range(lines // SUBS):
        for i in range(4):
            native = pl.ds(h * SUBS * 4 + i, SUBS, stride=4)
            so_ref[native, :] = x_ref[i, pl.ds(h * SUBS, SUBS), :]
            ro_ref[native, :] = resid[h][i]


def fine_restrict(*refs):
    arrivals = refs[:5]
    (r_ref, v_ref, c_ref, w_ref, p_ref, m2_ref, s2_ref, b2_ref, x2_ref, out_ref, edge_ref, line_ref, pad_ref) = refs[5:]
    lines = r_ref.shape[1]
    resid = fine_remote(arrivals, r_ref, v_ref, c_ref, edge_ref)
    for h in range(lines // SUBS):
        rows = pl.ds(h * SUBS, SUBS)
        for j in range(4):
            total = w_ref[0, j, rows, :] * resid[h][0]
            for i in range(1, 4):
                total = total + w_ref[i, j, rows, :] * resid[h][i]
            line_ref[j, rows, :] = total
    for j in range(4):
        total = None
        source = [wide(line_ref[j, pl.ds(r, 1), :]) for r in range(lines)]
        for part in range(2):
            place = p_ref[part]
            got = pick_lines(source, place >> 7, place & (LANES - 1))
            total = got if total is None else total + got
        b2 = duplicate(total)
        x2 = m2_ref[j] * b2
        b2_ref[j] = b2
        x2_ref[j] = x2
        middle_pad(pad_ref, j, x2)
    middle_out(out_ref, pad_ref, s2_ref)


def inverse_order(o_row, lines):
    count = lines * LANES
    high, lane = o_row >> 7, o_row & (LANES - 1)
    coarse = lax.broadcasted_iota(I32, (1, count), 1) >> 2
    here = lax.broadcasted_iota(I32, (lines, count), 0) == high
    upper = jnp.where(here, (coarse >> 4).astype(F32), 0.0)
    lower = jnp.where(here, (coarse & 15).astype(F32), 0.0)
    left = jnp.concatenate([upper, lower], axis=0).astype(jnp.bfloat16)
    right = jnp.where(
        lax.broadcasted_iota(I32, (LANES, count), 0) == lane, 1.0, 0.0
    ).astype(jnp.bfloat16)
    found = lax.dot_general(
        left, right, (((1,), (1,)), ((), ())), preferred_element_type=F32
    )
    return (found[:lines] * 16.0 + found[lines:]).astype(I32)


def pick_order(sources, unit):
    lane = tile_iota(1)
    place = 4 * (lane & 31) + unit
    result = jnp.zeros((SUBS, LANES), I32)
    for q, source in enumerate(sources):
        result = jnp.where((lane >> 5) == q, pick(source, place), result)
    return result


def fine_tables(w_ref, row_ref, o_ref, _, wo_ref, agg_ref, place_ref):
    lines = o_ref.shape[0]
    for i in range(4):
        for j in range(4):
            for h in range(lines // SUBS):
                start = (i * lines + h * SUBS) * 4 + j
                wo_ref[i, j, pl.ds(h * SUBS, SUBS), :] = w_ref[pl.ds(start, SUBS, stride=4), :]
    agg_ref[...] = inverse_order(row_ref[...], lines)
    sources = []
    for q in range(4):
        four = o_ref[pl.ds(q, 4, stride=4), :]
        sources.append(jnp.concatenate([four, four], axis=0))
    for part in range(2):
        place_ref[part] = pick_order(sources, (tile_iota(0) >> 2) + 2 * part)


def middle_tables(v_ref, c_ref, w_ref, row_ref, o_ref, s_ref, _, so_ref, vo_ref, co_ref, mo_ref, wo_ref, agg_ref, place_ref):
    lines = o_ref.shape[0]
    so_ref[...] = send_table(s_ref)

    def body(ki, carry):
        k, i = ki // 4, ki % 4
        kp, i2 = ki // 4, ki % 4
        for j in range(4):
            for odd in range(2):
                start = ((2 * kp + odd) * 4 + i2) * (lines * 4) + j
                vo_ref[k, i, j, pl.ds(4 * odd, 4), :] = v_ref[pl.ds(start, 4, stride=4), :]
        return carry

    lax.fori_loop(0, NNZ // 2 * 4, body, 0)
    for kp in range(NNZ // 2):
        for odd in range(2):
            co_ref[kp, pl.ds(4 * odd, 4), :] = c_ref[pl.ds(2 * kp + odd, 4, stride=NNZ), :]
    for i in range(4):
        four = 1.0 / v_ref[pl.ds(i * lines * 4 + i, 4, stride=4), :]
        mo_ref[i, pl.ds(0, 4), :] = four
        mo_ref[i, pl.ds(4, 4), :] = four
        for j in range(4):
            four = w_ref[pl.ds(i * lines * 4 + j, 4, stride=4), :]
            wo_ref[i, j, pl.ds(0, 4), :] = four
            wo_ref[i, j, pl.ds(4, 4), :] = four
    agg = inverse_order(row_ref[...], lines)
    agg_ref[...] = jnp.concatenate([agg, agg], axis=0)
    sources = [wide(o_ref[pl.ds(q, 1), :]) for q in range(4)]
    place_ref[...] = pick_order(sources, tile_iota(0) & 3)


def middle_pad(pad_ref, j, x):
    for twice in range(2):
        pad_ref[pl.ds((twice * 4 + j) * SUBS, SUBS), :] = x


def middle_out(out_ref, pad_ref, s_ref):
    out_ref[...] = outgoing(
        lambda r: pad_ref[pl.ds(r, SUBS, stride=SUBS), :], 4, s_ref[...]
    )


def middle_residual(arrivals, b_ref, x_ref, v_ref, c_ref, edge_ref):
    halo_lines(arrivals, edge_ref)
    acc = [jnp.zeros((SUBS, LANES), F32) for _ in range(4)]
    for j in range(4):
        source = [wide(x_ref[j, pl.ds(r, 1), :]) for r in range(4)]
        source += [wide(edge_ref[pl.ds(4 * e + j, 1), :]) for e in range(2)]
        for kp in range(NNZ // 2):
            col = c_ref[kp]
            got = pick_lines(source, col >> 7, col & (LANES - 1))
            for i in range(4):
                acc[i] = acc[i] + v_ref[kp, i, j] * got
    return [b_ref[i] - duplicate(acc[i]) for i in range(4)]


def middle_update(factors, resid, m_ref, x_ref, d_ref):
    keep, gain = factors
    xs, ds = [], []
    for i in range(4):
        d = gain * (m_ref[i] * resid[i])
        if keep:
            d = keep * d_ref[i] + d
        ds.append(d)
        xs.append(x_ref[i] + d)
    return xs, ds


def middle_step(factors, *refs):
    arrivals = refs[:5]
    (b_ref, m_ref, x_ref, d_ref, v_ref, c_ref, s_ref, xo_ref, do_ref, out_ref, edge_ref, pad_ref) = refs[5:]
    resid = middle_residual(arrivals, b_ref, x_ref, v_ref, c_ref, edge_ref)
    xs, ds = middle_update(factors, resid, m_ref, x_ref, d_ref)
    for i in range(4):
        xo_ref[i] = xs[i]
        do_ref[i] = ds[i]
        middle_pad(pad_ref, i, xs[i])
    middle_out(out_ref, pad_ref, s_ref)


def middle_restrict(*refs):
    arrivals = refs[:5]
    b_ref, x_ref, v_ref, c_ref, w_ref, p_ref, out_ref, edge_ref, line_ref = refs[5:]
    resid = middle_residual(arrivals, b_ref, x_ref, v_ref, c_ref, edge_ref)
    place = p_ref[...]
    high, lane = place >> 7, place & (LANES - 1)
    for j in range(4):
        total = w_ref[0, j] * resid[0]
        for i in range(1, 4):
            total = total + w_ref[i, j] * resid[i]
        line_ref[j] = total
        source = [wide(line_ref[j, pl.ds(r, 1), :]) for r in range(4)]
        got = pick_lines(source, high, lane)
        got = got + pltpu.roll(got, 2, 0)
        got = got + pltpu.roll(got, 1, 0)
        out_ref[pl.ds(j, 1), :] = got[0:1]
        out_ref[pl.ds(4 + j, 1), :] = got[0:1]


def middle_prolong(factors, *refs):
    arrivals = refs[:5]
    (b_ref, m_ref, x_ref, d_ref, v_ref, c_ref, x1_ref, w_ref, agg_ref, s_ref, xo_ref, out_ref, edge_ref, line_ref, pad_ref) = refs[5:]
    lines = x1_ref.shape[1]
    resid = middle_residual(arrivals, b_ref, x_ref, v_ref, c_ref, edge_ref)
    xs, _ = middle_update(factors, resid, m_ref, x_ref, d_ref)
    for j in range(4):
        line_ref[j] = xs[j]
    for h in range(lines // SUBS):
        rows = pl.ds(h * SUBS, SUBS)
        agg = agg_ref[rows, :]
        high, lane = agg >> 7, agg & (LANES - 1)
        spread = [
            pick_lines([wide(line_ref[j, pl.ds(r, 1), :]) for r in range(4)], high, lane)
            for j in range(4)
        ]
        for i in range(4):
            placed = w_ref[i, 0, rows, :] * spread[0]
            for j in range(1, 4):
                placed = placed + w_ref[i, j, rows, :] * spread[j]
            x = x1_ref[i, rows, :] + placed
            xo_ref[i, rows, :] = x
            for twice in range(2):
                pad_ref[pl.ds((twice * 4 + i) * lines + h * SUBS, SUBS), :] = x
    out_ref[...] = outgoing(
        lambda r: pad_ref[pl.ds(r, SUBS, stride=lines), :], lines, s_ref[...]
    )


def coarse_tables(group, *refs):
    vo_ref, co_ref, mo_ref, pad_ref = refs[-4:]
    me = refs[0][0]
    for piece, places in zip(refs[1:-5], span_places(group)):
        for t, place in enumerate(places):
            pad_ref[place] = piece[t]
    for h in range(group // SUBS):
        rows = pl.ds(h * SUBS, SUBS)
        for ki in range(NNZ * 4):
            k, i = ki // 4, ki % 4
            for j in range(4):
                tile = pad_ref[rows, ki * 4 + j, :]
                vo_ref[k, i, j, rows, :] = tile
                if k == 0 and i == j:
                    mo_ref[i, rows, :] = 1.0 / tile
        for k in range(NNZ):
            col = pad_ref[rows, NNZ * 16 + k, :].astype(I32)
            co_ref[k, rows, :] = ((col >> 7) ^ me) * LANES + (col & (LANES - 1))


def coarse_solve(group, *refs):
    (v_ref, c_ref, m_ref, x2_ref, w_ref, agg_ref, s_ref, xo_ref, out_ref, b_ref, x_ref, d_ref, pad_ref) = refs[-13:]
    for piece, places in zip(refs[:-13], span_places(group)):
        for t, place in enumerate(places):
            for j in range(4):
                b_ref[j, pl.ds(place, 1), :] = piece[t, pl.ds(j, 1), :]
    blocks = group // SUBS
    for j in range(4):
        first = m_ref[j] * b_ref[j]
        x_ref[j] = first
        d_ref[j] = first
    for keep, gain in cheb_factors(KC)[1:]:
        resid = []
        for h in range(blocks):
            rows = pl.ds(h * SUBS, SUBS)
            acc = [b_ref[i, rows, :] for i in range(4)]
            for k in range(NNZ):
                col = c_ref[k, rows, :]
                high, lane = col >> 7, col & (LANES - 1)
                for j in range(4):
                    if k:
                        got = pick_lines(
                            [wide(x_ref[j, pl.ds(r, 1), :]) for r in range(group)], high, lane
                        )
                    else:
                        got = x_ref[j, rows, :]
                    for i in range(4):
                        acc[i] = acc[i] - v_ref[k, i, j, rows, :] * got
            resid.append(acc)
        for h in range(blocks):
            rows = pl.ds(h * SUBS, SUBS)
            for i in range(4):
                d = keep * d_ref[i, rows, :] + gain * (m_ref[i, rows, :] * resid[h][i])
                d_ref[i, rows, :] = d
                x_ref[i, rows, :] = x_ref[i, rows, :] + d
    lane = agg_ref[...]
    spread = [pick(wide(x_ref[j, pl.ds(0, 1), :]), lane) for j in range(4)]
    for i in range(4):
        x = x2_ref[i]
        for j in range(4):
            x = x + w_ref[i, j] * spread[j]
        xo_ref[i] = x
        middle_pad(pad_ref, i, x)
    middle_out(out_ref, pad_ref, s_ref)


def call(body, outs, args, scratch=(), free=(), smem=()):
    specs = []
    for index in range(len(args)):
        if index in free:
            specs.append(pl.BlockSpec(memory_space=pl.ANY))
        elif index in smem:
            specs.append(pl.BlockSpec(memory_space=pltpu.SMEM))
        else:
            specs.append(pl.BlockSpec(memory_space=pltpu.VMEM))
    single = not isinstance(outs, (list, tuple))
    shapes = [outs] if single else list(outs)
    result = pl.pallas_call(
        body,
        out_shape=shapes,
        in_specs=specs,
        out_specs=[pl.BlockSpec(memory_space=pltpu.VMEM) for _ in shapes],
        scratch_shapes=list(scratch),
        compiler_params=pltpu.CompilerParams(vmem_limit_bytes=16 * 2**20),
    )(*args)
    return result[0] if single else result


def shape(*dims, dtype=F32):
    return jax.ShapeDtypeStruct(dims, dtype)


def vmem(*dims, dtype=F32):
    return pltpu.VMEM(dims, dtype)


def native_rows(x):
    lines = x.shape[-1] // LANES
    split = x.reshape(x.shape[:-1] + (lines, LANES))
    return jnp.swapaxes(split, -2, -3).reshape(-1, LANES)


def from_native(rows, lines):
    return jnp.swapaxes(rows.reshape(lines, 4, LANES), 0, 1).reshape(4, lines * LANES)


def exchange(mesh, out, which):
    slabs, count = mesh.shape["stream"], mesh.shape["span"]

    def partner(index, size, odd, closed):
        other = index ^ 1 if not odd else (index + 1 if index % 2 else index - 1)
        return other % size if closed or 0 <= other < size else index

    def swap(odd_s, odd_p):
        pairs = []
        for a in range(slabs):
            for b in range(count):
                to_a = a if odd_s is None else partner(a, slabs, odd_s, True)
                to_b = b if odd_p is None else partner(b, count, odd_p, False)
                pairs.append((a * count + b, to_a * count + to_b))
        return lax.ppermute(out, AXES, pairs)

    return [swap(True, None), swap(None, True), swap(False, None), swap(None, False), which]


def halo_choice(a, b, count):
    row, lane = (lax.broadcasted_iota(I32, (SUBS, LANES), d) for d in range(2))
    left = lane < LANES // 2
    index = jnp.where(row < 4, a, b)
    even = left == (index % 2 == 1)
    outside = (row >= 4) & jnp.where(left, b == 0, b == count - 1)
    return jnp.where(outside, 0, jnp.where(even, 1, 2)).astype(I32)


def span_places(group):
    places = [[0]]
    mask = group // 2
    while mask:
        places.append([mask ^ m for piece in places for m in piece])
        mask //= 2
    return places


def span_stage(mesh, pieces):
    slabs, count = mesh.shape["stream"], mesh.shape["span"]
    held = jnp.concatenate(pieces)
    mask = count // 2 // held.shape[0]
    pairs = [
        (a * count + b, a * count + (b ^ mask)) for a in range(slabs) for b in range(count)
    ]
    return pieces + [lax.ppermute(held, AXES, pairs)]


def per_device(mesh, right_side, fine_values, fine_columns, fine_sends, fine_order, fine_weights, middle_values, middle_columns, middle_sends, middle_order, middle_weights, coarsest_values, coarsest_columns):
    group = mesh.shape["span"]
    lines = right_side.shape[1] // LANES
    tile = shape(SUBS, LANES)
    vec1 = shape(4, lines, LANES)
    vec2 = shape(4, SUBS, LANES)
    edge = vmem(SUBS, LANES)
    pad1 = vmem(SUBS * lines, LANES)
    pad2 = vmem(SUBS * SUBS, LANES)
    factors = cheb_factors(KSM)
    me = lax.axis_index("span").astype(I32)
    choice = halo_choice(lax.axis_index("stream").astype(I32), me, group)
    values1 = native_rows(fine_values)
    values2 = native_rows(middle_values)

    b1, m1, x1, send1, out = call(
        fine_start,
        [vec1, vec1, vec1, shape(SUBS, LANES, dtype=I32), tile],
        [values1, native_rows(right_side), fine_sends],
        [pad1],
    )
    d1 = x1

    own3 = jnp.concatenate(
        [coarsest_values.reshape(NNZ * 16, LANES), coarsest_columns.astype(F32)], axis=0
    )
    v1, c1 = call(
        fine_prepare,
        [shape(NNZ, 4, 4, lines, LANES), shape(NNZ, lines, LANES, dtype=I32)],
        [values1, native_columns(fine_columns), out],
        free=(2,),
    )

    def fine_part(x):
        return call(fine_local, vec1, [x, b1, v1, c1], [vmem(4, lines, SUBS, LANES)])

    def fine_next(which, arrived, resid, x, d, after=()):
        args = arrived + [resid, v1, c1, m1, x, d, send1]
        return call(
            lambda *refs: fine_step(factors[which], *(refs[: len(args)] + refs[len(args) + len(after) :])),
            [vec1, vec1, tile],
            args + list(after),
            [edge, pad1],
            free=range(len(args), len(args) + len(after)),
        )

    arrived = exchange(mesh, out, choice)
    own3, _ = lax.optimization_barrier((own3, out))
    pieces3 = span_stage(mesh, [own3[None]])
    resid = fine_part(x1)
    x1, d1, out = fine_next(1, arrived, resid, x1, d1)

    arrived = exchange(mesh, out, choice)
    pieces3, _ = lax.optimization_barrier((pieces3, out))
    pieces3 = span_stage(mesh, pieces3)
    resid = fine_part(x1)
    w1, agg1, place1 = call(
        fine_tables,
        [shape(4, 4, lines, LANES), shape(lines, LANES, dtype=I32), shape(2, SUBS, LANES, dtype=I32)],
        [native_rows(fine_weights), fine_order, fine_order.reshape(lines, LANES), out],
        free=(3,),
    )
    x1, d1, out = fine_next(2, arrived, resid, x1, d1, [pieces3[1]])

    arrived = exchange(mesh, out, choice)
    pieces3, _ = lax.optimization_barrier((pieces3, out))
    while sum(piece.shape[0] for piece in pieces3) < group:
        pieces3 = span_stage(mesh, pieces3)
    resid = fine_part(x1)
    send2, v2, c2, m2, w2, agg2, place2 = call(
        middle_tables,
        [
            shape(SUBS, LANES, dtype=I32),
            shape(NNZ // 2, 4, 4, SUBS, LANES),
            shape(NNZ // 2, SUBS, LANES, dtype=I32),
            vec2,
            shape(4, 4, SUBS, LANES),
            shape(SUBS, LANES, dtype=I32),
            shape(SUBS, LANES, dtype=I32),
        ],
        [values2, native_columns(middle_columns), native_rows(middle_weights), middle_order, middle_order.reshape(-1, LANES), middle_sends, out],
        free=(6,),
    )
    b2, x2, out = call(
        fine_restrict,
        [vec2, vec2, tile],
        arrived + [resid, v1, c1, w1, place1, m2, send2],
        [edge, vmem(4, lines, LANES), pad2],
    )
    d2 = x2

    def middle_next(which, arrived, x, d, after=()):
        args = arrived + [b2, m2, x, d, v2, c2, send2]
        return call(
            lambda *refs: middle_step(factors[which], *(refs[: len(args)] + refs[len(args) + len(after) :])),
            [vec2, vec2, tile],
            args + list(after),
            [edge, pad2],
            free=range(len(args), len(args) + len(after)),
        )

    arrived = exchange(mesh, out, choice)
    v3, c3, m3 = call(
        lambda *refs: coarse_tables(group, *refs),
        [shape(NNZ, 4, 4, group, LANES), shape(NNZ, group, LANES, dtype=I32), shape(4, group, LANES)],
        [me.reshape(1)] + pieces3 + [out],
        [vmem(group, NNZ * 17, LANES)],
        free=(1 + len(pieces3),),
        smem=(0,),
    )
    x2, d2, out = middle_next(1, arrived, x2, d2, [m3])
    arrived = exchange(mesh, out, choice)
    x2, d2, out = middle_next(2, arrived, x2, d2)
    arrived = exchange(mesh, out, choice)
    rhs3 = call(
        middle_restrict,
        tile,
        arrived + [b2, x2, v2, c2, w2, place2],
        [edge, vmem(4, SUBS, LANES)],
    )
    pieces = [rhs3[None]]
    while sum(piece.shape[0] for piece in pieces) < group:
        pieces = span_stage(mesh, pieces)
    vec3 = vmem(4, group, LANES)
    x2, out = call(
        lambda *refs: coarse_solve(group, *refs),
        [vec2, tile],
        pieces + [v3, c3, m3, x2, w2, agg2, send2],
        [vec3, vec3, vec3, pad2],
    )
    arrived = exchange(mesh, out, choice)
    x2, d2, out = middle_next(0, arrived, x2, x2)
    arrived = exchange(mesh, out, choice)
    x2, d2, out = middle_next(1, arrived, x2, d2)
    arrived = exchange(mesh, out, choice)
    x1, out = call(
        lambda *refs: middle_prolong(factors[2], *refs),
        [vec1, tile],
        arrived + [b2, m2, x2, d2, v2, c2, x1, w1, agg1, send1],
        [edge, vmem(4, SUBS, LANES), pad1],
    )
    for which in range(KSM):
        arrived = exchange(mesh, out, choice)
        resid = fine_part(x1)
        x1, d1, out = fine_next(which, arrived, resid, x1, d1)
    arrived = exchange(mesh, out, choice)
    resid = fine_part(x1)
    rows = shape(4 * lines, LANES)
    solved, left = call(fine_finish, [rows, rows], arrived + [resid, v1, c1, x1], [edge])
    return from_native(solved, lines), from_native(left, lines)


def native_columns(columns):
    lines = columns.shape[1] // LANES
    return jnp.swapaxes(columns.reshape(NNZ, lines, LANES), 0, 1).reshape(-1, LANES)


def solution(mesh):
    both = ("stream", "span")
    in_specs = (
        P(None, both),
        P(None, None, None, both),
        P(None, both),
        P(None, both),
        P(both, None),
        P(None, None, both),
        P(None, None, None, both),
        P(None, both),
        P(None, both),
        P(both, None),
        P(None, None, both),
        P(None, None, None, both),
        P(None, both),
    )
    return jax.shard_map(
        lambda *args: per_device(mesh, *args),
        mesh=mesh,
        in_specs=in_specs,
        out_specs=(P(None, both), P(None, both)),
        check_vma=False,
    )
```

```python
import jax
import jax.numpy as jnp
from jax import lax
from jax.experimental import pallas as pl
from jax.experimental.pallas import tpu as pltpu
from jax.sharding import PartitionSpec as P

KSM = 3
KC = 4
NNZ = 8
LANES = 128
SUBS = 8

CHEB_CENTRE = 1.0
CHEB_RADIUS = 0.9
AXES = ("stream", "span")
F32 = jnp.float32
I32 = jnp.int32


def cheb_factors(degree):
    sigma = CHEB_CENTRE / CHEB_RADIUS
    rho = 1.0 / sigma
    factors = [(0.0, 1.0 / CHEB_CENTRE)]
    for _ in range(degree - 1):
        rho_next = 1.0 / (2.0 * sigma - rho)
        factors.append((rho_next * rho, 2.0 * rho_next / CHEB_RADIUS))
        rho = rho_next
    return factors


def tile_iota(dim):
    return lax.broadcasted_iota(I32, (SUBS, LANES), dim)


def pick(line, lane):
    return jnp.take_along_axis(line, lane, axis=1, mode="promise_in_bounds")


def wide(line):
    return jnp.broadcast_to(line, (SUBS, LANES))


def pick_lines(lines, high, lane, first=0):
    result = jnp.zeros((SUBS, LANES), F32)
    for r, line in enumerate(lines):
        result = jnp.where(high == first + r, pick(line, lane), result)
    return result


def halo_lines(arrivals, edge_ref):
    s_odd, p_odd, s_even, p_even, which = [r[...] for r in arrivals]
    upper = tile_iota(0) < 4
    even = jnp.where(upper, s_even, p_even)
    odd = jnp.where(upper, s_odd, p_odd)
    edge_ref[...] = jnp.where(which == 1, even, jnp.where(which == 2, odd, 0.0))


def outgoing(lines_of, count, sends):
    high, lane = sends >> 7, sends & (LANES - 1)
    return pick_lines([lines_of(r) for r in range(count)], high, lane)


def send_table(s_ref):
    stream = jnp.concatenate([s_ref[pl.ds(1, 1), :], s_ref[pl.ds(0, 1), :]], axis=1)
    span = jnp.concatenate([s_ref[pl.ds(3, 1), :], s_ref[pl.ds(2, 1), :]], axis=1)
    return jnp.where(tile_iota(0) < 4, stream, span)


def duplicate(x):
    return x + pltpu.roll(x, 4, 0)


def fine_start(v_ref, b_ref, s_ref, bo_ref, mo_ref, x_ref, so_ref, out_ref, pad_ref):
    sends = send_table(s_ref)
    so_ref[...] = sends
    lines = bo_ref.shape[1]
    for i in range(4):
        for h in range(lines // SUBS):
            rows = pl.ds(h * SUBS, SUBS)
            native = pl.ds(h * SUBS * 4 + i, SUBS, stride=4)
            b = b_ref[native, :]
            m = 1.0 / v_ref[pl.ds((i * lines + h * SUBS) * 4 + i, SUBS, stride=4), :]
            x = m * b
            bo_ref[i, rows, :] = b
            mo_ref[i, rows, :] = m
            x_ref[i, rows, :] = x
            for twice in range(2):
                pad_ref[pl.ds((twice * 4 + i) * lines + h * SUBS, SUBS), :] = x
    out_ref[...] = outgoing(
        lambda r: pad_ref[pl.ds(r, SUBS, stride=lines), :], lines, sends
    )


def fine_prepare(v_ref, c_ref, _, vo_ref, co_ref):
    lines = vo_ref.shape[3]
    halves = lines // SUBS

    def body(ki, carry):
        k, i = ki // 4, ki % 4
        for j in range(4):
            for h in range(halves):
                start = ki * (lines * 4) + h * SUBS * 4 + j
                vo_ref[k, i, j, pl.ds(h * SUBS, SUBS), :] = v_ref[
                    pl.ds(start, SUBS, stride=4), :
                ]
        return carry

    lax.fori_loop(0, NNZ * 4, body, 0)
    for k in range(NNZ):
        for h in range(halves):
            co_ref[k, pl.ds(h * SUBS, SUBS), :] = c_ref[
                pl.ds(h * SUBS * NNZ + k, SUBS, stride=NNZ), :
            ]


def fine_local(x_ref, b_ref, v_ref, c_ref, r_ref, line_ref):
    lines = x_ref.shape[1]
    halves = lines // SUBS
    for j in range(4):
        for r in range(lines):
            line_ref[j, r] = wide(x_ref[j, pl.ds(r, 1), :])
    acc = []
    for h in range(halves):
        rows = pl.ds(h * SUBS, SUBS)
        for i in range(4):
            total = b_ref[i, rows, :]
            for j in range(4):
                total = total - v_ref[0, i, j, rows, :] * x_ref[j, rows, :]
            acc.append(total)

    def body(k, acc):
        acc = list(acc)
        for h in range(halves):
            rows = pl.ds(h * SUBS, SUBS)
            col = c_ref[k, rows, :]
            high, lane = col >> 7, col & (LANES - 1)
            for j in range(4):
                got = pick_lines([line_ref[j, r] for r in range(lines)], high, lane)
                for i in range(4):
                    acc[4 * h + i] = acc[4 * h + i] - v_ref[k, i, j, rows, :] * got
        return tuple(acc)

    acc = lax.fori_loop(1, NNZ, body, tuple(acc))
    for h in range(halves):
        for i in range(4):
            r_ref[i, pl.ds(h * SUBS, SUBS), :] = acc[4 * h + i]


def fine_remote(arrivals, r_ref, v_ref, c_ref, edge_ref):
    lines = r_ref.shape[1]
    halves = lines // SUBS
    halo_lines(arrivals, edge_ref)
    edges = [[wide(edge_ref[pl.ds(4 * e + j, 1), :]) for e in range(2)] for j in range(4)]
    result = []
    for h in range(halves):
        rows = pl.ds(h * SUBS, SUBS)
        acc = [r_ref[i, rows, :] for i in range(4)]
        for k in range(1, NNZ):
            col = c_ref[k, rows, :]
            high, lane = col >> 7, col & (LANES - 1)
            for j in range(4):
                got = pick_lines(edges[j], high, lane, lines)
                for i in range(4):
                    acc[i] = acc[i] - v_ref[k, i, j, rows, :] * got
        result.append(acc)
    return result


def fine_step(factors, last, *refs):
    arrivals = refs[:5]
    r_ref, v_ref, c_ref, m_ref, x_ref, d_ref, s_ref, xo_ref, out_ref = refs[5:14]
    do_ref = refs[14] if last is False else None
    edge_ref, pad_ref = refs[-2:]
    keep, gain = factors
    lines = r_ref.shape[1]
    resid = fine_remote(arrivals, r_ref, v_ref, c_ref, edge_ref)
    for h in range(lines // SUBS):
        rows = pl.ds(h * SUBS, SUBS)
        for i in range(4):
            d = gain * (m_ref[i, rows, :] * resid[h][i])
            if keep:
                d = keep * d_ref[i, rows, :] + d
            x = x_ref[i, rows, :] + d
            if not last:
                do_ref[i, rows, :] = d
            xo_ref[i, rows, :] = x
            for twice in range(2):
                pad_ref[pl.ds((twice * 4 + i) * lines + h * SUBS, SUBS), :] = x
    out_ref[...] = outgoing(
        lambda r: pad_ref[pl.ds(r, SUBS, stride=lines), :], lines, s_ref[...]
    )


def fine_finish(*refs):
    arrivals = refs[:5]
    r_ref, v_ref, c_ref, x_ref, so_ref, ro_ref, edge_ref = refs[5:]
    lines = r_ref.shape[1]
    resid = fine_remote(arrivals, r_ref, v_ref, c_ref, edge_ref)
    for h in range(lines // SUBS):
        for i in range(4):
            native = pl.ds(h * SUBS * 4 + i, SUBS, stride=4)
            so_ref[native, :] = x_ref[i, pl.ds(h * SUBS, SUBS), :]
            ro_ref[native, :] = resid[h][i]


def fine_restrict(*refs):
    arrivals = refs[:5]
    (r_ref, v_ref, c_ref, w_ref, p_ref, m2_ref, s2_ref, b2_ref, x2_ref, out_ref, edge_ref, line_ref, pad_ref) = refs[5:]
    lines = r_ref.shape[1]
    resid = fine_remote(arrivals, r_ref, v_ref, c_ref, edge_ref)
    for h in range(lines // SUBS):
        rows = pl.ds(h * SUBS, SUBS)
        for j in range(4):
            total = w_ref[0, j, rows, :] * resid[h][0]
            for i in range(1, 4):
                total = total + w_ref[i, j, rows, :] * resid[h][i]
            line_ref[j, rows, :] = total
    for j in range(4):
        total = None
        source = [wide(line_ref[j, pl.ds(r, 1), :]) for r in range(lines)]
        for part in range(2):
            place = p_ref[part]
            got = pick_lines(source, place >> 7, place & (LANES - 1))
            total = got if total is None else total + got
        b2 = duplicate(total)
        x2 = m2_ref[j] * b2
        b2_ref[j] = b2
        x2_ref[j] = x2
        middle_pad(pad_ref, j, x2)
    middle_out(out_ref, pad_ref, s2_ref)


def inverse_order(o_row, lines):
    count = lines * LANES
    high, lane = o_row >> 7, o_row & (LANES - 1)
    coarse = lax.broadcasted_iota(I32, (1, count), 1) >> 2
    here = lax.broadcasted_iota(I32, (lines, count), 0) == high
    upper = jnp.where(here, (coarse >> 4).astype(F32), 0.0)
    lower = jnp.where(here, (coarse & 15).astype(F32), 0.0)
    left = jnp.concatenate([upper, lower], axis=0).astype(jnp.bfloat16)
    right = jnp.where(
        lax.broadcasted_iota(I32, (LANES, count), 0) == lane, 1.0, 0.0
    ).astype(jnp.bfloat16)
    found = lax.dot_general(
        left, right, (((1,), (1,)), ((), ())), preferred_element_type=F32
    )
    return (found[:lines] * 16.0 + found[lines:]).astype(I32)


def pick_order(sources, unit):
    lane = tile_iota(1)
    place = 4 * (lane & 31) + unit
    result = jnp.zeros((SUBS, LANES), I32)
    for q, source in enumerate(sources):
        result = jnp.where((lane >> 5) == q, pick(source, place), result)
    return result


def fine_tables(w_ref, row_ref, o_ref, _, wo_ref, agg_ref, place_ref):
    lines = o_ref.shape[0]
    for i in range(4):
        for j in range(4):
            for h in range(lines // SUBS):
                start = (i * lines + h * SUBS) * 4 + j
                wo_ref[i, j, pl.ds(h * SUBS, SUBS), :] = w_ref[pl.ds(start, SUBS, stride=4), :]
    agg_ref[...] = inverse_order(row_ref[...], lines)
    sources = []
    for q in range(4):
        four = o_ref[pl.ds(q, 4, stride=4), :]
        sources.append(jnp.concatenate([four, four], axis=0))
    for part in range(2):
        place_ref[part] = pick_order(sources, (tile_iota(0) >> 2) + 2 * part)


def middle_tables(v_ref, c_ref, w_ref, row_ref, o_ref, s_ref, _, so_ref, vo_ref, co_ref, mo_ref, wo_ref, agg_ref, place_ref):
    lines = o_ref.shape[0]
    so_ref[...] = send_table(s_ref)

    def body(ki, carry):
        k, i = ki // 4, ki % 4
        kp, i2 = ki // 4, ki % 4
        for j in range(4):
            for odd in range(2):
                start = ((2 * kp + odd) * 4 + i2) * (lines * 4) + j
                vo_ref[k, i, j, pl.ds(4 * odd, 4), :] = v_ref[pl.ds(start, 4, stride=4), :]
        return carry

    lax.fori_loop(0, NNZ // 2 * 4, body, 0)
    for kp in range(NNZ // 2):
        for odd in range(2):
            co_ref[kp, pl.ds(4 * odd, 4), :] = c_ref[pl.ds(2 * kp + odd, 4, stride=NNZ), :]
    for i in range(4):
        four = 1.0 / v_ref[pl.ds(i * lines * 4 + i, 4, stride=4), :]
        mo_ref[i, pl.ds(0, 4), :] = four
        mo_ref[i, pl.ds(4, 4), :] = four
        for j in range(4):
            four = w_ref[pl.ds(i * lines * 4 + j, 4, stride=4), :]
            wo_ref[i, j, pl.ds(0, 4), :] = four
            wo_ref[i, j, pl.ds(4, 4), :] = four
    agg = inverse_order(row_ref[...], lines)
    agg_ref[...] = jnp.concatenate([agg, agg], axis=0)
    sources = [wide(o_ref[pl.ds(q, 1), :]) for q in range(4)]
    place_ref[...] = pick_order(sources, tile_iota(0) & 3)


def middle_pad(pad_ref, j, x):
    for twice in range(2):
        pad_ref[pl.ds((twice * 4 + j) * SUBS, SUBS), :] = x


def middle_out(out_ref, pad_ref, s_ref):
    out_ref[...] = outgoing(
        lambda r: pad_ref[pl.ds(r, SUBS, stride=SUBS), :], 4, s_ref[...]
    )


def middle_residual(arrivals, b_ref, x_ref, v_ref, c_ref, edge_ref):
    halo_lines(arrivals, edge_ref)
    acc = [jnp.zeros((SUBS, LANES), F32) for _ in range(4)]
    for j in range(4):
        source = [wide(x_ref[j, pl.ds(r, 1), :]) for r in range(4)]
        source += [wide(edge_ref[pl.ds(4 * e + j, 1), :]) for e in range(2)]
        for kp in range(NNZ // 2):
            col = c_ref[kp]
            got = pick_lines(source, col >> 7, col & (LANES - 1))
            for i in range(4):
                acc[i] = acc[i] + v_ref[kp, i, j] * got
    return [b_ref[i] - duplicate(acc[i]) for i in range(4)]


def middle_update(factors, resid, m_ref, x_ref, d_ref):
    keep, gain = factors
    xs, ds = [], []
    for i in range(4):
        d = gain * (m_ref[i] * resid[i])
        if keep:
            d = keep * d_ref[i] + d
        ds.append(d)
        xs.append(x_ref[i] + d)
    return xs, ds


def middle_step(factors, last, *refs):
    arrivals = refs[:5]
    b_ref, m_ref, x_ref, d_ref, v_ref, c_ref, s_ref, xo_ref, out_ref = refs[5:14]
    do_ref = refs[14] if last is False else None
    edge_ref, pad_ref = refs[-2:]
    resid = middle_residual(arrivals, b_ref, x_ref, v_ref, c_ref, edge_ref)
    xs, ds = middle_update(factors, resid, m_ref, x_ref, d_ref)
    for i in range(4):
        xo_ref[i] = xs[i]
        if not last:
            do_ref[i] = ds[i]
        middle_pad(pad_ref, i, xs[i])
    middle_out(out_ref, pad_ref, s_ref)


def middle_restrict(*refs):
    arrivals = refs[:5]
    b_ref, x_ref, v_ref, c_ref, w_ref, p_ref, out_ref, edge_ref, line_ref = refs[5:]
    resid = middle_residual(arrivals, b_ref, x_ref, v_ref, c_ref, edge_ref)
    place = p_ref[...]
    high, lane = place >> 7, place & (LANES - 1)
    for j in range(4):
        total = w_ref[0, j] * resid[0]
        for i in range(1, 4):
            total = total + w_ref[i, j] * resid[i]
        line_ref[j] = total
        source = [wide(line_ref[j, pl.ds(r, 1), :]) for r in range(4)]
        got = pick_lines(source, high, lane)
        got = got + pltpu.roll(got, 2, 0)
        got = got + pltpu.roll(got, 1, 0)
        out_ref[pl.ds(j, 1), :] = got[0:1]
        out_ref[pl.ds(4 + j, 1), :] = got[0:1]


def middle_prolong(factors, *refs):
    arrivals = refs[:5]
    (b_ref, m_ref, x_ref, d_ref, v_ref, c_ref, x1_ref, w_ref, agg_ref, s_ref, xo_ref, out_ref, edge_ref, line_ref, pad_ref) = refs[5:]
    lines = x1_ref.shape[1]
    resid = middle_residual(arrivals, b_ref, x_ref, v_ref, c_ref, edge_ref)
    xs, _ = middle_update(factors, resid, m_ref, x_ref, d_ref)
    for j in range(4):
        line_ref[j] = xs[j]
    for h in range(lines // SUBS):
        rows = pl.ds(h * SUBS, SUBS)
        agg = agg_ref[rows, :]
        high, lane = agg >> 7, agg & (LANES - 1)
        spread = [
            pick_lines([wide(line_ref[j, pl.ds(r, 1), :]) for r in range(4)], high, lane)
            for j in range(4)
        ]
        for i in range(4):
            placed = w_ref[i, 0, rows, :] * spread[0]
            for j in range(1, 4):
                placed = placed + w_ref[i, j, rows, :] * spread[j]
            x = x1_ref[i, rows, :] + placed
            xo_ref[i, rows, :] = x
            for twice in range(2):
                pad_ref[pl.ds((twice * 4 + i) * lines + h * SUBS, SUBS), :] = x
    out_ref[...] = outgoing(
        lambda r: pad_ref[pl.ds(r, SUBS, stride=lines), :], lines, s_ref[...]
    )


def coarse_tables(group, *refs):
    vo_ref, co_ref, mo_ref, pad_ref = refs[-4:]
    me = refs[0][0]
    for q in range(group):
        pad_ref[me ^ q] = refs[1][q]
    for h in range(group // SUBS):
        rows = pl.ds(h * SUBS, SUBS)
        for ki in range(NNZ * 4):
            k, i = ki // 4, ki % 4
            for j in range(4):
                tile = pad_ref[rows, ki * 4 + j, :]
                vo_ref[k, i, j, rows, :] = tile
                if k == 0 and i == j:
                    mo_ref[i, rows, :] = 1.0 / tile
        for k in range(NNZ):
            col = pad_ref[rows, NNZ * 16 + k, :].astype(I32)
            co_ref[k, rows, :] = ((col >> 7) ^ me) * LANES + (col & (LANES - 1))


def coarse_solve(group, *refs):
    (v_ref, c_ref, m_ref, x2_ref, w_ref, agg_ref, s_ref, xo_ref, out_ref, b_ref, x_ref, d_ref, pad_ref) = refs[-13:]
    for piece, places in zip(refs[:-13], span_places(group)):
        for t, place in enumerate(places):
            for j in range(4):
                b_ref[j, pl.ds(place, 1), :] = piece[t, pl.ds(j, 1), :]
    blocks = group // SUBS
    for j in range(4):
        first = m_ref[j] * b_ref[j]
        x_ref[j] = first
        d_ref[j] = first
    for keep, gain in cheb_factors(KC)[1:]:
        resid = []
        for h in range(blocks):
            rows = pl.ds(h * SUBS, SUBS)
            acc = [b_ref[i, rows, :] for i in range(4)]
            for k in range(NNZ):
                col = c_ref[k, rows, :]
                high, lane = col >> 7, col & (LANES - 1)
                for j in range(4):
                    if k:
                        got = pick_lines(
                            [wide(x_ref[j, pl.ds(r, 1), :]) for r in range(group)], high, lane
                        )
                    else:
                        got = x_ref[j, rows, :]
                    for i in range(4):
                        acc[i] = acc[i] - v_ref[k, i, j, rows, :] * got
            resid.append(acc)
        for h in range(blocks):
            rows = pl.ds(h * SUBS, SUBS)
            for i in range(4):
                d = keep * d_ref[i, rows, :] + gain * (m_ref[i, rows, :] * resid[h][i])
                d_ref[i, rows, :] = d
                x_ref[i, rows, :] = x_ref[i, rows, :] + d
    lane = agg_ref[...]
    spread = [pick(wide(x_ref[j, pl.ds(0, 1), :]), lane) for j in range(4)]
    for i in range(4):
        x = x2_ref[i]
        for j in range(4):
            x = x + w_ref[i, j] * spread[j]
        xo_ref[i] = x
        middle_pad(pad_ref, i, x)
    middle_out(out_ref, pad_ref, s_ref)


def call(body, outs, args, scratch=(), free=(), smem=()):
    specs = []
    for index in range(len(args)):
        if index in free:
            specs.append(pl.BlockSpec(memory_space=pl.ANY))
        elif index in smem:
            specs.append(pl.BlockSpec(memory_space=pltpu.SMEM))
        else:
            specs.append(pl.BlockSpec(memory_space=pltpu.VMEM))
    single = not isinstance(outs, (list, tuple))
    shapes = [outs] if single else list(outs)
    result = pl.pallas_call(
        body,
        out_shape=shapes,
        in_specs=specs,
        out_specs=[pl.BlockSpec(memory_space=pltpu.VMEM) for _ in shapes],
        scratch_shapes=list(scratch),
        compiler_params=pltpu.CompilerParams(vmem_limit_bytes=16 * 2**20),
    )(*args)
    return result[0] if single else result


def shape(*dims, dtype=F32):
    return jax.ShapeDtypeStruct(dims, dtype)


def vmem(*dims, dtype=F32):
    return pltpu.VMEM(dims, dtype)


def native_rows(x):
    lines = x.shape[-1] // LANES
    split = x.reshape(x.shape[:-1] + (lines, LANES))
    return jnp.swapaxes(split, -2, -3).reshape(-1, LANES)


def from_native(rows, lines):
    return jnp.swapaxes(rows.reshape(lines, 4, LANES), 0, 1).reshape(4, lines * LANES)


def exchange(mesh, out, which):
    slabs, count = mesh.shape["stream"], mesh.shape["span"]

    def swap(partner):
        pairs = []
        for a in range(slabs):
            for b in range(count):
                to_a, to_b = partner(a, b)
                pairs.append((a * count + b, to_a * count + to_b))
        return lax.ppermute(out, AXES, pairs)

    def odd(index):
        return index + 1 if index % 2 else index - 1

    def span_odd(a, b):
        return (a, odd(b)) if 0 <= odd(b) < count else (a ^ 1, b)

    return [
        swap(lambda a, b: (odd(a) % slabs, b)),
        swap(span_odd),
        swap(lambda a, b: (a ^ 1, b)),
        swap(lambda a, b: (a, b ^ 1)),
        which,
    ]


def halo_choice(a, b, count):
    row, lane = (lax.broadcasted_iota(I32, (SUBS, LANES), d) for d in range(2))
    left = lane < LANES // 2
    index = jnp.where(row < 4, a, b)
    even = left == (index % 2 == 1)
    outside = (row >= 4) & jnp.where(left, b == 0, b == count - 1)
    return jnp.where(outside, 0, jnp.where(even, 1, 2)).astype(I32)


def span_places(group):
    places = [[0]]
    mask = group // 2
    while mask:
        places.append([mask ^ m for piece in places for m in piece])
        mask //= 2
    return places


def span_stage(mesh, pieces):
    slabs, count = mesh.shape["stream"], mesh.shape["span"]
    held = jnp.concatenate(pieces)
    mask = count // 2 // held.shape[0]
    pairs = [
        (a * count + b, a * count + (b ^ mask)) for a in range(slabs) for b in range(count)
    ]
    return pieces + [lax.ppermute(held, AXES, pairs)]


def per_device(mesh, right_side, fine_values, fine_columns, fine_sends, fine_order, fine_weights, middle_values, middle_columns, middle_sends, middle_order, middle_weights, coarsest_values, coarsest_columns):
    group = mesh.shape["span"]
    lines = right_side.shape[1] // LANES
    tile = shape(SUBS, LANES)
    vec1 = shape(4, lines, LANES)
    vec2 = shape(4, SUBS, LANES)
    edge = vmem(SUBS, LANES)
    pad1 = vmem(SUBS * lines, LANES)
    pad2 = vmem(SUBS * SUBS, LANES)
    factors = cheb_factors(KSM)
    me = lax.axis_index("span").astype(I32)
    choice = halo_choice(lax.axis_index("stream").astype(I32), me, group)
    values1 = native_rows(fine_values)
    values2 = native_rows(middle_values)

    b1, m1, x1, send1, out = call(
        fine_start,
        [vec1, vec1, vec1, shape(SUBS, LANES, dtype=I32), tile],
        [values1, native_rows(right_side), fine_sends],
        [pad1],
    )
    d1 = x1

    own3 = jnp.concatenate(
        [coarsest_values.reshape(NNZ * 16, LANES), coarsest_columns.astype(F32)], axis=0
    )
    v1, c1 = call(
        fine_prepare,
        [shape(NNZ, 4, 4, lines, LANES), shape(NNZ, lines, LANES, dtype=I32)],
        [values1, native_columns(fine_columns), out],
        free=(2,),
    )

    def fine_part(x):
        return call(fine_local, vec1, [x, b1, v1, c1], [vmem(4, lines, SUBS, LANES)])

    def fine_next(which, arrived, resid, x, d, after=()):
        args = arrived + [resid, v1, c1, m1, x, d, send1]
        last = which == KSM - 1
        result = call(
            lambda *refs: fine_step(
                factors[which], last, *(refs[: len(args)] + refs[len(args) + len(after) :])
            ),
            [vec1, tile] + ([] if last else [vec1]),
            args + list(after),
            [edge, pad1],
            free=range(len(args), len(args) + len(after)),
        )
        return result[0], (None if last else result[2]), result[1]

    arrived = exchange(mesh, out, choice)
    own3, _ = lax.optimization_barrier((own3, out))
    slab3 = lax.all_gather(own3, "span", axis=0)
    resid = fine_part(x1)
    x1, d1, out = fine_next(1, arrived, resid, x1, d1)

    arrived = exchange(mesh, out, choice)
    resid = fine_part(x1)
    w1, agg1, place1 = call(
        fine_tables,
        [shape(4, 4, lines, LANES), shape(lines, LANES, dtype=I32), shape(2, SUBS, LANES, dtype=I32)],
        [native_rows(fine_weights), fine_order, fine_order.reshape(lines, LANES), out],
        free=(3,),
    )
    x1, d1, out = fine_next(2, arrived, resid, x1, d1, [])

    arrived = exchange(mesh, out, choice)
    resid = fine_part(x1)
    send2, v2, c2, m2, w2, agg2, place2 = call(
        middle_tables,
        [
            shape(SUBS, LANES, dtype=I32),
            shape(NNZ // 2, 4, 4, SUBS, LANES),
            shape(NNZ // 2, SUBS, LANES, dtype=I32),
            vec2,
            shape(4, 4, SUBS, LANES),
            shape(SUBS, LANES, dtype=I32),
            shape(SUBS, LANES, dtype=I32),
        ],
        [values2, native_columns(middle_columns), native_rows(middle_weights), middle_order, middle_order.reshape(-1, LANES), middle_sends, out],
        free=(6,),
    )
    b2, x2, out = call(
        fine_restrict,
        [vec2, vec2, tile],
        arrived + [resid, v1, c1, w1, place1, m2, send2],
        [edge, vmem(4, lines, LANES), pad2],
    )
    d2 = x2

    def middle_next(which, arrived, x, d, after=()):
        args = arrived + [b2, m2, x, d, v2, c2, send2]
        last = which == KSM - 1
        result = call(
            lambda *refs: middle_step(
                factors[which], last, *(refs[: len(args)] + refs[len(args) + len(after) :])
            ),
            [vec2, tile] + ([] if last else [vec2]),
            args + list(after),
            [edge, pad2],
            free=range(len(args), len(args) + len(after)),
        )
        return result[0], (None if last else result[2]), result[1]

    arrived = exchange(mesh, out, choice)
    v3, c3, m3 = call(
        lambda *refs: coarse_tables(group, *refs),
        [shape(NNZ, 4, 4, group, LANES), shape(NNZ, group, LANES, dtype=I32), shape(4, group, LANES)],
        [me.reshape(1), slab3, out],
        [vmem(group, NNZ * 17, LANES)],
        free=(2,),
        smem=(0,),
    )
    x2, d2, out = middle_next(1, arrived, x2, d2, [m3])
    arrived = exchange(mesh, out, choice)
    x2, d2, out = middle_next(2, arrived, x2, d2)
    arrived = exchange(mesh, out, choice)
    rhs3 = call(
        middle_restrict,
        tile,
        arrived + [b2, x2, v2, c2, w2, place2],
        [edge, vmem(4, SUBS, LANES)],
    )
    pieces = [rhs3[None]]
    while sum(piece.shape[0] for piece in pieces) < group:
        pieces = span_stage(mesh, pieces)
    vec3 = vmem(4, group, LANES)
    x2, out = call(
        lambda *refs: coarse_solve(group, *refs),
        [vec2, tile],
        pieces + [v3, c3, m3, x2, w2, agg2, send2],
        [vec3, vec3, vec3, pad2],
    )
    arrived = exchange(mesh, out, choice)
    x2, d2, out = middle_next(0, arrived, x2, x2)
    arrived = exchange(mesh, out, choice)
    x2, d2, out = middle_next(1, arrived, x2, d2)
    arrived = exchange(mesh, out, choice)
    x1, out = call(
        lambda *refs: middle_prolong(factors[2], *refs),
        [vec1, tile],
        arrived + [b2, m2, x2, d2, v2, c2, x1, w1, agg1, send1],
        [edge, vmem(4, SUBS, LANES), pad1],
    )
    d1 = x1
    for which in range(KSM):
        arrived = exchange(mesh, out, choice)
        resid = fine_part(x1)
        x1, d1, out = fine_next(which, arrived, resid, x1, d1)
    arrived = exchange(mesh, out, choice)
    resid = fine_part(x1)
    rows = shape(4 * lines, LANES)
    solved, left = call(fine_finish, [rows, rows], arrived + [resid, v1, c1, x1], [edge])
    return from_native(solved, lines), from_native(left, lines)


def native_columns(columns):
    lines = columns.shape[1] // LANES
    return jnp.swapaxes(columns.reshape(NNZ, lines, LANES), 0, 1).reshape(-1, LANES)


def solution(mesh):
    both = ("stream", "span")
    in_specs = (
        P(None, both),
        P(None, None, None, both),
        P(None, both),
        P(None, both),
        P(both, None),
        P(None, None, both),
        P(None, None, None, both),
        P(None, both),
        P(None, both),
        P(both, None),
        P(None, None, both),
        P(None, None, None, both),
        P(None, both),
    )
    return jax.shard_map(
        lambda *args: per_device(mesh, *args),
        mesh=mesh,
        in_specs=in_specs,
        out_specs=(P(None, both), P(None, both)),
        check_vma=False,
    )
```

```python
import jax
import jax.numpy as jnp
from jax import lax
from jax.experimental import pallas as pl
from jax.experimental.pallas import tpu as pltpu
from jax.sharding import PartitionSpec as P

KSM = 3
KC = 4
NNZ = 8
LANES = 128
SUBS = 8

CHEB_CENTRE = 1.0
CHEB_RADIUS = 0.9
AXES = ("stream", "span")
F32 = jnp.float32
I32 = jnp.int32


def cheb_factors(degree):
    sigma = CHEB_CENTRE / CHEB_RADIUS
    rho = 1.0 / sigma
    factors = [(0.0, 1.0 / CHEB_CENTRE)]
    for _ in range(degree - 1):
        rho_next = 1.0 / (2.0 * sigma - rho)
        factors.append((rho_next * rho, 2.0 * rho_next / CHEB_RADIUS))
        rho = rho_next
    return factors


def tile_iota(dim):
    return lax.broadcasted_iota(I32, (SUBS, LANES), dim)


def pick(line, lane):
    return jnp.take_along_axis(line, lane, axis=1, mode="promise_in_bounds")


def wide(line):
    return jnp.broadcast_to(line, (SUBS, LANES))


def pick_lines(lines, high, lane, first=0):
    result = jnp.zeros((SUBS, LANES), F32)
    for r, line in enumerate(lines):
        result = jnp.where(high == first + r, pick(line, lane), result)
    return result


def halo_lines(arrivals, edge_ref):
    s_odd, p_odd, s_even, p_even, which = [r[...] for r in arrivals]
    upper = tile_iota(0) < 4
    even = jnp.where(upper, s_even, p_even)
    odd = jnp.where(upper, s_odd, p_odd)
    edge_ref[...] = jnp.where(which == 1, even, jnp.where(which == 2, odd, 0.0))


def outgoing(lines_of, count, sends):
    high, lane = sends >> 7, sends & (LANES - 1)
    return pick_lines([lines_of(r) for r in range(count)], high, lane)


def send_table(s_ref):
    stream = jnp.concatenate([s_ref[pl.ds(1, 1), :], s_ref[pl.ds(0, 1), :]], axis=1)
    span = jnp.concatenate([s_ref[pl.ds(3, 1), :], s_ref[pl.ds(2, 1), :]], axis=1)
    return jnp.where(tile_iota(0) < 4, stream, span)


def duplicate(x):
    return x + pltpu.roll(x, 4, 0)


def fine_start(*refs):
    sources = refs[:7]
    (bo_ref, mo_ref, x_ref, so_ref, s2o_ref, co_ref, o3_ref, out_ref, pad_ref) = refs[7:16]
    held, sems = refs[16:23], refs[23]
    copies = [
        pltpu.make_async_copy(source.at[pl.ds(0, there.shape[0]), :], there, sems.at[t])
        for t, (source, there) in enumerate(zip(sources, held))
    ]
    for copy in copies:
        copy.start()
    for copy in copies:
        copy.wait()
    v_ref, b_ref, s_ref, s2_ref, c_ref, v3_ref, c3_ref = held
    sends = send_table(s_ref)
    so_ref[...] = sends
    s2o_ref[...] = send_table(s2_ref)
    count = v3_ref.shape[0]
    o3_ref[0, pl.ds(0, count), :] = v3_ref[...]
    o3_ref[0, pl.ds(count, NNZ), :] = c3_ref[...].astype(F32)
    for k in range(NNZ):
        for h in range(co_ref.shape[1] // SUBS):
            co_ref[k, pl.ds(h * SUBS, SUBS), :] = c_ref[
                pl.ds(h * SUBS * NNZ + k, SUBS, stride=NNZ), :
            ]
    lines = bo_ref.shape[1]
    for i in range(4):
        for h in range(lines // SUBS):
            rows = pl.ds(h * SUBS, SUBS)
            native = pl.ds(h * SUBS * 4 + i, SUBS, stride=4)
            b = b_ref[native, :]
            m = 1.0 / v_ref[pl.ds((i * lines + h * SUBS) * 4 + i, SUBS, stride=4), :]
            x = m * b
            bo_ref[i, rows, :] = b
            mo_ref[i, rows, :] = m
            x_ref[i, rows, :] = x
            for twice in range(2):
                pad_ref[pl.ds((twice * 4 + i) * lines + h * SUBS, SUBS), :] = x
    out_ref[...] = outgoing(
        lambda r: pad_ref[pl.ds(r, SUBS, stride=lines), :], lines, sends
    )


def fine_prepare(v_ref, _, vo_ref):
    lines = vo_ref.shape[3]
    halves = lines // SUBS

    def body(ki, carry):
        k, i = ki // 4, ki % 4
        for j in range(4):
            for h in range(halves):
                start = ki * (lines * 4) + h * SUBS * 4 + j
                vo_ref[k, i, j, pl.ds(h * SUBS, SUBS), :] = v_ref[
                    pl.ds(start, SUBS, stride=4), :
                ]
        return carry

    lax.fori_loop(0, NNZ * 4, body, 0)


def fine_local(x_ref, b_ref, v_ref, c_ref, r_ref, line_ref):
    lines = x_ref.shape[1]
    halves = lines // SUBS
    for j in range(4):
        for r in range(lines):
            line_ref[j, r] = wide(x_ref[j, pl.ds(r, 1), :])
    acc = []
    for h in range(halves):
        rows = pl.ds(h * SUBS, SUBS)
        for i in range(4):
            total = b_ref[i, rows, :]
            for j in range(4):
                total = total - v_ref[0, i, j, rows, :] * x_ref[j, rows, :]
            acc.append(total)

    def body(k, acc):
        acc = list(acc)
        for h in range(halves):
            rows = pl.ds(h * SUBS, SUBS)
            col = c_ref[k, rows, :]
            high, lane = col >> 7, col & (LANES - 1)
            for j in range(4):
                got = pick_lines([line_ref[j, r] for r in range(lines)], high, lane)
                for i in range(4):
                    acc[4 * h + i] = acc[4 * h + i] - v_ref[k, i, j, rows, :] * got
        return tuple(acc)

    acc = lax.fori_loop(1, NNZ, body, tuple(acc))
    for h in range(halves):
        for i in range(4):
            r_ref[i, pl.ds(h * SUBS, SUBS), :] = acc[4 * h + i]


def fine_remote(arrivals, r_ref, v_ref, c_ref, edge_ref):
    lines = r_ref.shape[1]
    halves = lines // SUBS
    halo_lines(arrivals, edge_ref)
    edges = [[wide(edge_ref[pl.ds(4 * e + j, 1), :]) for e in range(2)] for j in range(4)]
    result = []
    for h in range(halves):
        rows = pl.ds(h * SUBS, SUBS)
        acc = [r_ref[i, rows, :] for i in range(4)]
        for k in range(1, NNZ):
            col = c_ref[k, rows, :]
            high, lane = col >> 7, col & (LANES - 1)
            for j in range(4):
                got = pick_lines(edges[j], high, lane, lines)
                for i in range(4):
                    acc[i] = acc[i] - v_ref[k, i, j, rows, :] * got
        result.append(acc)
    return result


def fine_step(factors, last, *refs):
    arrivals = refs[:5]
    r_ref, v_ref, c_ref, m_ref, x_ref, d_ref, s_ref, xo_ref, out_ref = refs[5:14]
    do_ref = refs[14] if last is False else None
    edge_ref, pad_ref = refs[-2:]
    keep, gain = factors
    lines = r_ref.shape[1]
    resid = fine_remote(arrivals, r_ref, v_ref, c_ref, edge_ref)
    for h in range(lines // SUBS):
        rows = pl.ds(h * SUBS, SUBS)
        for i in range(4):
            d = gain * (m_ref[i, rows, :] * resid[h][i])
            if keep:
                d = keep * d_ref[i, rows, :] + d
            x = x_ref[i, rows, :] + d
            if not last:
                do_ref[i, rows, :] = d
            xo_ref[i, rows, :] = x
            for twice in range(2):
                pad_ref[pl.ds((twice * 4 + i) * lines + h * SUBS, SUBS), :] = x
    out_ref[...] = outgoing(
        lambda r: pad_ref[pl.ds(r, SUBS, stride=lines), :], lines, s_ref[...]
    )


def fine_finish(*refs):
    arrivals = refs[:5]
    r_ref, v_ref, c_ref, x_ref, so_ref, ro_ref, edge_ref = refs[5:]
    lines = r_ref.shape[1]
    resid = fine_remote(arrivals, r_ref, v_ref, c_ref, edge_ref)
    for h in range(lines // SUBS):
        for i in range(4):
            native = pl.ds(h * SUBS * 4 + i, SUBS, stride=4)
            so_ref[native, :] = x_ref[i, pl.ds(h * SUBS, SUBS), :]
            ro_ref[native, :] = resid[h][i]


def fine_restrict(*refs):
    arrivals = refs[:5]
    (r_ref, v_ref, c_ref, w_ref, p_ref, m2_ref, s2_ref, b2_ref, x2_ref, out_ref, edge_ref, line_ref, pad_ref) = refs[5:]
    lines = r_ref.shape[1]
    resid = fine_remote(arrivals, r_ref, v_ref, c_ref, edge_ref)
    for h in range(lines // SUBS):
        rows = pl.ds(h * SUBS, SUBS)
        for j in range(4):
            total = w_ref[0, j, rows, :] * resid[h][0]
            for i in range(1, 4):
                total = total + w_ref[i, j, rows, :] * resid[h][i]
            line_ref[j, rows, :] = total
    for j in range(4):
        total = None
        source = [wide(line_ref[j, pl.ds(r, 1), :]) for r in range(lines)]
        for part in range(2):
            place = p_ref[part]
            got = pick_lines(source, place >> 7, place & (LANES - 1))
            total = got if total is None else total + got
        b2 = duplicate(total)
        x2 = m2_ref[j] * b2
        b2_ref[j] = b2
        x2_ref[j] = x2
        middle_pad(pad_ref, j, x2)
    middle_out(out_ref, pad_ref, s2_ref)


def inverse_order(o_row, lines):
    count = lines * LANES
    high, lane = o_row >> 7, o_row & (LANES - 1)
    coarse = lax.broadcasted_iota(I32, (1, count), 1) >> 2
    here = lax.broadcasted_iota(I32, (lines, count), 0) == high
    upper = jnp.where(here, (coarse >> 4).astype(F32), 0.0)
    lower = jnp.where(here, (coarse & 15).astype(F32), 0.0)
    left = jnp.concatenate([upper, lower], axis=0).astype(jnp.bfloat16)
    right = jnp.where(
        lax.broadcasted_iota(I32, (LANES, count), 0) == lane, 1.0, 0.0
    ).astype(jnp.bfloat16)
    found = lax.dot_general(
        left, right, (((1,), (1,)), ((), ())), preferred_element_type=F32
    )
    return (found[:lines] * 16.0 + found[lines:]).astype(I32)


def pick_order(sources, unit):
    lane = tile_iota(1)
    place = 4 * (lane & 31) + unit
    result = jnp.zeros((SUBS, LANES), I32)
    for q, source in enumerate(sources):
        result = jnp.where((lane >> 5) == q, pick(source, place), result)
    return result


def fine_tables(w_ref, o_ref, v2_ref, _, wo_ref, place_ref, m2_ref):
    lines = o_ref.shape[0]
    for i in range(4):
        for j in range(4):
            for h in range(lines // SUBS):
                start = (i * lines + h * SUBS) * 4 + j
                wo_ref[i, j, pl.ds(h * SUBS, SUBS), :] = w_ref[pl.ds(start, SUBS, stride=4), :]
    sources = []
    for q in range(4):
        four = o_ref[pl.ds(q, 4, stride=4), :]
        sources.append(jnp.concatenate([four, four], axis=0))
    for part in range(2):
        place_ref[part] = pick_order(sources, (tile_iota(0) >> 2) + 2 * part)
    for i in range(4):
        four = 1.0 / v2_ref[pl.ds(i * 16 + i, 4, stride=4), :]
        m2_ref[i, pl.ds(0, 4), :] = four
        m2_ref[i, pl.ds(4, 4), :] = four


def fine_inverse(row_ref, _, agg_ref):
    agg_ref[...] = inverse_order(row_ref[...], agg_ref.shape[0])


def middle_blocks(v_ref, c_ref, _, vo_ref, co_ref):
    def body(ki, carry):
        k, i = ki // 4, ki % 4
        for j in range(4):
            for odd in range(2):
                start = ((2 * k + odd) * 4 + i) * 16 + j
                vo_ref[k, i, j, pl.ds(4 * odd, 4), :] = v_ref[pl.ds(start, 4, stride=4), :]
        return carry

    lax.fori_loop(0, NNZ // 2 * 4, body, 0)
    for k in range(NNZ // 2):
        for odd in range(2):
            co_ref[k, pl.ds(4 * odd, 4), :] = c_ref[pl.ds(2 * k + odd, 4, stride=NNZ), :]


def middle_tables(w_ref, row_ref, o_ref, _, wo_ref, agg_ref, place_ref):
    lines = o_ref.shape[0]
    for i in range(4):
        for j in range(4):
            four = w_ref[pl.ds(i * lines * 4 + j, 4, stride=4), :]
            wo_ref[i, j, pl.ds(0, 4), :] = four
            wo_ref[i, j, pl.ds(4, 4), :] = four
    agg = inverse_order(row_ref[...], lines)
    agg_ref[...] = jnp.concatenate([agg, agg], axis=0)
    sources = [wide(o_ref[pl.ds(q, 1), :]) for q in range(4)]
    place_ref[...] = pick_order(sources, tile_iota(0) & 3)


def middle_pad(pad_ref, j, x):
    for twice in range(2):
        pad_ref[pl.ds((twice * 4 + j) * SUBS, SUBS), :] = x


def middle_out(out_ref, pad_ref, s_ref):
    out_ref[...] = outgoing(
        lambda r: pad_ref[pl.ds(r, SUBS, stride=SUBS), :], 4, s_ref[...]
    )


def middle_residual(arrivals, b_ref, x_ref, v_ref, c_ref, edge_ref):
    halo_lines(arrivals, edge_ref)
    acc = [jnp.zeros((SUBS, LANES), F32) for _ in range(4)]
    for j in range(4):
        source = [wide(x_ref[j, pl.ds(r, 1), :]) for r in range(4)]
        source += [wide(edge_ref[pl.ds(4 * e + j, 1), :]) for e in range(2)]
        for kp in range(NNZ // 2):
            col = c_ref[kp]
            got = pick_lines(source, col >> 7, col & (LANES - 1))
            for i in range(4):
                acc[i] = acc[i] + v_ref[kp, i, j] * got
    return [b_ref[i] - duplicate(acc[i]) for i in range(4)]


def middle_update(factors, resid, m_ref, x_ref, d_ref):
    keep, gain = factors
    xs, ds = [], []
    for i in range(4):
        d = gain * (m_ref[i] * resid[i])
        if keep:
            d = keep * d_ref[i] + d
        ds.append(d)
        xs.append(x_ref[i] + d)
    return xs, ds


def middle_step(factors, last, *refs):
    arrivals = refs[:5]
    b_ref, m_ref, x_ref, d_ref, v_ref, c_ref, s_ref, xo_ref, out_ref = refs[5:14]
    do_ref = refs[14] if last is False else None
    edge_ref, pad_ref = refs[-2:]
    resid = middle_residual(arrivals, b_ref, x_ref, v_ref, c_ref, edge_ref)
    xs, ds = middle_update(factors, resid, m_ref, x_ref, d_ref)
    for i in range(4):
        xo_ref[i] = xs[i]
        if not last:
            do_ref[i] = ds[i]
        middle_pad(pad_ref, i, xs[i])
    middle_out(out_ref, pad_ref, s_ref)


def middle_restrict(*refs):
    arrivals = refs[:5]
    b_ref, x_ref, v_ref, c_ref, w_ref, p_ref, out_ref, edge_ref, line_ref = refs[5:]
    resid = middle_residual(arrivals, b_ref, x_ref, v_ref, c_ref, edge_ref)
    place = p_ref[...]
    high, lane = place >> 7, place & (LANES - 1)
    for j in range(4):
        total = w_ref[0, j] * resid[0]
        for i in range(1, 4):
            total = total + w_ref[i, j] * resid[i]
        line_ref[j] = total
        source = [wide(line_ref[j, pl.ds(r, 1), :]) for r in range(4)]
        got = pick_lines(source, high, lane)
        got = got + pltpu.roll(got, 2, 0)
        got = got + pltpu.roll(got, 1, 0)
        out_ref[pl.ds(j, 1), :] = got[0:1]
        out_ref[pl.ds(4 + j, 1), :] = got[0:1]


def middle_prolong(factors, *refs):
    arrivals = refs[:5]
    (b_ref, m_ref, x_ref, d_ref, v_ref, c_ref, x1_ref, w_ref, agg_ref, s_ref, xo_ref, out_ref, edge_ref, line_ref, pad_ref) = refs[5:]
    lines = x1_ref.shape[1]
    resid = middle_residual(arrivals, b_ref, x_ref, v_ref, c_ref, edge_ref)
    xs, _ = middle_update(factors, resid, m_ref, x_ref, d_ref)
    for j in range(4):
        line_ref[j] = xs[j]
    for h in range(lines // SUBS):
        rows = pl.ds(h * SUBS, SUBS)
        agg = agg_ref[rows, :]
        high, lane = agg >> 7, agg & (LANES - 1)
        spread = [
            pick_lines([wide(line_ref[j, pl.ds(r, 1), :]) for r in range(4)], high, lane)
            for j in range(4)
        ]
        for i in range(4):
            placed = w_ref[i, 0, rows, :] * spread[0]
            for j in range(1, 4):
                placed = placed + w_ref[i, j, rows, :] * spread[j]
            x = x1_ref[i, rows, :] + placed
            xo_ref[i, rows, :] = x
            for twice in range(2):
                pad_ref[pl.ds((twice * 4 + i) * lines + h * SUBS, SUBS), :] = x
    out_ref[...] = outgoing(
        lambda r: pad_ref[pl.ds(r, SUBS, stride=lines), :], lines, s_ref[...]
    )


def coarse_tables(group, *refs):
    vo_ref, co_ref, mo_ref, pad_ref = refs[-4:]
    me = refs[0][0]
    for piece, places in zip(refs[1:-5], span_places(group)):
        for t, place in enumerate(places):
            pad_ref[place] = piece[t]
    for h in range(group // SUBS):
        rows = pl.ds(h * SUBS, SUBS)
        for ki in range(NNZ * 4):
            k, i = ki // 4, ki % 4
            for j in range(4):
                tile = pad_ref[rows, ki * 4 + j, :]
                vo_ref[k, i, j, rows, :] = tile
                if k == 0 and i == j:
                    mo_ref[i, rows, :] = 1.0 / tile
        for k in range(NNZ):
            col = pad_ref[rows, NNZ * 16 + k, :].astype(I32)
            co_ref[k, rows, :] = ((col >> 7) ^ me) * LANES + (col & (LANES - 1))


def coarse_solve(group, *refs):
    (v_ref, c_ref, m_ref, x2_ref, w_ref, agg_ref, s_ref, xo_ref, out_ref, b_ref, x_ref, d_ref, pad_ref) = refs[-13:]
    for odd, piece in enumerate(refs[:-13]):
        for t, place in enumerate(range(odd, group, 2)):
            for j in range(4):
                b_ref[j, pl.ds(place, 1), :] = piece[t, pl.ds(j, 1), :]
    blocks = group // SUBS
    for j in range(4):
        first = m_ref[j] * b_ref[j]
        x_ref[j] = first
        d_ref[j] = first
    for keep, gain in cheb_factors(KC)[1:]:
        resid = []
        for h in range(blocks):
            rows = pl.ds(h * SUBS, SUBS)
            acc = [b_ref[i, rows, :] for i in range(4)]
            for k in range(NNZ):
                col = c_ref[k, rows, :]
                high, lane = col >> 7, col & (LANES - 1)
                for j in range(4):
                    if k:
                        got = pick_lines(
                            [wide(x_ref[j, pl.ds(r, 1), :]) for r in range(group)], high, lane
                        )
                    else:
                        got = x_ref[j, rows, :]
                    for i in range(4):
                        acc[i] = acc[i] - v_ref[k, i, j, rows, :] * got
            resid.append(acc)
        for h in range(blocks):
            rows = pl.ds(h * SUBS, SUBS)
            for i in range(4):
                d = keep * d_ref[i, rows, :] + gain * (m_ref[i, rows, :] * resid[h][i])
                d_ref[i, rows, :] = d
                x_ref[i, rows, :] = x_ref[i, rows, :] + d
    lane = agg_ref[...]
    spread = [pick(wide(x_ref[j, pl.ds(0, 1), :]), lane) for j in range(4)]
    for i in range(4):
        x = x2_ref[i]
        for j in range(4):
            x = x + w_ref[i, j] * spread[j]
        xo_ref[i] = x
        middle_pad(pad_ref, i, x)
    middle_out(out_ref, pad_ref, s_ref)


def call(body, outs, args, scratch=(), free=(), smem=(), hbm=(), limit=16):
    specs = []
    for index in range(len(args)):
        if index in hbm:
            specs.append(pl.BlockSpec(memory_space=pltpu.HBM))
        elif index in free:
            specs.append(pl.BlockSpec(memory_space=pl.ANY))
        elif index in smem:
            specs.append(pl.BlockSpec(memory_space=pltpu.SMEM))
        else:
            specs.append(pl.BlockSpec(memory_space=pltpu.VMEM))
    single = not isinstance(outs, (list, tuple))
    shapes = [outs] if single else list(outs)
    result = pl.pallas_call(
        body,
        out_shape=shapes,
        in_specs=specs,
        out_specs=[pl.BlockSpec(memory_space=pltpu.VMEM) for _ in shapes],
        scratch_shapes=list(scratch),
        compiler_params=pltpu.CompilerParams(vmem_limit_bytes=limit * 2**20),
    )(*args)
    return result[0] if single else result


def shape(*dims, dtype=F32):
    return jax.ShapeDtypeStruct(dims, dtype)


def vmem(*dims, dtype=F32):
    return pltpu.VMEM(dims, dtype)


def native_rows(x):
    lines = x.shape[-1] // LANES
    split = x.reshape(x.shape[:-1] + (lines, LANES))
    return jnp.swapaxes(split, -2, -3).reshape(-1, LANES)


def from_native(rows, lines):
    return jnp.swapaxes(rows.reshape(lines, 4, LANES), 0, 1).reshape(4, lines * LANES)


def exchange(mesh, out, which):
    slabs, count = mesh.shape["stream"], mesh.shape["span"]

    def swap(partner):
        pairs = []
        for a in range(slabs):
            for b in range(count):
                to_a, to_b = partner(a, b)
                pairs.append((a * count + b, to_a * count + to_b))
        return lax.ppermute(out, AXES, pairs)

    def odd(index):
        return index + 1 if index % 2 else index - 1

    def span_odd(a, b):
        return (a, odd(b)) if 0 <= odd(b) < count else (a ^ 1, b)

    return [
        swap(lambda a, b: (odd(a) % slabs, b)),
        swap(span_odd),
        swap(lambda a, b: (a ^ 1, b)),
        swap(lambda a, b: (a, b ^ 1)),
        which,
    ]


def halo_choice(a, b, count):
    row, lane = (lax.broadcasted_iota(I32, (SUBS, LANES), d) for d in range(2))
    left = lane < LANES // 2
    index = jnp.where(row < 4, a, b)
    even = left == (index % 2 == 1)
    outside = (row >= 4) & jnp.where(left, b == 0, b == count - 1)
    return jnp.where(outside, 0, jnp.where(even, 1, 2)).astype(I32)


def span_places(group):
    places = [[0]]
    mask = group // 2
    while mask:
        places.append([mask ^ m for piece in places for m in piece])
        mask //= 2
    return places


def span_swap(mesh, value, mask):
    slabs, count = mesh.shape["stream"], mesh.shape["span"]
    pairs = [
        (a * count + b, a * count + (b ^ mask)) for a in range(slabs) for b in range(count)
    ]
    return lax.ppermute(value, AXES, pairs)


def span_stage(mesh, pieces, out):
    pieces, _ = lax.optimization_barrier((pieces, out))
    held = jnp.concatenate(pieces)
    return pieces + [span_swap(mesh, held, mesh.shape["span"] // 2 // held.shape[0])]


def span_gather(mesh, value):
    even = jnp.stack([value] + [span_swap(mesh, value, m) for m in range(2, mesh.shape["span"], 2)])
    return [even, span_swap(mesh, even, 1)]


def per_device(mesh, right_side, fine_values, fine_columns, fine_sends, fine_order, fine_weights, middle_values, middle_columns, middle_sends, middle_order, middle_weights, coarsest_values, coarsest_columns):
    group = mesh.shape["span"]
    lines = right_side.shape[1] // LANES
    tile = shape(SUBS, LANES)
    vec1 = shape(4, lines, LANES)
    vec2 = shape(4, SUBS, LANES)
    edge = vmem(SUBS, LANES)
    pad1 = vmem(SUBS * lines, LANES)
    pad2 = vmem(SUBS * SUBS, LANES)
    factors = cheb_factors(KSM)
    me = lax.axis_index("span").astype(I32)
    choice = halo_choice(lax.axis_index("stream").astype(I32), me, group)
    values1 = native_rows(fine_values)
    values2 = native_rows(middle_values)

    starts = [
        values1,
        native_rows(right_side),
        fine_sends,
        middle_sends,
        native_columns(fine_columns),
        coarsest_values.reshape(NNZ * 16, LANES),
        coarsest_columns,
    ]
    int_tile = shape(SUBS, LANES, dtype=I32)
    b1, m1, x1, send1, send2, c1, own3, out = call(
        fine_start,
        [
            vec1,
            vec1,
            vec1,
            int_tile,
            int_tile,
            shape(NNZ, lines, LANES, dtype=I32),
            shape(1, NNZ * 17, LANES),
            tile,
        ],
        [pltpu.with_memory_space_constraint(x, pltpu.HBM) for x in starts],
        [pad1, vmem(16 * lines, LANES)]
        + [vmem(*x.shape, dtype=x.dtype) for x in starts[1:]]
        + [pltpu.SemaphoreType.DMA((len(starts),))],
        hbm=range(len(starts)),
    )
    d1 = x1
    v1 = call(fine_prepare, shape(NNZ, 4, 4, lines, LANES), [values1, out], free=(1,))

    def fine_part(x):
        return call(fine_local, vec1, [x, b1, v1, c1], [vmem(4, lines, SUBS, LANES)])

    def fine_next(which, arrived, resid, x, d, after=()):
        args = arrived + [resid, v1, c1, m1, x, d, send1]
        last = which == KSM - 1
        result = call(
            lambda *refs: fine_step(
                factors[which], last, *(refs[: len(args)] + refs[len(args) + len(after) :])
            ),
            [vec1, tile] + ([] if last else [vec1]),
            args + list(after),
            [edge, pad1],
            free=range(len(args), len(args) + len(after)),
        )
        return result[0], (None if last else result[2]), result[1]

    arrived = exchange(mesh, out, choice)
    pieces3 = span_stage(mesh, [own3], out)
    resid = fine_part(x1)
    x1, d1, out = fine_next(1, arrived, resid, x1, d1)

    arrived = exchange(mesh, out, choice)
    resid = fine_part(x1)
    w1, place1, m2 = call(
        fine_tables,
        [
            shape(4, 4, lines, LANES),
            shape(2, SUBS, LANES, dtype=I32),
            vec2,
        ],
        [native_rows(fine_weights), fine_order.reshape(lines, LANES), values2, out],
        free=(3,),
    )
    x1, d1, out = fine_next(2, arrived, resid, x1, d1, [m2])

    arrived = exchange(mesh, out, choice)
    stages = len(span_places(group)) - 1
    for _ in range(stages - 2):
        pieces3 = span_stage(mesh, pieces3, out)
    resid = fine_part(x1)
    b2, x2, out = call(
        fine_restrict,
        [vec2, vec2, tile],
        arrived + [resid, v1, c1, w1, place1, m2, send2],
        [edge, vmem(4, lines, LANES), pad2],
    )
    d2 = x2

    def middle_next(which, arrived, x, d, after=()):
        args = arrived + [b2, m2, x, d, v2, c2, send2]
        last = which == KSM - 1
        result = call(
            lambda *refs: middle_step(
                factors[which], last, *(refs[: len(args)] + refs[len(args) + len(after) :])
            ),
            [vec2, tile] + ([] if last else [vec2]),
            args + list(after),
            [edge, pad2],
            free=range(len(args), len(args) + len(after)),
        )
        return result[0], (None if last else result[2]), result[1]

    arrived = exchange(mesh, out, choice)
    pieces3 = span_stage(mesh, pieces3, out)
    v2, c2 = call(
        middle_blocks,
        [shape(NNZ // 2, 4, 4, SUBS, LANES), shape(NNZ // 2, SUBS, LANES, dtype=I32)],
        [values2, native_columns(middle_columns), out],
        free=(2,),
    )
    x2, d2, out = middle_next(1, arrived, x2, d2)

    arrived = exchange(mesh, out, choice)
    w2, agg2, place2 = call(
        middle_tables,
        [
            shape(4, 4, SUBS, LANES),
            shape(SUBS, LANES, dtype=I32),
            shape(SUBS, LANES, dtype=I32),
        ],
        [native_rows(middle_weights), middle_order, middle_order.reshape(-1, LANES), out],
        free=(3,),
    )
    v3, c3, m3 = call(
        lambda *refs: coarse_tables(group, *refs),
        [shape(NNZ, 4, 4, group, LANES), shape(NNZ, group, LANES, dtype=I32), shape(4, group, LANES)],
        [me.reshape(1)] + pieces3 + [out],
        [vmem(group, NNZ * 17, LANES)],
        free=(1 + len(pieces3),),
        smem=(0,),
    )
    x2, d2, out = middle_next(2, arrived, x2, d2, [agg2, m3])

    arrived = exchange(mesh, out, choice)
    agg1 = call(fine_inverse, shape(lines, LANES, dtype=I32), [fine_order, out], free=(1,))
    rhs3 = call(
        lambda *refs: middle_restrict(*(refs[:11] + refs[12:])),
        tile,
        arrived + [b2, x2, v2, c2, w2, place2, agg1],
        [edge, vmem(4, SUBS, LANES)],
        free=(11,),
    )
    vec3 = vmem(4, group, LANES)
    x2, out = call(
        lambda *refs: coarse_solve(group, *refs),
        [vec2, tile],
        span_gather(mesh, rhs3) + [v3, c3, m3, x2, w2, agg2, send2],
        [vec3, vec3, vec3, pad2],
    )
    arrived = exchange(mesh, out, choice)
    x2, d2, out = middle_next(0, arrived, x2, x2)
    arrived = exchange(mesh, out, choice)
    x2, d2, out = middle_next(1, arrived, x2, d2)
    arrived = exchange(mesh, out, choice)
    x1, out = call(
        lambda *refs: middle_prolong(factors[2], *refs),
        [vec1, tile],
        arrived + [b2, m2, x2, d2, v2, c2, x1, w1, agg1, send1],
        [edge, vmem(4, SUBS, LANES), pad1],
    )
    d1 = x1
    for which in range(KSM):
        arrived = exchange(mesh, out, choice)
        resid = fine_part(x1)
        x1, d1, out = fine_next(which, arrived, resid, x1, d1)
    arrived = exchange(mesh, out, choice)
    resid = fine_part(x1)
    rows = shape(4 * lines, LANES)
    solved, left = call(fine_finish, [rows, rows], arrived + [resid, v1, c1, x1], [edge])
    return from_native(solved, lines), from_native(left, lines)


def native_columns(columns):
    lines = columns.shape[1] // LANES
    return jnp.swapaxes(columns.reshape(NNZ, lines, LANES), 0, 1).reshape(-1, LANES)


def solution(mesh):
    both = ("stream", "span")
    in_specs = (
        P(None, both),
        P(None, None, None, both),
        P(None, both),
        P(None, both),
        P(both, None),
        P(None, None, both),
        P(None, None, None, both),
        P(None, both),
        P(None, both),
        P(both, None),
        P(None, None, both),
        P(None, None, None, both),
        P(None, both),
    )
    return jax.shard_map(
        lambda *args: per_device(mesh, *args),
        mesh=mesh,
        in_specs=in_specs,
        out_specs=(P(None, both), P(None, both)),
        check_vma=False,
    )
```

```python
import jax
import jax.numpy as jnp
from jax import lax
from jax.experimental import pallas as pl
from jax.experimental.pallas import tpu as pltpu
from jax.sharding import PartitionSpec as P

KSM = 3
KC = 4
NNZ = 8
LANES = 128
SUBS = 8

CHEB_CENTRE = 1.0
CHEB_RADIUS = 0.9
AXES = ("stream", "span")
F32 = jnp.float32
I32 = jnp.int32


def cheb_factors(degree):
    sigma = CHEB_CENTRE / CHEB_RADIUS
    rho = 1.0 / sigma
    factors = [(0.0, 1.0 / CHEB_CENTRE)]
    for _ in range(degree - 1):
        rho_next = 1.0 / (2.0 * sigma - rho)
        factors.append((rho_next * rho, 2.0 * rho_next / CHEB_RADIUS))
        rho = rho_next
    return factors


def tile_iota(dim):
    return lax.broadcasted_iota(I32, (SUBS, LANES), dim)


def pick(line, lane):
    return jnp.take_along_axis(line, lane, axis=1, mode="promise_in_bounds")


def wide(line):
    return jnp.broadcast_to(line, (SUBS, LANES))


def pick_lines(lines, high, lane, first=0):
    result = jnp.zeros((SUBS, LANES), F32)
    for r, line in enumerate(lines):
        result = jnp.where(high == first + r, pick(line, lane), result)
    return result


def halo_lines(arrivals, edge_ref):
    s_odd, s_even, p_odd, p_even, which = [r[...] for r in arrivals]
    upper = tile_iota(0) < 4
    even = jnp.where(upper, s_even, p_even)
    odd = jnp.where(upper, s_odd, p_odd)
    edge_ref[...] = jnp.where(which == 1, even, jnp.where(which == 2, odd, 0.0))


def outgoing(lines_of, count, sends):
    high, lane = sends >> 7, sends & (LANES - 1)
    return pick_lines([lines_of(r) for r in range(count)], high, lane)


def send_table(s_ref):
    stream = jnp.concatenate([s_ref[pl.ds(1, 1), :], s_ref[pl.ds(0, 1), :]], axis=1)
    span = jnp.concatenate([s_ref[pl.ds(3, 1), :], s_ref[pl.ds(2, 1), :]], axis=1)
    return jnp.where(tile_iota(0) < 4, stream, span)


def duplicate(x):
    return x + pltpu.roll(x, 4, 0)


def fine_start(*refs):
    sources = refs[:7]
    (bo_ref, mo_ref, x_ref, so_ref, s2o_ref, co_ref, o3_ref, out_ref, pad_ref) = refs[7:16]
    held, sems = refs[16:23], refs[23]
    copies = [
        pltpu.make_async_copy(source.at[pl.ds(0, there.shape[0]), :], there, sems.at[t])
        for t, (source, there) in enumerate(zip(sources, held))
    ]
    for copy in copies:
        copy.start()
    for copy in copies:
        copy.wait()
    v_ref, b_ref, s_ref, s2_ref, c_ref, v3_ref, c3_ref = held
    sends = send_table(s_ref)
    so_ref[...] = sends
    s2o_ref[...] = send_table(s2_ref)
    count = v3_ref.shape[0]
    o3_ref[0, pl.ds(0, count), :] = v3_ref[...]
    o3_ref[0, pl.ds(count, NNZ), :] = c3_ref[...].astype(F32)
    for k in range(NNZ):
        for h in range(co_ref.shape[1] // SUBS):
            co_ref[k, pl.ds(h * SUBS, SUBS), :] = c_ref[
                pl.ds(h * SUBS * NNZ + k, SUBS, stride=NNZ), :
            ]
    lines = bo_ref.shape[1]
    for i in range(4):
        for h in range(lines // SUBS):
            rows = pl.ds(h * SUBS, SUBS)
            native = pl.ds(h * SUBS * 4 + i, SUBS, stride=4)
            b = b_ref[native, :]
            m = 1.0 / v_ref[pl.ds((i * lines + h * SUBS) * 4 + i, SUBS, stride=4), :]
            x = m * b
            bo_ref[i, rows, :] = b
            mo_ref[i, rows, :] = m
            x_ref[i, rows, :] = x
            for twice in range(2):
                pad_ref[pl.ds((twice * 4 + i) * lines + h * SUBS, SUBS), :] = x
    out_ref[...] = outgoing(
        lambda r: pad_ref[pl.ds(r, SUBS, stride=lines), :], lines, sends
    )


def fine_prepare(v_ref, _, vo_ref):
    lines = vo_ref.shape[3]
    halves = lines // SUBS

    def body(ki, carry):
        k, i = ki // 4, ki % 4
        for j in range(4):
            for h in range(halves):
                start = ki * (lines * 4) + h * SUBS * 4 + j
                vo_ref[k, i, j, pl.ds(h * SUBS, SUBS), :] = v_ref[
                    pl.ds(start, SUBS, stride=4), :
                ]
        return carry

    lax.fori_loop(0, NNZ * 4, body, 0)


def fine_local(x_ref, b_ref, v_ref, c_ref, r_ref, line_ref):
    lines = x_ref.shape[1]
    halves = lines // SUBS
    for j in range(4):
        for r in range(lines):
            line_ref[j, r] = wide(x_ref[j, pl.ds(r, 1), :])
    acc = []
    for h in range(halves):
        rows = pl.ds(h * SUBS, SUBS)
        for i in range(4):
            total = b_ref[i, rows, :]
            for j in range(4):
                total = total - v_ref[0, i, j, rows, :] * x_ref[j, rows, :]
            acc.append(total)

    def body(k, acc):
        acc = list(acc)
        for h in range(halves):
            rows = pl.ds(h * SUBS, SUBS)
            col = c_ref[k, rows, :]
            high, lane = col >> 7, col & (LANES - 1)
            for j in range(4):
                got = pick_lines([line_ref[j, r] for r in range(lines)], high, lane)
                for i in range(4):
                    acc[4 * h + i] = acc[4 * h + i] - v_ref[k, i, j, rows, :] * got
        return tuple(acc)

    acc = lax.fori_loop(1, NNZ, body, tuple(acc))
    for h in range(halves):
        for i in range(4):
            r_ref[i, pl.ds(h * SUBS, SUBS), :] = acc[4 * h + i]


def fine_remote(arrivals, r_ref, v_ref, c_ref, edge_ref):
    lines = r_ref.shape[1]
    halves = lines // SUBS
    halo_lines(arrivals, edge_ref)
    edges = [[wide(edge_ref[pl.ds(4 * e + j, 1), :]) for e in range(2)] for j in range(4)]
    result = []
    for h in range(halves):
        rows = pl.ds(h * SUBS, SUBS)
        acc = [r_ref[i, rows, :] for i in range(4)]
        for k in range(1, NNZ):
            col = c_ref[k, rows, :]
            high, lane = col >> 7, col & (LANES - 1)
            for j in range(4):
                got = pick_lines(edges[j], high, lane, lines)
                for i in range(4):
                    acc[i] = acc[i] - v_ref[k, i, j, rows, :] * got
        result.append(acc)
    return result


def fine_step(factors, last, *refs):
    arrivals = refs[:5]
    r_ref, v_ref, c_ref, m_ref, x_ref, d_ref, s_ref, xo_ref, out_ref = refs[5:14]
    do_ref = refs[14] if last is False else None
    edge_ref, pad_ref = refs[-2:]
    keep, gain = factors
    lines = r_ref.shape[1]
    resid = fine_remote(arrivals, r_ref, v_ref, c_ref, edge_ref)
    for h in range(lines // SUBS):
        rows = pl.ds(h * SUBS, SUBS)
        for i in range(4):
            d = gain * (m_ref[i, rows, :] * resid[h][i])
            if keep:
                d = keep * d_ref[i, rows, :] + d
            x = x_ref[i, rows, :] + d
            if not last:
                do_ref[i, rows, :] = d
            xo_ref[i, rows, :] = x
            for twice in range(2):
                pad_ref[pl.ds((twice * 4 + i) * lines + h * SUBS, SUBS), :] = x
    out_ref[...] = outgoing(
        lambda r: pad_ref[pl.ds(r, SUBS, stride=lines), :], lines, s_ref[...]
    )


def fine_finish(*refs):
    arrivals = refs[:5]
    r_ref, v_ref, c_ref, x_ref, so_ref, ro_ref, edge_ref = refs[5:]
    lines = r_ref.shape[1]
    resid = fine_remote(arrivals, r_ref, v_ref, c_ref, edge_ref)
    for h in range(lines // SUBS):
        for i in range(4):
            native = pl.ds(h * SUBS * 4 + i, SUBS, stride=4)
            so_ref[native, :] = x_ref[i, pl.ds(h * SUBS, SUBS), :]
            ro_ref[native, :] = resid[h][i]


def fine_restrict(*refs):
    arrivals = refs[:5]
    (r_ref, v_ref, c_ref, w_ref, p_ref, m2_ref, s2_ref, b2_ref, x2_ref, out_ref, edge_ref, line_ref, pad_ref) = refs[5:]
    lines = r_ref.shape[1]
    resid = fine_remote(arrivals, r_ref, v_ref, c_ref, edge_ref)
    for h in range(lines // SUBS):
        rows = pl.ds(h * SUBS, SUBS)
        for j in range(4):
            total = w_ref[0, j, rows, :] * resid[h][0]
            for i in range(1, 4):
                total = total + w_ref[i, j, rows, :] * resid[h][i]
            line_ref[j, rows, :] = total
    for j in range(4):
        total = None
        source = [wide(line_ref[j, pl.ds(r, 1), :]) for r in range(lines)]
        for part in range(2):
            place = p_ref[part]
            got = pick_lines(source, place >> 7, place & (LANES - 1))
            total = got if total is None else total + got
        b2 = duplicate(total)
        x2 = m2_ref[j] * b2
        b2_ref[j] = b2
        x2_ref[j] = x2
        middle_pad(pad_ref, j, x2)
    middle_out(out_ref, pad_ref, s2_ref)


def inverse_order(o_row, lines):
    count = lines * LANES
    high, lane = o_row >> 7, o_row & (LANES - 1)
    coarse = lax.broadcasted_iota(I32, (1, count), 1) >> 2
    here = lax.broadcasted_iota(I32, (lines, count), 0) == high
    upper = jnp.where(here, (coarse >> 4).astype(F32), 0.0)
    lower = jnp.where(here, (coarse & 15).astype(F32), 0.0)
    left = jnp.concatenate([upper, lower], axis=0).astype(jnp.bfloat16)
    right = jnp.where(
        lax.broadcasted_iota(I32, (LANES, count), 0) == lane, 1.0, 0.0
    ).astype(jnp.bfloat16)
    found = lax.dot_general(
        left, right, (((1,), (1,)), ((), ())), preferred_element_type=F32
    )
    return (found[:lines] * 16.0 + found[lines:]).astype(I32)


def pick_order(sources, unit):
    lane = tile_iota(1)
    place = 4 * (lane & 31) + unit
    result = jnp.zeros((SUBS, LANES), I32)
    for q, source in enumerate(sources):
        result = jnp.where((lane >> 5) == q, pick(source, place), result)
    return result


def fine_tables(w_ref, o_ref, v2_ref, _, wo_ref, place_ref, m2_ref):
    lines = o_ref.shape[0]
    for i in range(4):
        for j in range(4):
            for h in range(lines // SUBS):
                start = (i * lines + h * SUBS) * 4 + j
                wo_ref[i, j, pl.ds(h * SUBS, SUBS), :] = w_ref[pl.ds(start, SUBS, stride=4), :]
    sources = []
    for q in range(4):
        four = o_ref[pl.ds(q, 4, stride=4), :]
        sources.append(jnp.concatenate([four, four], axis=0))
    for part in range(2):
        place_ref[part] = pick_order(sources, (tile_iota(0) >> 2) + 2 * part)
    for i in range(4):
        four = 1.0 / v2_ref[pl.ds(i * 16 + i, 4, stride=4), :]
        m2_ref[i, pl.ds(0, 4), :] = four
        m2_ref[i, pl.ds(4, 4), :] = four


def fine_inverse(row_ref, _, agg_ref):
    agg_ref[...] = inverse_order(row_ref[...], agg_ref.shape[0])


def middle_blocks(v_ref, c_ref, _, vo_ref, co_ref):
    def body(ki, carry):
        k, i = ki // 4, ki % 4
        for j in range(4):
            for odd in range(2):
                start = ((2 * k + odd) * 4 + i) * 16 + j
                vo_ref[k, i, j, pl.ds(4 * odd, 4), :] = v_ref[pl.ds(start, 4, stride=4), :]
        return carry

    lax.fori_loop(0, NNZ // 2 * 4, body, 0)
    for k in range(NNZ // 2):
        for odd in range(2):
            co_ref[k, pl.ds(4 * odd, 4), :] = c_ref[pl.ds(2 * k + odd, 4, stride=NNZ), :]


def middle_tables(w_ref, row_ref, o_ref, _, wo_ref, agg_ref, place_ref):
    lines = o_ref.shape[0]
    for i in range(4):
        for j in range(4):
            four = w_ref[pl.ds(i * lines * 4 + j, 4, stride=4), :]
            wo_ref[i, j, pl.ds(0, 4), :] = four
            wo_ref[i, j, pl.ds(4, 4), :] = four
    agg = inverse_order(row_ref[...], lines)
    agg_ref[...] = jnp.concatenate([agg, agg], axis=0)
    sources = [wide(o_ref[pl.ds(q, 1), :]) for q in range(4)]
    place_ref[...] = pick_order(sources, tile_iota(0) & 3)


def middle_pad(pad_ref, j, x):
    for twice in range(2):
        pad_ref[pl.ds((twice * 4 + j) * SUBS, SUBS), :] = x


def middle_out(out_ref, pad_ref, s_ref):
    out_ref[...] = outgoing(
        lambda r: pad_ref[pl.ds(r, SUBS, stride=SUBS), :], 4, s_ref[...]
    )


def middle_residual(arrivals, b_ref, x_ref, v_ref, c_ref, edge_ref):
    halo_lines(arrivals, edge_ref)
    acc = [jnp.zeros((SUBS, LANES), F32) for _ in range(4)]
    for j in range(4):
        source = [wide(x_ref[j, pl.ds(r, 1), :]) for r in range(4)]
        source += [wide(edge_ref[pl.ds(4 * e + j, 1), :]) for e in range(2)]
        for kp in range(NNZ // 2):
            col = c_ref[kp]
            got = pick_lines(source, col >> 7, col & (LANES - 1))
            for i in range(4):
                acc[i] = acc[i] + v_ref[kp, i, j] * got
    return [b_ref[i] - duplicate(acc[i]) for i in range(4)]


def middle_update(factors, resid, m_ref, x_ref, d_ref):
    keep, gain = factors
    xs, ds = [], []
    for i in range(4):
        d = gain * (m_ref[i] * resid[i])
        if keep:
            d = keep * d_ref[i] + d
        ds.append(d)
        xs.append(x_ref[i] + d)
    return xs, ds


def middle_step(factors, last, *refs):
    arrivals = refs[:5]
    b_ref, m_ref, x_ref, d_ref, v_ref, c_ref, s_ref, xo_ref, out_ref = refs[5:14]
    do_ref = refs[14] if last is False else None
    edge_ref, pad_ref = refs[-2:]
    resid = middle_residual(arrivals, b_ref, x_ref, v_ref, c_ref, edge_ref)
    xs, ds = middle_update(factors, resid, m_ref, x_ref, d_ref)
    for i in range(4):
        xo_ref[i] = xs[i]
        if not last:
            do_ref[i] = ds[i]
        middle_pad(pad_ref, i, xs[i])
    middle_out(out_ref, pad_ref, s_ref)


def middle_restrict(*refs):
    arrivals = refs[:5]
    b_ref, x_ref, v_ref, c_ref, w_ref, p_ref, out_ref, edge_ref, line_ref = refs[5:]
    resid = middle_residual(arrivals, b_ref, x_ref, v_ref, c_ref, edge_ref)
    place = p_ref[...]
    high, lane = place >> 7, place & (LANES - 1)
    for j in range(4):
        total = w_ref[0, j] * resid[0]
        for i in range(1, 4):
            total = total + w_ref[i, j] * resid[i]
        line_ref[j] = total
        source = [wide(line_ref[j, pl.ds(r, 1), :]) for r in range(4)]
        got = pick_lines(source, high, lane)
        got = got + pltpu.roll(got, 2, 0)
        got = got + pltpu.roll(got, 1, 0)
        out_ref[pl.ds(j, 1), :] = got[0:1]
        out_ref[pl.ds(4 + j, 1), :] = got[0:1]


def middle_prolong(factors, *refs):
    arrivals = refs[:5]
    (b_ref, m_ref, x_ref, d_ref, v_ref, c_ref, x1_ref, w_ref, agg_ref, s_ref, xo_ref, out_ref, edge_ref, line_ref, pad_ref) = refs[5:]
    lines = x1_ref.shape[1]
    resid = middle_residual(arrivals, b_ref, x_ref, v_ref, c_ref, edge_ref)
    xs, _ = middle_update(factors, resid, m_ref, x_ref, d_ref)
    for j in range(4):
        line_ref[j] = xs[j]
    for h in range(lines // SUBS):
        rows = pl.ds(h * SUBS, SUBS)
        agg = agg_ref[rows, :]
        high, lane = agg >> 7, agg & (LANES - 1)
        spread = [
            pick_lines([wide(line_ref[j, pl.ds(r, 1), :]) for r in range(4)], high, lane)
            for j in range(4)
        ]
        for i in range(4):
            placed = w_ref[i, 0, rows, :] * spread[0]
            for j in range(1, 4):
                placed = placed + w_ref[i, j, rows, :] * spread[j]
            x = x1_ref[i, rows, :] + placed
            xo_ref[i, rows, :] = x
            for twice in range(2):
                pad_ref[pl.ds((twice * 4 + i) * lines + h * SUBS, SUBS), :] = x
    out_ref[...] = outgoing(
        lambda r: pad_ref[pl.ds(r, SUBS, stride=lines), :], lines, s_ref[...]
    )


def coarse_tables(group, *refs):
    vo_ref, co_ref, mo_ref, pad_ref = refs[-4:]
    me = refs[0][0]
    for piece, places in zip(refs[1:-5], span_places(group)):
        for t, place in enumerate(places):
            pad_ref[place] = piece[t]
    for h in range(group // SUBS):
        rows = pl.ds(h * SUBS, SUBS)
        for ki in range(NNZ * 4):
            k, i = ki // 4, ki % 4
            for j in range(4):
                tile = pad_ref[rows, ki * 4 + j, :]
                vo_ref[k, i, j, rows, :] = tile
                if k == 0 and i == j:
                    mo_ref[i, rows, :] = 1.0 / tile
        for k in range(NNZ):
            col = pad_ref[rows, NNZ * 16 + k, :].astype(I32)
            co_ref[k, rows, :] = ((col >> 7) ^ me) * LANES + (col & (LANES - 1))


def coarse_solve(group, *refs):
    (v_ref, c_ref, m_ref, x2_ref, w_ref, agg_ref, s_ref, xo_ref, out_ref, b_ref, x_ref, d_ref, pad_ref) = refs[-13:]
    first = [0] + list(range(group - 1, 1, -2))
    for swapped, piece in enumerate(refs[:-13]):
        for t, place in enumerate([m ^ swapped for m in first]):
            for j in range(4):
                b_ref[j, pl.ds(place, 1), :] = piece[t, pl.ds(j, 1), :]
    blocks = group // SUBS
    for j in range(4):
        first = m_ref[j] * b_ref[j]
        x_ref[j] = first
        d_ref[j] = first
    for keep, gain in cheb_factors(KC)[1:]:
        resid = []
        for h in range(blocks):
            rows = pl.ds(h * SUBS, SUBS)
            acc = [b_ref[i, rows, :] for i in range(4)]
            for k in range(NNZ):
                col = c_ref[k, rows, :]
                high, lane = col >> 7, col & (LANES - 1)
                for j in range(4):
                    if k:
                        got = pick_lines(
                            [wide(x_ref[j, pl.ds(r, 1), :]) for r in range(group)], high, lane
                        )
                    else:
                        got = x_ref[j, rows, :]
                    for i in range(4):
                        acc[i] = acc[i] - v_ref[k, i, j, rows, :] * got
            resid.append(acc)
        for h in range(blocks):
            rows = pl.ds(h * SUBS, SUBS)
            for i in range(4):
                d = keep * d_ref[i, rows, :] + gain * (m_ref[i, rows, :] * resid[h][i])
                d_ref[i, rows, :] = d
                x_ref[i, rows, :] = x_ref[i, rows, :] + d
    lane = agg_ref[...]
    spread = [pick(wide(x_ref[j, pl.ds(0, 1), :]), lane) for j in range(4)]
    for i in range(4):
        x = x2_ref[i]
        for j in range(4):
            x = x + w_ref[i, j] * spread[j]
        xo_ref[i] = x
        middle_pad(pad_ref, i, x)
    middle_out(out_ref, pad_ref, s_ref)


def call(body, outs, args, scratch=(), free=(), smem=(), hbm=(), limit=16):
    specs = []
    for index in range(len(args)):
        if index in hbm:
            specs.append(pl.BlockSpec(memory_space=pltpu.HBM))
        elif index in free:
            specs.append(pl.BlockSpec(memory_space=pl.ANY))
        elif index in smem:
            specs.append(pl.BlockSpec(memory_space=pltpu.SMEM))
        else:
            specs.append(pl.BlockSpec(memory_space=pltpu.VMEM))
    single = not isinstance(outs, (list, tuple))
    shapes = [outs] if single else list(outs)
    result = pl.pallas_call(
        body,
        out_shape=shapes,
        in_specs=specs,
        out_specs=[pl.BlockSpec(memory_space=pltpu.VMEM) for _ in shapes],
        scratch_shapes=list(scratch),
        compiler_params=pltpu.CompilerParams(vmem_limit_bytes=limit * 2**20),
    )(*args)
    return result[0] if single else result


def shape(*dims, dtype=F32):
    return jax.ShapeDtypeStruct(dims, dtype)


def vmem(*dims, dtype=F32):
    return pltpu.VMEM(dims, dtype)


def native_rows(x):
    lines = x.shape[-1] // LANES
    split = x.reshape(x.shape[:-1] + (lines, LANES))
    return jnp.swapaxes(split, -2, -3).reshape(-1, LANES)


def from_native(rows, lines):
    return jnp.swapaxes(rows.reshape(lines, 4, LANES), 0, 1).reshape(4, lines * LANES)


def exchange(mesh, out, which):
    slabs, count = mesh.shape["stream"], mesh.shape["span"]

    def swap(partner):
        pairs = []
        for a in range(slabs):
            for b in range(count):
                to_a, to_b = partner(a, b)
                pairs.append((a * count + b, to_a * count + to_b))
        return lax.ppermute(out, AXES, pairs)

    def odd(index):
        return index + 1 if index % 2 else index - 1

    def span_odd(a, b):
        return (a, odd(b)) if 0 <= odd(b) < count else (a ^ 1, b)

    partners = [
        lambda a, b: (odd(a) % slabs, b),
        lambda a, b: (a ^ 1, b),
        span_odd,
        lambda a, b: (a, b ^ 1),
    ]
    return [swap(partner) for partner in partners] + [which]


def halo_choice(a, b, count):
    row, lane = (lax.broadcasted_iota(I32, (SUBS, LANES), d) for d in range(2))
    left = lane < LANES // 2
    index = jnp.where(row < 4, a, b)
    even = left == (index % 2 == 1)
    outside = (row >= 4) & jnp.where(left, b == 0, b == count - 1)
    return jnp.where(outside, 0, jnp.where(even, 1, 2)).astype(I32)


def span_places(group):
    places = [[0]]
    mask = group // 2
    while mask:
        places.append([mask ^ m for piece in places for m in piece])
        mask //= 2
    return places


def span_swap(mesh, value, mask):
    slabs, count = mesh.shape["stream"], mesh.shape["span"]
    pairs = [
        (a * count + b, a * count + (b ^ mask)) for a in range(slabs) for b in range(count)
    ]
    return lax.ppermute(value, AXES, pairs)


def span_stage(mesh, pieces, out):
    pieces, _ = lax.optimization_barrier((pieces, out))
    held = jnp.concatenate(pieces)
    return pieces + [span_swap(mesh, held, mesh.shape["span"] // 2 // held.shape[0])]


def span_gather(mesh, value):
    masks = range(mesh.shape["span"] - 1, 1, -2)
    held = jnp.stack([value] + [span_swap(mesh, value, m) for m in masks])
    return [held, span_swap(mesh, held, 1)]


def per_device(mesh, right_side, fine_values, fine_columns, fine_sends, fine_order, fine_weights, middle_values, middle_columns, middle_sends, middle_order, middle_weights, coarsest_values, coarsest_columns):
    group = mesh.shape["span"]
    lines = right_side.shape[1] // LANES
    tile = shape(SUBS, LANES)
    vec1 = shape(4, lines, LANES)
    vec2 = shape(4, SUBS, LANES)
    edge = vmem(SUBS, LANES)
    pad1 = vmem(SUBS * lines, LANES)
    pad2 = vmem(SUBS * SUBS, LANES)
    factors = cheb_factors(KSM)
    me = lax.axis_index("span").astype(I32)
    choice = halo_choice(lax.axis_index("stream").astype(I32), me, group)
    values1 = native_rows(fine_values)
    values2 = native_rows(middle_values)

    starts = [
        values1,
        native_rows(right_side),
        fine_sends,
        middle_sends,
        native_columns(fine_columns),
        coarsest_values.reshape(NNZ * 16, LANES),
        coarsest_columns,
    ]
    int_tile = shape(SUBS, LANES, dtype=I32)
    b1, m1, x1, send1, send2, c1, own3, out = call(
        fine_start,
        [
            vec1,
            vec1,
            vec1,
            int_tile,
            int_tile,
            shape(NNZ, lines, LANES, dtype=I32),
            shape(1, NNZ * 17, LANES),
            tile,
        ],
        [pltpu.with_memory_space_constraint(x, pltpu.HBM) for x in starts],
        [pad1, vmem(16 * lines, LANES)]
        + [vmem(*x.shape, dtype=x.dtype) for x in starts[1:]]
        + [pltpu.SemaphoreType.DMA((len(starts),))],
        hbm=range(len(starts)),
    )
    d1 = x1
    v1 = call(fine_prepare, shape(NNZ, 4, 4, lines, LANES), [values1, out], free=(1,))

    def fine_part(x):
        return call(fine_local, vec1, [x, b1, v1, c1], [vmem(4, lines, SUBS, LANES)])

    def fine_next(which, arrived, resid, x, d, after=()):
        args = arrived + [resid, v1, c1, m1, x, d, send1]
        last = which == KSM - 1
        result = call(
            lambda *refs: fine_step(
                factors[which], last, *(refs[: len(args)] + refs[len(args) + len(after) :])
            ),
            [vec1, tile] + ([] if last else [vec1]),
            args + list(after),
            [edge, pad1],
            free=range(len(args), len(args) + len(after)),
        )
        return result[0], (None if last else result[2]), result[1]

    arrived = exchange(mesh, out, choice)
    pieces3 = span_stage(mesh, [own3], out)
    resid = fine_part(x1)
    x1, d1, out = fine_next(1, arrived, resid, x1, d1)

    arrived = exchange(mesh, out, choice)
    resid = fine_part(x1)
    w1, place1, m2 = call(
        fine_tables,
        [
            shape(4, 4, lines, LANES),
            shape(2, SUBS, LANES, dtype=I32),
            vec2,
        ],
        [native_rows(fine_weights), fine_order.reshape(lines, LANES), values2, out],
        free=(3,),
    )
    x1, d1, out = fine_next(2, arrived, resid, x1, d1, [m2])

    arrived = exchange(mesh, out, choice)
    stages = len(span_places(group)) - 1
    for _ in range(stages - 2):
        pieces3 = span_stage(mesh, pieces3, out)
    resid = fine_part(x1)
    b2, x2, out = call(
        lambda *refs: fine_restrict(*(refs[2:4] + refs[:2] + refs[4:])),
        [vec2, vec2, tile],
        arrived[2:4] + arrived[:2] + arrived[4:] + [resid, v1, c1, w1, place1, m2, send2],
        [edge, vmem(4, lines, LANES), pad2],
    )
    d2 = x2

    def middle_next(which, arrived, x, d, after=()):
        args = arrived + [b2, m2, x, d, v2, c2, send2]
        last = which == KSM - 1
        result = call(
            lambda *refs: middle_step(
                factors[which], last, *(refs[: len(args)] + refs[len(args) + len(after) :])
            ),
            [vec2, tile] + ([] if last else [vec2]),
            args + list(after),
            [edge, pad2],
            free=range(len(args), len(args) + len(after)),
        )
        return result[0], (None if last else result[2]), result[1]

    arrived = exchange(mesh, out, choice)
    pieces3 = span_stage(mesh, pieces3, out)
    v2, c2 = call(
        middle_blocks,
        [shape(NNZ // 2, 4, 4, SUBS, LANES), shape(NNZ // 2, SUBS, LANES, dtype=I32)],
        [values2, native_columns(middle_columns), out],
        free=(2,),
    )
    x2, d2, out = middle_next(1, arrived, x2, d2)

    arrived = exchange(mesh, out, choice)
    w2, agg2, place2 = call(
        middle_tables,
        [
            shape(4, 4, SUBS, LANES),
            shape(SUBS, LANES, dtype=I32),
            shape(SUBS, LANES, dtype=I32),
        ],
        [native_rows(middle_weights), middle_order, middle_order.reshape(-1, LANES), out],
        free=(3,),
    )
    v3, c3, m3 = call(
        lambda *refs: coarse_tables(group, *refs),
        [shape(NNZ, 4, 4, group, LANES), shape(NNZ, group, LANES, dtype=I32), shape(4, group, LANES)],
        [me.reshape(1)] + pieces3 + [out],
        [vmem(group, NNZ * 17, LANES)],
        free=(1 + len(pieces3),),
        smem=(0,),
    )
    x2, d2, out = middle_next(2, arrived, x2, d2, [agg2, m3])

    arrived = exchange(mesh, out, choice)
    agg1 = call(fine_inverse, shape(lines, LANES, dtype=I32), [fine_order, out], free=(1,))
    rhs3 = call(
        lambda *refs: middle_restrict(*(refs[:11] + refs[12:])),
        tile,
        arrived + [b2, x2, v2, c2, w2, place2, agg1],
        [edge, vmem(4, SUBS, LANES)],
        free=(11,),
    )
    vec3 = vmem(4, group, LANES)
    x2, out = call(
        lambda *refs: coarse_solve(group, *refs),
        [vec2, tile],
        span_gather(mesh, rhs3) + [v3, c3, m3, x2, w2, agg2, send2],
        [vec3, vec3, vec3, pad2],
    )
    arrived = exchange(mesh, out, choice)
    x2, d2, out = middle_next(0, arrived, x2, x2)
    arrived = exchange(mesh, out, choice)
    x2, d2, out = middle_next(1, arrived, x2, d2)
    arrived = exchange(mesh, out, choice)
    x1, out = call(
        lambda *refs: middle_prolong(factors[2], *refs),
        [vec1, tile],
        arrived + [b2, m2, x2, d2, v2, c2, x1, w1, agg1, send1],
        [edge, vmem(4, SUBS, LANES), pad1],
    )
    d1 = x1
    for which in range(KSM):
        arrived = exchange(mesh, out, choice)
        resid = fine_part(x1)
        x1, d1, out = fine_next(which, arrived, resid, x1, d1)
    arrived = exchange(mesh, out, choice)
    resid = fine_part(x1)
    rows = shape(4 * lines, LANES)
    solved, left = call(fine_finish, [rows, rows], arrived + [resid, v1, c1, x1], [edge])
    return from_native(solved, lines), from_native(left, lines)


def native_columns(columns):
    lines = columns.shape[1] // LANES
    return jnp.swapaxes(columns.reshape(NNZ, lines, LANES), 0, 1).reshape(-1, LANES)


def solution(mesh):
    both = ("stream", "span")
    in_specs = (
        P(None, both),
        P(None, None, None, both),
        P(None, both),
        P(None, both),
        P(both, None),
        P(None, None, both),
        P(None, None, None, both),
        P(None, both),
        P(None, both),
        P(both, None),
        P(None, None, both),
        P(None, None, None, both),
        P(None, both),
    )
    return jax.shard_map(
        lambda *args: per_device(mesh, *args),
        mesh=mesh,
        in_specs=in_specs,
        out_specs=(P(None, both), P(None, both)),
        check_vma=False,
    )
```

```python
import jax
import jax.numpy as jnp
from jax import lax
from jax.experimental import pallas as pl
from jax.experimental.pallas import tpu as pltpu
from jax.sharding import PartitionSpec as P

KSM = 3
KC = 4
NNZ = 8
LANES = 128
SUBS = 8

CHEB_CENTRE = 1.0
CHEB_RADIUS = 0.9
AXES = ("stream", "span")
F32 = jnp.float32
I32 = jnp.int32


def cheb_factors(degree):
    sigma = CHEB_CENTRE / CHEB_RADIUS
    rho = 1.0 / sigma
    factors = [(0.0, 1.0 / CHEB_CENTRE)]
    for _ in range(degree - 1):
        rho_next = 1.0 / (2.0 * sigma - rho)
        factors.append((rho_next * rho, 2.0 * rho_next / CHEB_RADIUS))
        rho = rho_next
    return factors


def tile_iota(dim):
    return lax.broadcasted_iota(I32, (SUBS, LANES), dim)


def pick(line, lane):
    return jnp.take_along_axis(line, lane, axis=1, mode="promise_in_bounds")


def wide(line):
    return jnp.broadcast_to(line, (SUBS, LANES))


def pick_lines(lines, high, lane, first=0):
    result = jnp.zeros((SUBS, LANES), F32)
    for r, line in enumerate(lines):
        result = jnp.where(high == first + r, pick(line, lane), result)
    return result


def halo_lines(arrivals, edge_ref):
    s_odd, s_even, p_odd, p_even, which = [r[...] for r in arrivals]
    upper = tile_iota(0) < 4
    even = jnp.where(upper, s_even, p_even)
    odd = jnp.where(upper, s_odd, p_odd)
    edge_ref[...] = jnp.where(which == 1, even, jnp.where(which == 2, odd, 0.0))


def outgoing(lines_of, count, sends):
    high, lane = sends >> 7, sends & (LANES - 1)
    return pick_lines([lines_of(r) for r in range(count)], high, lane)


def send_table(s_ref):
    stream = jnp.concatenate([s_ref[pl.ds(1, 1), :], s_ref[pl.ds(0, 1), :]], axis=1)
    span = jnp.concatenate([s_ref[pl.ds(3, 1), :], s_ref[pl.ds(2, 1), :]], axis=1)
    return jnp.where(tile_iota(0) < 4, stream, span)


def duplicate(x):
    return x + pltpu.roll(x, 4, 0)


def fine_start(*refs):
    sources = refs[:7]
    (bo_ref, mo_ref, x_ref, so_ref, s2o_ref, co_ref, o3_ref, out_ref, pad_ref) = refs[7:16]
    held, sems = refs[16:23], refs[23]
    copies = [
        pltpu.make_async_copy(source.at[pl.ds(0, there.shape[0]), :], there, sems.at[t])
        for t, (source, there) in enumerate(zip(sources, held))
    ]
    for copy in copies:
        copy.start()
    for copy in copies:
        copy.wait()
    v_ref, b_ref, s_ref, s2_ref, c_ref, v3_ref, c3_ref = held
    sends = send_table(s_ref)
    so_ref[...] = sends
    s2o_ref[...] = send_table(s2_ref)
    count = v3_ref.shape[0]
    o3_ref[0, pl.ds(0, count), :] = v3_ref[...]
    o3_ref[0, pl.ds(count, NNZ), :] = c3_ref[...].astype(F32)
    for k in range(NNZ):
        for h in range(co_ref.shape[1] // SUBS):
            co_ref[k, pl.ds(h * SUBS, SUBS), :] = c_ref[
                pl.ds(h * SUBS * NNZ + k, SUBS, stride=NNZ), :
            ]
    lines = bo_ref.shape[1]
    for i in range(4):
        for h in range(lines // SUBS):
            rows = pl.ds(h * SUBS, SUBS)
            native = pl.ds(h * SUBS * 4 + i, SUBS, stride=4)
            b = b_ref[native, :]
            m = 1.0 / v_ref[pl.ds((i * lines + h * SUBS) * 4 + i, SUBS, stride=4), :]
            x = m * b
            bo_ref[i, rows, :] = b
            mo_ref[i, rows, :] = m
            x_ref[i, rows, :] = x
            for twice in range(2):
                pad_ref[pl.ds((twice * 4 + i) * lines + h * SUBS, SUBS), :] = x
    out_ref[...] = outgoing(
        lambda r: pad_ref[pl.ds(r, SUBS, stride=lines), :], lines, sends
    )


def fine_prepare(v_ref, _, vo_ref):
    lines = vo_ref.shape[3]
    halves = lines // SUBS

    def body(ki, carry):
        k, i = ki // 4, ki % 4
        for j in range(4):
            for h in range(halves):
                start = ki * (lines * 4) + h * SUBS * 4 + j
                vo_ref[k, i, j, pl.ds(h * SUBS, SUBS), :] = v_ref[
                    pl.ds(start, SUBS, stride=4), :
                ]
        return carry

    lax.fori_loop(0, NNZ * 4, body, 0)


def fine_local(x_ref, b_ref, v_ref, c_ref, r_ref, line_ref):
    lines = x_ref.shape[1]
    halves = lines // SUBS
    for j in range(4):
        for r in range(lines):
            line_ref[j, r] = wide(x_ref[j, pl.ds(r, 1), :])
    acc = []
    for h in range(halves):
        rows = pl.ds(h * SUBS, SUBS)
        for i in range(4):
            total = b_ref[i, rows, :]
            for j in range(4):
                total = total - v_ref[0, i, j, rows, :] * x_ref[j, rows, :]
            acc.append(total)

    def body(k, acc):
        acc = list(acc)
        for h in range(halves):
            rows = pl.ds(h * SUBS, SUBS)
            col = c_ref[k, rows, :]
            high, lane = col >> 7, col & (LANES - 1)
            for j in range(4):
                got = pick_lines([line_ref[j, r] for r in range(lines)], high, lane)
                for i in range(4):
                    acc[4 * h + i] = acc[4 * h + i] - v_ref[k, i, j, rows, :] * got
        return tuple(acc)

    acc = lax.fori_loop(1, NNZ, body, tuple(acc))
    for h in range(halves):
        for i in range(4):
            r_ref[i, pl.ds(h * SUBS, SUBS), :] = acc[4 * h + i]


def fine_remote(arrivals, r_ref, v_ref, c_ref, edge_ref):
    lines = r_ref.shape[1]
    halves = lines // SUBS
    halo_lines(arrivals, edge_ref)
    edges = [[wide(edge_ref[pl.ds(4 * e + j, 1), :]) for e in range(2)] for j in range(4)]
    result = []
    for h in range(halves):
        rows = pl.ds(h * SUBS, SUBS)
        acc = [r_ref[i, rows, :] for i in range(4)]
        for k in range(1, NNZ):
            col = c_ref[k, rows, :]
            high, lane = col >> 7, col & (LANES - 1)
            for j in range(4):
                got = pick_lines(edges[j], high, lane, lines)
                for i in range(4):
                    acc[i] = acc[i] - v_ref[k, i, j, rows, :] * got
        result.append(acc)
    return result


def fine_step(factors, last, *refs):
    arrivals = refs[:5]
    r_ref, v_ref, c_ref, m_ref, x_ref, d_ref, s_ref, xo_ref, out_ref = refs[5:14]
    do_ref = refs[14] if last is False else None
    edge_ref, pad_ref = refs[-2:]
    keep, gain = factors
    lines = r_ref.shape[1]
    resid = fine_remote(arrivals, r_ref, v_ref, c_ref, edge_ref)
    for h in range(lines // SUBS):
        rows = pl.ds(h * SUBS, SUBS)
        for i in range(4):
            d = gain * (m_ref[i, rows, :] * resid[h][i])
            if keep:
                d = keep * d_ref[i, rows, :] + d
            x = x_ref[i, rows, :] + d
            if not last:
                do_ref[i, rows, :] = d
            xo_ref[i, rows, :] = x
            for twice in range(2):
                pad_ref[pl.ds((twice * 4 + i) * lines + h * SUBS, SUBS), :] = x
    out_ref[...] = outgoing(
        lambda r: pad_ref[pl.ds(r, SUBS, stride=lines), :], lines, s_ref[...]
    )


def fine_finish(*refs):
    arrivals = refs[:5]
    r_ref, v_ref, c_ref, x_ref, so_ref, ro_ref, edge_ref = refs[5:]
    lines = r_ref.shape[1]
    resid = fine_remote(arrivals, r_ref, v_ref, c_ref, edge_ref)
    for h in range(lines // SUBS):
        for i in range(4):
            native = pl.ds(h * SUBS * 4 + i, SUBS, stride=4)
            so_ref[native, :] = x_ref[i, pl.ds(h * SUBS, SUBS), :]
            ro_ref[native, :] = resid[h][i]


def fine_restrict(*refs):
    arrivals = refs[:5]
    (r_ref, v_ref, c_ref, w_ref, p_ref, m2_ref, s2_ref, b2_ref, x2_ref, out_ref, edge_ref, line_ref, pad_ref) = refs[5:]
    lines = r_ref.shape[1]
    resid = fine_remote(arrivals, r_ref, v_ref, c_ref, edge_ref)
    for h in range(lines // SUBS):
        rows = pl.ds(h * SUBS, SUBS)
        for j in range(4):
            total = w_ref[0, j, rows, :] * resid[h][0]
            for i in range(1, 4):
                total = total + w_ref[i, j, rows, :] * resid[h][i]
            line_ref[j, rows, :] = total
    for j in range(4):
        total = None
        source = [wide(line_ref[j, pl.ds(r, 1), :]) for r in range(lines)]
        for part in range(2):
            place = p_ref[part]
            got = pick_lines(source, place >> 7, place & (LANES - 1))
            total = got if total is None else total + got
        b2 = duplicate(total)
        x2 = m2_ref[j] * b2
        b2_ref[j] = b2
        x2_ref[j] = x2
        middle_pad(pad_ref, j, x2)
    middle_out(out_ref, pad_ref, s2_ref)


def inverse_order(o_row, lines):
    count = lines * LANES
    high, lane = o_row >> 7, o_row & (LANES - 1)
    coarse = lax.broadcasted_iota(I32, (1, count), 1) >> 2
    here = lax.broadcasted_iota(I32, (lines, count), 0) == high
    upper = jnp.where(here, (coarse >> 4).astype(F32), 0.0)
    lower = jnp.where(here, (coarse & 15).astype(F32), 0.0)
    left = jnp.concatenate([upper, lower], axis=0).astype(jnp.bfloat16)
    right = jnp.where(
        lax.broadcasted_iota(I32, (LANES, count), 0) == lane, 1.0, 0.0
    ).astype(jnp.bfloat16)
    found = lax.dot_general(
        left, right, (((1,), (1,)), ((), ())), preferred_element_type=F32
    )
    return (found[:lines] * 16.0 + found[lines:]).astype(I32)


def pick_order(sources, unit):
    lane = tile_iota(1)
    place = 4 * (lane & 31) + unit
    result = jnp.zeros((SUBS, LANES), I32)
    for q, source in enumerate(sources):
        result = jnp.where((lane >> 5) == q, pick(source, place), result)
    return result


def fine_tables(w_ref, o_ref, v2_ref, _, wo_ref, place_ref, m2_ref):
    lines = o_ref.shape[0]
    for i in range(4):
        for j in range(4):
            for h in range(lines // SUBS):
                start = (i * lines + h * SUBS) * 4 + j
                wo_ref[i, j, pl.ds(h * SUBS, SUBS), :] = w_ref[pl.ds(start, SUBS, stride=4), :]
    sources = []
    for q in range(4):
        four = o_ref[pl.ds(q, 4, stride=4), :]
        sources.append(jnp.concatenate([four, four], axis=0))
    for part in range(2):
        place_ref[part] = pick_order(sources, (tile_iota(0) >> 2) + 2 * part)
    for i in range(4):
        four = 1.0 / v2_ref[pl.ds(i * 16 + i, 4, stride=4), :]
        m2_ref[i, pl.ds(0, 4), :] = four
        m2_ref[i, pl.ds(4, 4), :] = four


def fine_inverse(row_ref, _, agg_ref):
    agg_ref[...] = inverse_order(row_ref[...], agg_ref.shape[0])


def middle_blocks(v_ref, c_ref, _, vo_ref, co_ref):
    def body(ki, carry):
        k, i = ki // 4, ki % 4
        for j in range(4):
            for odd in range(2):
                start = ((2 * k + odd) * 4 + i) * 16 + j
                vo_ref[k, i, j, pl.ds(4 * odd, 4), :] = v_ref[pl.ds(start, 4, stride=4), :]
        return carry

    lax.fori_loop(0, NNZ // 2 * 4, body, 0)
    for k in range(NNZ // 2):
        for odd in range(2):
            co_ref[k, pl.ds(4 * odd, 4), :] = c_ref[pl.ds(2 * k + odd, 4, stride=NNZ), :]


def middle_tables(w_ref, row_ref, o_ref, _, wo_ref, agg_ref, place_ref):
    lines = o_ref.shape[0]
    for i in range(4):
        for j in range(4):
            four = w_ref[pl.ds(i * lines * 4 + j, 4, stride=4), :]
            wo_ref[i, j, pl.ds(0, 4), :] = four
            wo_ref[i, j, pl.ds(4, 4), :] = four
    agg = inverse_order(row_ref[...], lines)
    agg_ref[...] = jnp.concatenate([agg, agg], axis=0)
    sources = [wide(o_ref[pl.ds(q, 1), :]) for q in range(4)]
    place_ref[...] = pick_order(sources, tile_iota(0) & 3)


def middle_pad(pad_ref, j, x):
    for twice in range(2):
        pad_ref[pl.ds((twice * 4 + j) * SUBS, SUBS), :] = x


def middle_out(out_ref, pad_ref, s_ref):
    out_ref[...] = outgoing(
        lambda r: pad_ref[pl.ds(r, SUBS, stride=SUBS), :], 4, s_ref[...]
    )


def middle_local(x_ref, v_ref, c_ref, a_ref):
    acc = [jnp.zeros((SUBS, LANES), F32) for _ in range(4)]
    for j in range(4):
        source = [wide(x_ref[j, pl.ds(r, 1), :]) for r in range(4)]
        for kp in range(NNZ // 2):
            col = c_ref[kp]
            got = pick_lines(source, col >> 7, col & (LANES - 1))
            for i in range(4):
                acc[i] = acc[i] + v_ref[kp, i, j] * got
    for i in range(4):
        a_ref[i] = acc[i]


def middle_residual(arrivals, b_ref, a_ref, v_ref, c_ref, edge_ref):
    halo_lines(arrivals, edge_ref)
    acc = [a_ref[i] for i in range(4)]
    for j in range(4):
        source = [wide(edge_ref[pl.ds(4 * e + j, 1), :]) for e in range(2)]
        for kp in range(NNZ // 2):
            col = c_ref[kp]
            got = pick_lines(source, col >> 7, col & (LANES - 1), 4)
            for i in range(4):
                acc[i] = acc[i] + v_ref[kp, i, j] * got
    return [b_ref[i] - duplicate(acc[i]) for i in range(4)]


def middle_update(factors, resid, m_ref, x_ref, d_ref):
    keep, gain = factors
    xs, ds = [], []
    for i in range(4):
        d = gain * (m_ref[i] * resid[i])
        if keep:
            d = keep * d_ref[i] + d
        ds.append(d)
        xs.append(x_ref[i] + d)
    return xs, ds


def middle_step(factors, last, *refs):
    arrivals = refs[:5]
    b_ref, a_ref, m_ref, x_ref, d_ref, v_ref, c_ref, s_ref, xo_ref, out_ref = refs[5:15]
    do_ref = refs[15] if last is False else None
    edge_ref, pad_ref = refs[-2:]
    resid = middle_residual(arrivals, b_ref, a_ref, v_ref, c_ref, edge_ref)
    xs, ds = middle_update(factors, resid, m_ref, x_ref, d_ref)
    for i in range(4):
        xo_ref[i] = xs[i]
        if not last:
            do_ref[i] = ds[i]
        middle_pad(pad_ref, i, xs[i])
    middle_out(out_ref, pad_ref, s_ref)


def middle_restrict(*refs):
    arrivals = refs[:5]
    b_ref, a_ref, v_ref, c_ref, w_ref, p_ref, out_ref, edge_ref, line_ref = refs[5:]
    resid = middle_residual(arrivals, b_ref, a_ref, v_ref, c_ref, edge_ref)
    place = p_ref[...]
    high, lane = place >> 7, place & (LANES - 1)
    for j in range(4):
        total = w_ref[0, j] * resid[0]
        for i in range(1, 4):
            total = total + w_ref[i, j] * resid[i]
        line_ref[j] = total
        source = [wide(line_ref[j, pl.ds(r, 1), :]) for r in range(4)]
        got = pick_lines(source, high, lane)
        got = got + pltpu.roll(got, 2, 0)
        got = got + pltpu.roll(got, 1, 0)
        out_ref[pl.ds(j, 1), :] = got[0:1]
        out_ref[pl.ds(4 + j, 1), :] = got[0:1]


def middle_prolong(factors, *refs):
    arrivals = refs[:5]
    (b_ref, a_ref, m_ref, x_ref, d_ref, v_ref, c_ref, x1_ref, w_ref, agg_ref, s_ref, xo_ref, out_ref, edge_ref, line_ref, pad_ref) = refs[5:]
    lines = x1_ref.shape[1]
    resid = middle_residual(arrivals, b_ref, a_ref, v_ref, c_ref, edge_ref)
    xs, _ = middle_update(factors, resid, m_ref, x_ref, d_ref)
    for j in range(4):
        line_ref[j] = xs[j]
    for h in range(lines // SUBS):
        rows = pl.ds(h * SUBS, SUBS)
        agg = agg_ref[rows, :]
        high, lane = agg >> 7, agg & (LANES - 1)
        spread = [
            pick_lines([wide(line_ref[j, pl.ds(r, 1), :]) for r in range(4)], high, lane)
            for j in range(4)
        ]
        for i in range(4):
            placed = w_ref[i, 0, rows, :] * spread[0]
            for j in range(1, 4):
                placed = placed + w_ref[i, j, rows, :] * spread[j]
            x = x1_ref[i, rows, :] + placed
            xo_ref[i, rows, :] = x
            for twice in range(2):
                pad_ref[pl.ds((twice * 4 + i) * lines + h * SUBS, SUBS), :] = x
    out_ref[...] = outgoing(
        lambda r: pad_ref[pl.ds(r, SUBS, stride=lines), :], lines, s_ref[...]
    )


def coarse_tables(group, *refs):
    vo_ref, co_ref, mo_ref, pad_ref = refs[-4:]
    me = refs[0][0]
    for piece, places in zip(refs[1:-5], span_places(group)):
        for t, place in enumerate(places):
            pad_ref[place] = piece[t]
    for h in range(group // SUBS):
        rows = pl.ds(h * SUBS, SUBS)
        for ki in range(NNZ * 4):
            k, i = ki // 4, ki % 4
            for j in range(4):
                tile = pad_ref[rows, ki * 4 + j, :]
                vo_ref[k, i, j, rows, :] = tile
                if k == 0 and i == j:
                    mo_ref[i, rows, :] = 1.0 / tile
        for k in range(NNZ):
            col = pad_ref[rows, NNZ * 16 + k, :].astype(I32)
            co_ref[k, rows, :] = ((col >> 7) ^ me) * LANES + (col & (LANES - 1))


def coarse_solve(group, *refs):
    (v_ref, c_ref, m_ref, x2_ref, w_ref, agg_ref, s_ref, xo_ref, out_ref, b_ref, x_ref, d_ref, pad_ref) = refs[-13:]
    first = [0] + list(range(group - 1, 1, -2))
    for swapped, piece in enumerate(refs[:-13]):
        for t, place in enumerate([m ^ swapped for m in first]):
            for j in range(4):
                b_ref[j, pl.ds(place, 1), :] = piece[t, pl.ds(j, 1), :]
    blocks = group // SUBS
    for j in range(4):
        first = m_ref[j] * b_ref[j]
        x_ref[j] = first
        d_ref[j] = first
    for keep, gain in cheb_factors(KC)[1:]:
        resid = []
        for h in range(blocks):
            rows = pl.ds(h * SUBS, SUBS)
            acc = [b_ref[i, rows, :] for i in range(4)]
            for k in range(NNZ):
                col = c_ref[k, rows, :]
                high, lane = col >> 7, col & (LANES - 1)
                for j in range(4):
                    if k:
                        got = pick_lines(
                            [wide(x_ref[j, pl.ds(r, 1), :]) for r in range(group)], high, lane
                        )
                    else:
                        got = x_ref[j, rows, :]
                    for i in range(4):
                        acc[i] = acc[i] - v_ref[k, i, j, rows, :] * got
            resid.append(acc)
        for h in range(blocks):
            rows = pl.ds(h * SUBS, SUBS)
            for i in range(4):
                d = keep * d_ref[i, rows, :] + gain * (m_ref[i, rows, :] * resid[h][i])
                d_ref[i, rows, :] = d
                x_ref[i, rows, :] = x_ref[i, rows, :] + d
    lane = agg_ref[...]
    spread = [pick(wide(x_ref[j, pl.ds(0, 1), :]), lane) for j in range(4)]
    for i in range(4):
        x = x2_ref[i]
        for j in range(4):
            x = x + w_ref[i, j] * spread[j]
        xo_ref[i] = x
        middle_pad(pad_ref, i, x)
    middle_out(out_ref, pad_ref, s_ref)


def call(body, outs, args, scratch=(), free=(), smem=(), hbm=(), limit=16):
    specs = []
    for index in range(len(args)):
        if index in hbm:
            specs.append(pl.BlockSpec(memory_space=pltpu.HBM))
        elif index in free:
            specs.append(pl.BlockSpec(memory_space=pl.ANY))
        elif index in smem:
            specs.append(pl.BlockSpec(memory_space=pltpu.SMEM))
        else:
            specs.append(pl.BlockSpec(memory_space=pltpu.VMEM))
    single = not isinstance(outs, (list, tuple))
    shapes = [outs] if single else list(outs)
    result = pl.pallas_call(
        body,
        out_shape=shapes,
        in_specs=specs,
        out_specs=[pl.BlockSpec(memory_space=pltpu.VMEM) for _ in shapes],
        scratch_shapes=list(scratch),
        compiler_params=pltpu.CompilerParams(vmem_limit_bytes=limit * 2**20),
    )(*args)
    return result[0] if single else result


def shape(*dims, dtype=F32):
    return jax.ShapeDtypeStruct(dims, dtype)


def vmem(*dims, dtype=F32):
    return pltpu.VMEM(dims, dtype)


def native_rows(x):
    lines = x.shape[-1] // LANES
    split = x.reshape(x.shape[:-1] + (lines, LANES))
    return jnp.swapaxes(split, -2, -3).reshape(-1, LANES)


def from_native(rows, lines):
    return jnp.swapaxes(rows.reshape(lines, 4, LANES), 0, 1).reshape(4, lines * LANES)


def exchange(mesh, out, which):
    slabs, count = mesh.shape["stream"], mesh.shape["span"]

    def swap(partner):
        pairs = []
        for a in range(slabs):
            for b in range(count):
                to_a, to_b = partner(a, b)
                pairs.append((a * count + b, to_a * count + to_b))
        return lax.ppermute(out, AXES, pairs)

    def odd(index):
        return index + 1 if index % 2 else index - 1

    def span_odd(a, b):
        return (a, odd(b)) if 0 <= odd(b) < count else (a ^ 1, b)

    partners = [
        lambda a, b: (odd(a) % slabs, b),
        lambda a, b: (a ^ 1, b),
        span_odd,
        lambda a, b: (a, b ^ 1),
    ]
    return [swap(partner) for partner in partners] + [which]


def halo_choice(a, b, count):
    row, lane = (lax.broadcasted_iota(I32, (SUBS, LANES), d) for d in range(2))
    left = lane < LANES // 2
    index = jnp.where(row < 4, a, b)
    even = left == (index % 2 == 1)
    outside = (row >= 4) & jnp.where(left, b == 0, b == count - 1)
    return jnp.where(outside, 0, jnp.where(even, 1, 2)).astype(I32)


def span_places(group):
    places = [[0]]
    mask = group // 2
    while mask:
        places.append([mask ^ m for piece in places for m in piece])
        mask //= 2
    return places


def span_swap(mesh, value, mask):
    slabs, count = mesh.shape["stream"], mesh.shape["span"]
    pairs = [
        (a * count + b, a * count + (b ^ mask)) for a in range(slabs) for b in range(count)
    ]
    return lax.ppermute(value, AXES, pairs)


def span_stage(mesh, pieces, out):
    pieces, _ = lax.optimization_barrier((pieces, out))
    held = jnp.concatenate(pieces)
    return pieces + [span_swap(mesh, held, mesh.shape["span"] // 2 // held.shape[0])]


def span_gather(mesh, value):
    masks = range(mesh.shape["span"] - 1, 1, -2)
    held = jnp.stack([value] + [span_swap(mesh, value, m) for m in masks])
    return [held, span_swap(mesh, held, 1)]


def per_device(mesh, right_side, fine_values, fine_columns, fine_sends, fine_order, fine_weights, middle_values, middle_columns, middle_sends, middle_order, middle_weights, coarsest_values, coarsest_columns):
    group = mesh.shape["span"]
    lines = right_side.shape[1] // LANES
    tile = shape(SUBS, LANES)
    vec1 = shape(4, lines, LANES)
    vec2 = shape(4, SUBS, LANES)
    edge = vmem(SUBS, LANES)
    pad1 = vmem(SUBS * lines, LANES)
    pad2 = vmem(SUBS * SUBS, LANES)
    factors = cheb_factors(KSM)
    me = lax.axis_index("span").astype(I32)
    choice = halo_choice(lax.axis_index("stream").astype(I32), me, group)
    values1 = native_rows(fine_values)
    values2 = native_rows(middle_values)

    starts = [
        values1,
        native_rows(right_side),
        fine_sends,
        middle_sends,
        native_columns(fine_columns),
        coarsest_values.reshape(NNZ * 16, LANES),
        coarsest_columns,
    ]
    int_tile = shape(SUBS, LANES, dtype=I32)
    b1, m1, x1, send1, send2, c1, own3, out = call(
        fine_start,
        [
            vec1,
            vec1,
            vec1,
            int_tile,
            int_tile,
            shape(NNZ, lines, LANES, dtype=I32),
            shape(1, NNZ * 17, LANES),
            tile,
        ],
        [pltpu.with_memory_space_constraint(x, pltpu.HBM) for x in starts],
        [pad1, vmem(16 * lines, LANES)]
        + [vmem(*x.shape, dtype=x.dtype) for x in starts[1:]]
        + [pltpu.SemaphoreType.DMA((len(starts),))],
        hbm=range(len(starts)),
    )
    d1 = x1
    v1 = call(fine_prepare, shape(NNZ, 4, 4, lines, LANES), [values1, out], free=(1,))

    def fine_part(x):
        return call(fine_local, vec1, [x, b1, v1, c1], [vmem(4, lines, SUBS, LANES)])

    def fine_next(which, arrived, resid, x, d, after=()):
        args = arrived + [resid, v1, c1, m1, x, d, send1]
        last = which == KSM - 1
        result = call(
            lambda *refs: fine_step(
                factors[which], last, *(refs[: len(args)] + refs[len(args) + len(after) :])
            ),
            [vec1, tile] + ([] if last else [vec1]),
            args + list(after),
            [edge, pad1],
            free=range(len(args), len(args) + len(after)),
        )
        return result[0], (None if last else result[2]), result[1]

    arrived = exchange(mesh, out, choice)
    pieces3 = span_stage(mesh, [own3], out)
    resid = fine_part(x1)
    x1, d1, out = fine_next(1, arrived, resid, x1, d1)

    arrived = exchange(mesh, out, choice)
    resid = fine_part(x1)
    w1, place1, m2 = call(
        fine_tables,
        [
            shape(4, 4, lines, LANES),
            shape(2, SUBS, LANES, dtype=I32),
            vec2,
        ],
        [native_rows(fine_weights), fine_order.reshape(lines, LANES), values2, out],
        free=(3,),
    )
    x1, d1, out = fine_next(2, arrived, resid, x1, d1, [m2])

    arrived = exchange(mesh, out, choice)
    resid = fine_part(x1)
    b2, x2, out = call(
        lambda *refs: fine_restrict(*(refs[2:4] + refs[:2] + refs[4:])),
        [vec2, vec2, tile],
        arrived[2:4] + arrived[:2] + arrived[4:] + [resid, v1, c1, w1, place1, m2, send2],
        [edge, vmem(4, lines, LANES), pad2],
    )
    d2 = x2

    def middle_part(x):
        return call(middle_local, vec2, [x, v2, c2])

    def middle_next(which, arrived, x, d, after=()):
        args = arrived + [b2, middle_part(x), m2, x, d, v2, c2, send2]
        last = which == KSM - 1
        result = call(
            lambda *refs: middle_step(
                factors[which], last, *(refs[: len(args)] + refs[len(args) + len(after) :])
            ),
            [vec2, tile] + ([] if last else [vec2]),
            args + list(after),
            [edge, pad2],
            free=range(len(args), len(args) + len(after)),
        )
        return result[0], (None if last else result[2]), result[1]

    arrived = exchange(mesh, out, choice)
    for _ in range(len(span_places(group)) - 3):
        pieces3 = span_stage(mesh, pieces3, out)
    v2, c2 = call(
        middle_blocks,
        [shape(NNZ // 2, 4, 4, SUBS, LANES), shape(NNZ // 2, SUBS, LANES, dtype=I32)],
        [values2, native_columns(middle_columns), out],
        free=(2,),
    )
    x2, d2, out = middle_next(1, arrived, x2, d2)

    arrived = exchange(mesh, out, choice)
    w2, agg2, place2 = call(
        middle_tables,
        [
            shape(4, 4, SUBS, LANES),
            shape(SUBS, LANES, dtype=I32),
            shape(SUBS, LANES, dtype=I32),
        ],
        [native_rows(middle_weights), middle_order, middle_order.reshape(-1, LANES), out],
        free=(3,),
    )
    pieces3 = span_stage(mesh, pieces3, out)
    x2, d2, out = middle_next(2, arrived, x2, d2, [agg2])

    arrived = exchange(mesh, out, choice)
    agg1 = call(fine_inverse, shape(lines, LANES, dtype=I32), [fine_order, out], free=(1,))
    rhs3 = call(
        lambda *refs: middle_restrict(*(refs[:11] + refs[12:])),
        tile,
        arrived + [b2, middle_part(x2), v2, c2, w2, place2, agg1],
        [edge, vmem(4, SUBS, LANES)],
        free=(11,),
    )
    v3, c3, m3 = call(
        lambda *refs: coarse_tables(group, *refs),
        [shape(NNZ, 4, 4, group, LANES), shape(NNZ, group, LANES, dtype=I32), shape(4, group, LANES)],
        [me.reshape(1)] + pieces3 + [rhs3],
        [vmem(group, NNZ * 17, LANES)],
        free=(1 + len(pieces3),),
        smem=(0,),
    )
    vec3 = vmem(4, group, LANES)
    x2, out = call(
        lambda *refs: coarse_solve(group, *refs),
        [vec2, tile],
        span_gather(mesh, rhs3) + [v3, c3, m3, x2, w2, agg2, send2],
        [vec3, vec3, vec3, pad2],
    )
    arrived = exchange(mesh, out, choice)
    x2, d2, out = middle_next(0, arrived, x2, x2)
    arrived = exchange(mesh, out, choice)
    x2, d2, out = middle_next(1, arrived, x2, d2)
    arrived = exchange(mesh, out, choice)
    x1, out = call(
        lambda *refs: middle_prolong(factors[2], *refs),
        [vec1, tile],
        arrived + [b2, middle_part(x2), m2, x2, d2, v2, c2, x1, w1, agg1, send1],
        [edge, vmem(4, SUBS, LANES), pad1],
    )
    d1 = x1
    for which in range(KSM):
        arrived = exchange(mesh, out, choice)
        resid = fine_part(x1)
        x1, d1, out = fine_next(which, arrived, resid, x1, d1)
    arrived = exchange(mesh, out, choice)
    resid = fine_part(x1)
    rows = shape(4 * lines, LANES)
    solved, left = call(fine_finish, [rows, rows], arrived + [resid, v1, c1, x1], [edge])
    return from_native(solved, lines), from_native(left, lines)


def native_columns(columns):
    lines = columns.shape[1] // LANES
    return jnp.swapaxes(columns.reshape(NNZ, lines, LANES), 0, 1).reshape(-1, LANES)


def solution(mesh):
    both = ("stream", "span")
    in_specs = (
        P(None, both),
        P(None, None, None, both),
        P(None, both),
        P(None, both),
        P(both, None),
        P(None, None, both),
        P(None, None, None, both),
        P(None, both),
        P(None, both),
        P(both, None),
        P(None, None, both),
        P(None, None, None, both),
        P(None, both),
    )
    return jax.shard_map(
        lambda *args: per_device(mesh, *args),
        mesh=mesh,
        in_specs=in_specs,
        out_specs=(P(None, both), P(None, both)),
        check_vma=False,
    )
```

```python
import jax
import jax.numpy as jnp
from jax import lax
from jax.experimental import pallas as pl
from jax.experimental.pallas import tpu as pltpu
from jax.sharding import PartitionSpec as P

KSM = 3
KC = 4
NNZ = 8
LANES = 128
SUBS = 8

CHEB_CENTRE = 1.0
CHEB_RADIUS = 0.9
AXES = ("stream", "span")
F32 = jnp.float32
I32 = jnp.int32


def cheb_factors(degree):
    sigma = CHEB_CENTRE / CHEB_RADIUS
    rho = 1.0 / sigma
    factors = [(0.0, 1.0 / CHEB_CENTRE)]
    for _ in range(degree - 1):
        rho_next = 1.0 / (2.0 * sigma - rho)
        factors.append((rho_next * rho, 2.0 * rho_next / CHEB_RADIUS))
        rho = rho_next
    return factors


def tile_iota(dim):
    return lax.broadcasted_iota(I32, (SUBS, LANES), dim)


def pick(line, lane):
    return jnp.take_along_axis(line, lane, axis=1, mode="promise_in_bounds")


def wide(line):
    return jnp.broadcast_to(line, (SUBS, LANES))


def pick_lines(lines, high, lane, first=0):
    result = jnp.zeros((SUBS, LANES), F32)
    for r, line in enumerate(lines):
        result = jnp.where(high == first + r, pick(line, lane), result)
    return result


def halo_lines(arrivals, edge_ref):
    s_odd, s_even, p_odd, p_even, which = [r[...] for r in arrivals]
    upper = tile_iota(0) < 4
    even = jnp.where(upper, s_even, p_even)
    odd = jnp.where(upper, s_odd, p_odd)
    edge_ref[...] = jnp.where(which == 1, even, jnp.where(which == 2, odd, 0.0))


def outgoing(lines_of, count, sends):
    high, lane = sends >> 7, sends & (LANES - 1)
    return pick_lines([lines_of(r) for r in range(count)], high, lane)


def send_table(s_ref):
    stream = jnp.concatenate([s_ref[pl.ds(1, 1), :], s_ref[pl.ds(0, 1), :]], axis=1)
    span = jnp.concatenate([s_ref[pl.ds(3, 1), :], s_ref[pl.ds(2, 1), :]], axis=1)
    return jnp.where(tile_iota(0) < 4, stream, span)


def duplicate(x):
    return x + pltpu.roll(x, 4, 0)


def fine_start(*refs):
    sources = refs[:7]
    (bo_ref, mo_ref, x_ref, so_ref, s2o_ref, co_ref, o3_ref, out_ref, pad_ref) = refs[7:16]
    held, sems = refs[16:23], refs[23]
    copies = [
        pltpu.make_async_copy(source.at[pl.ds(0, there.shape[0]), :], there, sems.at[t])
        for t, (source, there) in enumerate(zip(sources, held))
    ]
    for copy in copies:
        copy.start()
    for copy in copies:
        copy.wait()
    v_ref, b_ref, s_ref, s2_ref, c_ref, v3_ref, c3_ref = held
    sends = send_table(s_ref)
    so_ref[...] = sends
    s2o_ref[...] = send_table(s2_ref)
    count = v3_ref.shape[0]
    o3_ref[0, pl.ds(0, count), :] = v3_ref[...]
    o3_ref[0, pl.ds(count, NNZ), :] = c3_ref[...].astype(F32)
    for k in range(NNZ):
        for h in range(co_ref.shape[1] // SUBS):
            co_ref[k, pl.ds(h * SUBS, SUBS), :] = c_ref[
                pl.ds(h * SUBS * NNZ + k, SUBS, stride=NNZ), :
            ]
    lines = bo_ref.shape[1]
    for i in range(4):
        for h in range(lines // SUBS):
            rows = pl.ds(h * SUBS, SUBS)
            native = pl.ds(h * SUBS * 4 + i, SUBS, stride=4)
            b = b_ref[native, :]
            m = 1.0 / v_ref[pl.ds((i * lines + h * SUBS) * 4 + i, SUBS, stride=4), :]
            x = m * b
            bo_ref[i, rows, :] = b
            mo_ref[i, rows, :] = m
            x_ref[i, rows, :] = x
            for twice in range(2):
                pad_ref[pl.ds((twice * 4 + i) * lines + h * SUBS, SUBS), :] = x
    out_ref[...] = outgoing(
        lambda r: pad_ref[pl.ds(r, SUBS, stride=lines), :], lines, sends
    )


def fine_first(x_ref, b_ref, v_ref, c_ref, r_ref, vo_ref, line_ref):
    lines = x_ref.shape[1]

    def values(k, i, j, h):
        start = ((k * 4 + i) * lines + h * SUBS) * 4 + j
        tile = v_ref[pl.ds(start, SUBS, stride=4), :]
        vo_ref[k, i, j, pl.ds(h * SUBS, SUBS), :] = tile
        return tile

    fine_product(values, x_ref, b_ref, c_ref, r_ref, line_ref)


def fine_local(x_ref, b_ref, v_ref, c_ref, r_ref, line_ref):
    def values(k, i, j, h):
        return v_ref[k, i, j, pl.ds(h * SUBS, SUBS), :]

    fine_product(values, x_ref, b_ref, c_ref, r_ref, line_ref)


def fine_product(values, x_ref, b_ref, c_ref, r_ref, line_ref):
    lines = x_ref.shape[1]
    halves = lines // SUBS
    for j in range(4):
        for r in range(lines):
            line_ref[j, r] = wide(x_ref[j, pl.ds(r, 1), :])
    acc = []
    for h in range(halves):
        rows = pl.ds(h * SUBS, SUBS)
        for i in range(4):
            total = b_ref[i, rows, :]
            for j in range(4):
                total = total - values(0, i, j, h) * x_ref[j, rows, :]
            acc.append(total)

    def body(k, acc):
        acc = list(acc)
        for h in range(halves):
            rows = pl.ds(h * SUBS, SUBS)
            col = c_ref[k, rows, :]
            high, lane = col >> 7, col & (LANES - 1)
            for j in range(4):
                got = pick_lines([line_ref[j, r] for r in range(lines)], high, lane)
                for i in range(4):
                    acc[4 * h + i] = acc[4 * h + i] - values(k, i, j, h) * got
        return tuple(acc)

    acc = lax.fori_loop(1, NNZ, body, tuple(acc))
    for h in range(halves):
        for i in range(4):
            r_ref[i, pl.ds(h * SUBS, SUBS), :] = acc[4 * h + i]


def fine_remote(arrivals, r_ref, v_ref, c_ref, edge_ref):
    lines = r_ref.shape[1]
    halves = lines // SUBS
    halo_lines(arrivals, edge_ref)
    edges = [[wide(edge_ref[pl.ds(4 * e + j, 1), :]) for e in range(2)] for j in range(4)]
    result = []
    for h in range(halves):
        rows = pl.ds(h * SUBS, SUBS)
        acc = [r_ref[i, rows, :] for i in range(4)]
        for k in range(1, NNZ):
            col = c_ref[k, rows, :]
            high, lane = col >> 7, col & (LANES - 1)
            for j in range(4):
                got = pick_lines(edges[j], high, lane, lines)
                for i in range(4):
                    acc[i] = acc[i] - v_ref[k, i, j, rows, :] * got
        result.append(acc)
    return result


def fine_step(factors, last, *refs):
    arrivals = refs[:5]
    r_ref, v_ref, c_ref, m_ref, x_ref, d_ref, s_ref, xo_ref, out_ref = refs[5:14]
    do_ref = refs[14] if last is False else None
    edge_ref, pad_ref = refs[-2:]
    keep, gain = factors
    lines = r_ref.shape[1]
    resid = fine_remote(arrivals, r_ref, v_ref, c_ref, edge_ref)
    for h in range(lines // SUBS):
        rows = pl.ds(h * SUBS, SUBS)
        for i in range(4):
            d = gain * (m_ref[i, rows, :] * resid[h][i])
            if keep:
                d = keep * d_ref[i, rows, :] + d
            x = x_ref[i, rows, :] + d
            if not last:
                do_ref[i, rows, :] = d
            xo_ref[i, rows, :] = x
            for twice in range(2):
                pad_ref[pl.ds((twice * 4 + i) * lines + h * SUBS, SUBS), :] = x
    out_ref[...] = outgoing(
        lambda r: pad_ref[pl.ds(r, SUBS, stride=lines), :], lines, s_ref[...]
    )


def fine_finish(*refs):
    arrivals = refs[:5]
    r_ref, v_ref, c_ref, x_ref, so_ref, ro_ref, edge_ref = refs[5:]
    lines = r_ref.shape[1]
    resid = fine_remote(arrivals, r_ref, v_ref, c_ref, edge_ref)
    for h in range(lines // SUBS):
        for i in range(4):
            native = pl.ds(h * SUBS * 4 + i, SUBS, stride=4)
            so_ref[native, :] = x_ref[i, pl.ds(h * SUBS, SUBS), :]
            ro_ref[native, :] = resid[h][i]


def fine_restrict(*refs):
    arrivals = refs[:5]
    (r_ref, v_ref, c_ref, w_ref, p_ref, m2_ref, s2_ref, b2_ref, x2_ref, out_ref, edge_ref, line_ref, pad_ref) = refs[5:]
    lines = r_ref.shape[1]
    resid = fine_remote(arrivals, r_ref, v_ref, c_ref, edge_ref)
    for h in range(lines // SUBS):
        rows = pl.ds(h * SUBS, SUBS)
        for j in range(4):
            total = w_ref[0, j, rows, :] * resid[h][0]
            for i in range(1, 4):
                total = total + w_ref[i, j, rows, :] * resid[h][i]
            line_ref[j, rows, :] = total
    for j in range(4):
        total = None
        source = [wide(line_ref[j, pl.ds(r, 1), :]) for r in range(lines)]
        for part in range(2):
            place = p_ref[part]
            got = pick_lines(source, place >> 7, place & (LANES - 1))
            total = got if total is None else total + got
        b2 = duplicate(total)
        x2 = m2_ref[j] * b2
        b2_ref[j] = b2
        x2_ref[j] = x2
        middle_pad(pad_ref, j, x2)
    middle_out(out_ref, pad_ref, s2_ref)


def inverse_order(o_row, lines):
    count = lines * LANES
    high, lane = o_row >> 7, o_row & (LANES - 1)
    coarse = lax.broadcasted_iota(I32, (1, count), 1) >> 2
    here = lax.broadcasted_iota(I32, (lines, count), 0) == high
    upper = jnp.where(here, (coarse >> 4).astype(F32), 0.0)
    lower = jnp.where(here, (coarse & 15).astype(F32), 0.0)
    left = jnp.concatenate([upper, lower], axis=0).astype(jnp.bfloat16)
    right = jnp.where(
        lax.broadcasted_iota(I32, (LANES, count), 0) == lane, 1.0, 0.0
    ).astype(jnp.bfloat16)
    found = lax.dot_general(
        left, right, (((1,), (1,)), ((), ())), preferred_element_type=F32
    )
    return (found[:lines] * 16.0 + found[lines:]).astype(I32)


def pick_order(sources, unit):
    lane = tile_iota(1)
    place = 4 * (lane & 31) + unit
    result = jnp.zeros((SUBS, LANES), I32)
    for q, source in enumerate(sources):
        result = jnp.where((lane >> 5) == q, pick(source, place), result)
    return result


def fine_tables(w_ref, o_ref, v2_ref, _, wo_ref, place_ref, m2_ref):
    lines = o_ref.shape[0]
    for i in range(4):
        for j in range(4):
            for h in range(lines // SUBS):
                start = (i * lines + h * SUBS) * 4 + j
                wo_ref[i, j, pl.ds(h * SUBS, SUBS), :] = w_ref[pl.ds(start, SUBS, stride=4), :]
    sources = []
    for q in range(4):
        four = o_ref[pl.ds(q, 4, stride=4), :]
        sources.append(jnp.concatenate([four, four], axis=0))
    for part in range(2):
        place_ref[part] = pick_order(sources, (tile_iota(0) >> 2) + 2 * part)
    for i in range(4):
        four = 1.0 / v2_ref[pl.ds(i * 16 + i, 4, stride=4), :]
        m2_ref[i, pl.ds(0, 4), :] = four
        m2_ref[i, pl.ds(4, 4), :] = four


def fine_inverse(row_ref, _, agg_ref):
    agg_ref[...] = inverse_order(row_ref[...], agg_ref.shape[0])


def middle_blocks(v_ref, c_ref, _, vo_ref, co_ref):
    def body(ki, carry):
        k, i = ki // 4, ki % 4
        for j in range(4):
            for odd in range(2):
                start = ((2 * k + odd) * 4 + i) * 16 + j
                vo_ref[k, i, j, pl.ds(4 * odd, 4), :] = v_ref[pl.ds(start, 4, stride=4), :]
        return carry

    lax.fori_loop(0, NNZ // 2 * 4, body, 0)
    for k in range(NNZ // 2):
        for odd in range(2):
            co_ref[k, pl.ds(4 * odd, 4), :] = c_ref[pl.ds(2 * k + odd, 4, stride=NNZ), :]


def middle_tables(w_ref, row_ref, o_ref, _, wo_ref, agg_ref, place_ref):
    lines = o_ref.shape[0]
    for i in range(4):
        for j in range(4):
            four = w_ref[pl.ds(i * lines * 4 + j, 4, stride=4), :]
            wo_ref[i, j, pl.ds(0, 4), :] = four
            wo_ref[i, j, pl.ds(4, 4), :] = four
    agg = inverse_order(row_ref[...], lines)
    agg_ref[...] = jnp.concatenate([agg, agg], axis=0)
    sources = [wide(o_ref[pl.ds(q, 1), :]) for q in range(4)]
    place_ref[...] = pick_order(sources, tile_iota(0) & 3)


def middle_pad(pad_ref, j, x):
    for twice in range(2):
        pad_ref[pl.ds((twice * 4 + j) * SUBS, SUBS), :] = x


def middle_out(out_ref, pad_ref, s_ref):
    out_ref[...] = outgoing(
        lambda r: pad_ref[pl.ds(r, SUBS, stride=SUBS), :], 4, s_ref[...]
    )


def middle_local(x_ref, v_ref, c_ref, a_ref):
    acc = [jnp.zeros((SUBS, LANES), F32) for _ in range(4)]
    for j in range(4):
        source = [wide(x_ref[j, pl.ds(r, 1), :]) for r in range(4)]
        for kp in range(NNZ // 2):
            col = c_ref[kp]
            got = pick_lines(source, col >> 7, col & (LANES - 1))
            for i in range(4):
                acc[i] = acc[i] + v_ref[kp, i, j] * got
    for i in range(4):
        a_ref[i] = acc[i]


def middle_residual(arrivals, b_ref, a_ref, v_ref, c_ref, edge_ref):
    halo_lines(arrivals, edge_ref)
    acc = [a_ref[i] for i in range(4)]
    for j in range(4):
        source = [wide(edge_ref[pl.ds(4 * e + j, 1), :]) for e in range(2)]
        for kp in range(NNZ // 2):
            col = c_ref[kp]
            got = pick_lines(source, col >> 7, col & (LANES - 1), 4)
            for i in range(4):
                acc[i] = acc[i] + v_ref[kp, i, j] * got
    return [b_ref[i] - duplicate(acc[i]) for i in range(4)]


def middle_update(factors, resid, m_ref, x_ref, d_ref):
    keep, gain = factors
    xs, ds = [], []
    for i in range(4):
        d = gain * (m_ref[i] * resid[i])
        if keep:
            d = keep * d_ref[i] + d
        ds.append(d)
        xs.append(x_ref[i] + d)
    return xs, ds


def middle_step(factors, last, *refs):
    arrivals = refs[:5]
    b_ref, a_ref, m_ref, x_ref, d_ref, v_ref, c_ref, s_ref, xo_ref, out_ref = refs[5:15]
    do_ref = refs[15] if last is False else None
    edge_ref, pad_ref = refs[-2:]
    resid = middle_residual(arrivals, b_ref, a_ref, v_ref, c_ref, edge_ref)
    xs, ds = middle_update(factors, resid, m_ref, x_ref, d_ref)
    for i in range(4):
        xo_ref[i] = xs[i]
        if not last:
            do_ref[i] = ds[i]
        middle_pad(pad_ref, i, xs[i])
    middle_out(out_ref, pad_ref, s_ref)


def middle_restrict(*refs):
    arrivals = refs[:5]
    b_ref, a_ref, v_ref, c_ref, w_ref, p_ref, out_ref, edge_ref, line_ref = refs[5:]
    resid = middle_residual(arrivals, b_ref, a_ref, v_ref, c_ref, edge_ref)
    place = p_ref[...]
    high, lane = place >> 7, place & (LANES - 1)
    for j in range(4):
        total = w_ref[0, j] * resid[0]
        for i in range(1, 4):
            total = total + w_ref[i, j] * resid[i]
        line_ref[j] = total
        source = [wide(line_ref[j, pl.ds(r, 1), :]) for r in range(4)]
        got = pick_lines(source, high, lane)
        got = got + pltpu.roll(got, 2, 0)
        got = got + pltpu.roll(got, 1, 0)
        out_ref[pl.ds(j, 1), :] = got[0:1]
        out_ref[pl.ds(4 + j, 1), :] = got[0:1]


def middle_prolong(factors, *refs):
    arrivals = refs[:5]
    (b_ref, a_ref, m_ref, x_ref, d_ref, v_ref, c_ref, x1_ref, w_ref, agg_ref, s_ref, xo_ref, out_ref, edge_ref, line_ref, pad_ref) = refs[5:]
    lines = x1_ref.shape[1]
    resid = middle_residual(arrivals, b_ref, a_ref, v_ref, c_ref, edge_ref)
    xs, _ = middle_update(factors, resid, m_ref, x_ref, d_ref)
    for j in range(4):
        line_ref[j] = xs[j]
    for h in range(lines // SUBS):
        rows = pl.ds(h * SUBS, SUBS)
        agg = agg_ref[rows, :]
        high, lane = agg >> 7, agg & (LANES - 1)
        spread = [
            pick_lines([wide(line_ref[j, pl.ds(r, 1), :]) for r in range(4)], high, lane)
            for j in range(4)
        ]
        for i in range(4):
            placed = w_ref[i, 0, rows, :] * spread[0]
            for j in range(1, 4):
                placed = placed + w_ref[i, j, rows, :] * spread[j]
            x = x1_ref[i, rows, :] + placed
            xo_ref[i, rows, :] = x
            for twice in range(2):
                pad_ref[pl.ds((twice * 4 + i) * lines + h * SUBS, SUBS), :] = x
    out_ref[...] = outgoing(
        lambda r: pad_ref[pl.ds(r, SUBS, stride=lines), :], lines, s_ref[...]
    )


def coarse_tables(group, *refs):
    vo_ref, co_ref, mo_ref, pad_ref = refs[-4:]
    me = refs[0][0]
    for piece, places in zip(refs[1:-5], span_places(group)):
        for t, place in enumerate(places):
            pad_ref[place] = piece[t]
    for h in range(group // SUBS):
        rows = pl.ds(h * SUBS, SUBS)
        for ki in range(NNZ * 4):
            k, i = ki // 4, ki % 4
            for j in range(4):
                tile = pad_ref[rows, ki * 4 + j, :]
                vo_ref[k, i, j, rows, :] = tile
                if k == 0 and i == j:
                    mo_ref[i, rows, :] = 1.0 / tile
        for k in range(NNZ):
            col = pad_ref[rows, NNZ * 16 + k, :].astype(I32)
            co_ref[k, rows, :] = ((col >> 7) ^ me) * LANES + (col & (LANES - 1))


def coarse_solve(group, *refs):
    (v_ref, c_ref, m_ref, x2_ref, w_ref, agg_ref, s_ref, xo_ref, out_ref, b_ref, x_ref, d_ref, pad_ref) = refs[-13:]
    first = [0] + list(range(group - 1, 1, -2))
    for swapped, piece in enumerate(refs[:-13]):
        for t, place in enumerate([m ^ swapped for m in first]):
            for j in range(4):
                b_ref[j, pl.ds(place, 1), :] = piece[t, pl.ds(j, 1), :]
    blocks = group // SUBS
    for j in range(4):
        first = m_ref[j] * b_ref[j]
        x_ref[j] = first
        d_ref[j] = first
    for keep, gain in cheb_factors(KC)[1:]:
        resid = []
        for h in range(blocks):
            rows = pl.ds(h * SUBS, SUBS)
            acc = [b_ref[i, rows, :] for i in range(4)]
            for k in range(NNZ):
                col = c_ref[k, rows, :]
                high, lane = col >> 7, col & (LANES - 1)
                for j in range(4):
                    if k:
                        got = pick_lines(
                            [wide(x_ref[j, pl.ds(r, 1), :]) for r in range(group)], high, lane
                        )
                    else:
                        got = x_ref[j, rows, :]
                    for i in range(4):
                        acc[i] = acc[i] - v_ref[k, i, j, rows, :] * got
            resid.append(acc)
        for h in range(blocks):
            rows = pl.ds(h * SUBS, SUBS)
            for i in range(4):
                d = keep * d_ref[i, rows, :] + gain * (m_ref[i, rows, :] * resid[h][i])
                d_ref[i, rows, :] = d
                x_ref[i, rows, :] = x_ref[i, rows, :] + d
    lane = agg_ref[...]
    spread = [pick(wide(x_ref[j, pl.ds(0, 1), :]), lane) for j in range(4)]
    for i in range(4):
        x = x2_ref[i]
        for j in range(4):
            x = x + w_ref[i, j] * spread[j]
        xo_ref[i] = x
        middle_pad(pad_ref, i, x)
    middle_out(out_ref, pad_ref, s_ref)


def call(body, outs, args, scratch=(), free=(), smem=(), hbm=(), limit=16):
    specs = []
    for index in range(len(args)):
        if index in hbm:
            specs.append(pl.BlockSpec(memory_space=pltpu.HBM))
        elif index in free:
            specs.append(pl.BlockSpec(memory_space=pl.ANY))
        elif index in smem:
            specs.append(pl.BlockSpec(memory_space=pltpu.SMEM))
        else:
            specs.append(pl.BlockSpec(memory_space=pltpu.VMEM))
    single = not isinstance(outs, (list, tuple))
    shapes = [outs] if single else list(outs)
    result = pl.pallas_call(
        body,
        out_shape=shapes,
        in_specs=specs,
        out_specs=[pl.BlockSpec(memory_space=pltpu.VMEM) for _ in shapes],
        scratch_shapes=list(scratch),
        compiler_params=pltpu.CompilerParams(vmem_limit_bytes=limit * 2**20),
    )(*args)
    return result[0] if single else result


def shape(*dims, dtype=F32):
    return jax.ShapeDtypeStruct(dims, dtype)


def vmem(*dims, dtype=F32):
    return pltpu.VMEM(dims, dtype)


def native_rows(x):
    lines = x.shape[-1] // LANES
    split = x.reshape(x.shape[:-1] + (lines, LANES))
    return jnp.swapaxes(split, -2, -3).reshape(-1, LANES)


def from_native(rows, lines):
    return jnp.swapaxes(rows.reshape(lines, 4, LANES), 0, 1).reshape(4, lines * LANES)


def exchange(mesh, out, which):
    slabs, count = mesh.shape["stream"], mesh.shape["span"]

    def swap(partner):
        pairs = []
        for a in range(slabs):
            for b in range(count):
                to_a, to_b = partner(a, b)
                pairs.append((a * count + b, to_a * count + to_b))
        return lax.ppermute(out, AXES, pairs)

    def odd(index):
        return index + 1 if index % 2 else index - 1

    def span_odd(a, b):
        return (a, odd(b)) if 0 <= odd(b) < count else (a ^ 1, b)

    partners = [
        lambda a, b: (odd(a) % slabs, b),
        lambda a, b: (a ^ 1, b),
        span_odd,
        lambda a, b: (a, b ^ 1),
    ]
    return [swap(partner) for partner in partners] + [which]


def halo_choice(a, b, count):
    row, lane = (lax.broadcasted_iota(I32, (SUBS, LANES), d) for d in range(2))
    left = lane < LANES // 2
    index = jnp.where(row < 4, a, b)
    even = left == (index % 2 == 1)
    outside = (row >= 4) & jnp.where(left, b == 0, b == count - 1)
    return jnp.where(outside, 0, jnp.where(even, 1, 2)).astype(I32)


def span_places(group):
    places = [[0]]
    mask = group // 2
    while mask:
        places.append([mask ^ m for piece in places for m in piece])
        mask //= 2
    return places


def span_swap(mesh, value, mask):
    slabs, count = mesh.shape["stream"], mesh.shape["span"]
    pairs = [
        (a * count + b, a * count + (b ^ mask)) for a in range(slabs) for b in range(count)
    ]
    return lax.ppermute(value, AXES, pairs)


def span_stage(mesh, held, out):
    held, _ = lax.optimization_barrier((held, out))
    return span_swap(mesh, held, mesh.shape["span"] // 2 // held.shape[0])


def join_kernel(*refs):
    place = 0
    for piece in refs[:-1]:
        for t in range(piece.shape[0]):
            refs[-1][place] = piece[t]
            place += 1


def join(pieces):
    count = sum(piece.shape[0] for piece in pieces)
    return call(join_kernel, shape(count, *pieces[0].shape[1:]), pieces)


def span_gather(mesh, value):
    masks = range(mesh.shape["span"] - 1, 1, -2)
    held = jnp.stack([value] + [span_swap(mesh, value, m) for m in masks])
    return [held, span_swap(mesh, held, 1)]


def per_device(mesh, right_side, fine_values, fine_columns, fine_sends, fine_order, fine_weights, middle_values, middle_columns, middle_sends, middle_order, middle_weights, coarsest_values, coarsest_columns):
    group = mesh.shape["span"]
    lines = right_side.shape[1] // LANES
    tile = shape(SUBS, LANES)
    vec1 = shape(4, lines, LANES)
    vec2 = shape(4, SUBS, LANES)
    edge = vmem(SUBS, LANES)
    pad1 = vmem(SUBS * lines, LANES)
    pad2 = vmem(SUBS * SUBS, LANES)
    factors = cheb_factors(KSM)
    me = lax.axis_index("span").astype(I32)
    choice = halo_choice(lax.axis_index("stream").astype(I32), me, group)
    values1 = native_rows(fine_values)
    values2 = native_rows(middle_values)

    starts = [
        values1,
        native_rows(right_side),
        fine_sends,
        middle_sends,
        native_columns(fine_columns),
        coarsest_values.reshape(NNZ * 16, LANES),
        coarsest_columns,
    ]
    int_tile = shape(SUBS, LANES, dtype=I32)
    b1, m1, x1, send1, send2, c1, own3, out = call(
        fine_start,
        [
            vec1,
            vec1,
            vec1,
            int_tile,
            int_tile,
            shape(NNZ, lines, LANES, dtype=I32),
            shape(1, NNZ * 17, LANES),
            tile,
        ],
        [pltpu.with_memory_space_constraint(x, pltpu.HBM) for x in starts],
        [pad1, vmem(16 * lines, LANES)]
        + [vmem(*x.shape, dtype=x.dtype) for x in starts[1:]]
        + [pltpu.SemaphoreType.DMA((len(starts),))],
        hbm=range(len(starts)),
    )
    d1 = x1

    arrived = exchange(mesh, out, choice)
    pieces3 = [own3, span_stage(mesh, own3, out)]
    resid, v1 = call(
        fine_first,
        [vec1, shape(NNZ, 4, 4, lines, LANES)],
        [x1, b1, values1, c1],
        [vmem(4, lines, SUBS, LANES)],
    )

    def fine_part(x):
        return call(fine_local, vec1, [x, b1, v1, c1], [vmem(4, lines, SUBS, LANES)])

    def fine_next(which, arrived, resid, x, d, after=()):
        args = arrived + [resid, v1, c1, m1, x, d, send1]
        last = which == KSM - 1
        result = call(
            lambda *refs: fine_step(
                factors[which], last, *(refs[: len(args)] + refs[len(args) + len(after) :])
            ),
            [vec1, tile] + ([] if last else [vec1]),
            args + list(after),
            [edge, pad1],
            free=range(len(args), len(args) + len(after)),
        )
        return result[0], (None if last else result[2]), result[1]

    x1, d1, out = fine_next(1, arrived, resid, x1, d1)

    arrived = exchange(mesh, out, choice)
    resid = fine_part(x1)
    w1, place1, m2 = call(
        fine_tables,
        [
            shape(4, 4, lines, LANES),
            shape(2, SUBS, LANES, dtype=I32),
            vec2,
        ],
        [native_rows(fine_weights), fine_order.reshape(lines, LANES), values2, out],
        free=(3,),
    )
    x1, d1, out = fine_next(2, arrived, resid, x1, d1, [m2])

    arrived = exchange(mesh, out, choice)
    resid = fine_part(x1)
    held3 = join(pieces3)
    b2, x2, out = call(
        lambda *refs: fine_restrict(*(refs[2:4] + refs[:2] + refs[4:12] + refs[13:])),
        [vec2, vec2, tile],
        arrived[2:4] + arrived[:2] + arrived[4:] + [resid, v1, c1, w1, place1, m2, send2, held3],
        [edge, vmem(4, lines, LANES), pad2],
        free=(12,),
    )
    d2 = x2

    def middle_part(x):
        return call(middle_local, vec2, [x, v2, c2])

    def middle_next(which, arrived, x, d, after=()):
        args = arrived + [b2, middle_part(x), m2, x, d, v2, c2, send2]
        last = which == KSM - 1
        result = call(
            lambda *refs: middle_step(
                factors[which], last, *(refs[: len(args)] + refs[len(args) + len(after) :])
            ),
            [vec2, tile] + ([] if last else [vec2]),
            args + list(after),
            [edge, pad2],
            free=range(len(args), len(args) + len(after)),
        )
        return result[0], (None if last else result[2]), result[1]

    arrived = exchange(mesh, out, choice)
    for _ in range(len(span_places(group)) - 4):
        pieces3.append(span_stage(mesh, held3, out))
        held3 = join(pieces3)
    pieces3.append(span_stage(mesh, held3, out))
    v2, c2 = call(
        middle_blocks,
        [shape(NNZ // 2, 4, 4, SUBS, LANES), shape(NNZ // 2, SUBS, LANES, dtype=I32)],
        [values2, native_columns(middle_columns), out],
        free=(2,),
    )
    x2, d2, out = middle_next(1, arrived, x2, d2)

    arrived = exchange(mesh, out, choice)
    w2, agg2, place2 = call(
        middle_tables,
        [
            shape(4, 4, SUBS, LANES),
            shape(SUBS, LANES, dtype=I32),
            shape(SUBS, LANES, dtype=I32),
        ],
        [native_rows(middle_weights), middle_order, middle_order.reshape(-1, LANES), out],
        free=(3,),
    )
    x2, d2, out = middle_next(2, arrived, x2, d2, [agg2])

    arrived = exchange(mesh, out, choice)
    held3 = join(pieces3)
    agg1 = call(fine_inverse, shape(lines, LANES, dtype=I32), [fine_order, out], free=(1,))
    rhs3 = call(
        lambda *refs: middle_restrict(*(refs[:11] + refs[13:])),
        tile,
        arrived + [b2, middle_part(x2), v2, c2, w2, place2, agg1, held3],
        [edge, vmem(4, SUBS, LANES)],
        free=(11, 12),
    )
    pieces3.append(span_stage(mesh, held3, rhs3))
    v3, c3, m3 = call(
        lambda *refs: coarse_tables(group, *refs),
        [shape(NNZ, 4, 4, group, LANES), shape(NNZ, group, LANES, dtype=I32), shape(4, group, LANES)],
        [me.reshape(1)] + pieces3 + [rhs3],
        [vmem(group, NNZ * 17, LANES)],
        free=(1 + len(pieces3),),
        smem=(0,),
    )
    vec3 = vmem(4, group, LANES)
    x2, out = call(
        lambda *refs: coarse_solve(group, *refs),
        [vec2, tile],
        span_gather(mesh, rhs3) + [v3, c3, m3, x2, w2, agg2, send2],
        [vec3, vec3, vec3, pad2],
    )
    arrived = exchange(mesh, out, choice)
    x2, d2, out = middle_next(0, arrived, x2, x2)
    arrived = exchange(mesh, out, choice)
    x2, d2, out = middle_next(1, arrived, x2, d2)
    arrived = exchange(mesh, out, choice)
    x1, out = call(
        lambda *refs: middle_prolong(factors[2], *refs),
        [vec1, tile],
        arrived + [b2, middle_part(x2), m2, x2, d2, v2, c2, x1, w1, agg1, send1],
        [edge, vmem(4, SUBS, LANES), pad1],
    )
    d1 = x1
    for which in range(KSM):
        arrived = exchange(mesh, out, choice)
        resid = fine_part(x1)
        x1, d1, out = fine_next(which, arrived, resid, x1, d1)
    arrived = exchange(mesh, out, choice)
    resid = fine_part(x1)
    rows = shape(4 * lines, LANES)
    solved, left = call(fine_finish, [rows, rows], arrived + [resid, v1, c1, x1], [edge])
    return from_native(solved, lines), from_native(left, lines)


def native_columns(columns):
    lines = columns.shape[1] // LANES
    return jnp.swapaxes(columns.reshape(NNZ, lines, LANES), 0, 1).reshape(-1, LANES)


def solution(mesh):
    both = ("stream", "span")
    in_specs = (
        P(None, both),
        P(None, None, None, both),
        P(None, both),
        P(None, both),
        P(both, None),
        P(None, None, both),
        P(None, None, None, both),
        P(None, both),
        P(None, both),
        P(both, None),
        P(None, None, both),
        P(None, None, None, both),
        P(None, both),
    )
    return jax.shard_map(
        lambda *args: per_device(mesh, *args),
        mesh=mesh,
        in_specs=in_specs,
        out_specs=(P(None, both), P(None, both)),
        check_vma=False,
    )
```

```python
import jax
import jax.numpy as jnp
from jax import lax
from jax.experimental import pallas as pl
from jax.experimental.pallas import tpu as pltpu
from jax.sharding import PartitionSpec as P

KSM = 3
KC = 4
NNZ = 8
LANES = 128
SUBS = 8

CHEB_CENTRE = 1.0
CHEB_RADIUS = 0.9
AXES = ("stream", "span")
F32 = jnp.float32
I32 = jnp.int32


def cheb_factors(degree):
    sigma = CHEB_CENTRE / CHEB_RADIUS
    rho = 1.0 / sigma
    factors = [(0.0, 1.0 / CHEB_CENTRE)]
    for _ in range(degree - 1):
        rho_next = 1.0 / (2.0 * sigma - rho)
        factors.append((rho_next * rho, 2.0 * rho_next / CHEB_RADIUS))
        rho = rho_next
    return factors


def tile_iota(dim):
    return lax.broadcasted_iota(I32, (SUBS, LANES), dim)


def pick(line, lane):
    return jnp.take_along_axis(line, lane, axis=1, mode="promise_in_bounds")


def wide(line):
    return jnp.broadcast_to(line, (SUBS, LANES))


def pick_lines(lines, high, lane, first=0):
    result = jnp.zeros((SUBS, LANES), F32)
    for r, line in enumerate(lines):
        result = jnp.where(high == first + r, pick(line, lane), result)
    return result


def halo_lines(arrivals, edge_ref):
    s_odd, s_even, p_odd, p_even, which = [r[...] for r in arrivals]
    upper = tile_iota(0) < 4
    even = jnp.where(upper, s_even, p_even)
    odd = jnp.where(upper, s_odd, p_odd)
    edge_ref[...] = jnp.where(which == 1, even, jnp.where(which == 2, odd, 0.0))


def edge_lines(arrivals, edge_ref):
    odd, even, which = [r[...] for r in arrivals]
    edge_ref[...] = jnp.where(which == 1, even, jnp.where(which == 2, odd, 0.0))


def outgoing(lines_of, count, sends):
    high, lane = sends >> 7, sends & (LANES - 1)
    return pick_lines([lines_of(r) for r in range(count)], high, lane)


def send_table(s_ref):
    stream = jnp.concatenate([s_ref[pl.ds(1, 1), :], s_ref[pl.ds(0, 1), :]], axis=1)
    span = jnp.concatenate([s_ref[pl.ds(3, 1), :], s_ref[pl.ds(2, 1), :]], axis=1)
    return jnp.where(tile_iota(0) < 4, stream, span)


def duplicate(x):
    return x + pltpu.roll(x, 4, 0)


def fine_start(*refs):
    sources = refs[:7]
    (bo_ref, mo_ref, x_ref, so_ref, s2o_ref, co_ref, o3_ref, out_ref, pad_ref) = refs[7:16]
    held, sems = refs[16:23], refs[23]
    copies = [
        pltpu.make_async_copy(source.at[pl.ds(0, there.shape[0]), :], there, sems.at[t])
        for t, (source, there) in enumerate(zip(sources, held))
    ]
    for copy in copies:
        copy.start()
    for copy in copies:
        copy.wait()
    v_ref, b_ref, s_ref, s2_ref, c_ref, v3_ref, c3_ref = held
    sends = send_table(s_ref)
    so_ref[...] = sends
    s2o_ref[...] = send_table(s2_ref)
    count = v3_ref.shape[0]
    o3_ref[0, pl.ds(0, count), :] = v3_ref[...]
    o3_ref[0, pl.ds(count, NNZ), :] = c3_ref[...].astype(F32)
    for k in range(NNZ):
        for h in range(co_ref.shape[1] // SUBS):
            co_ref[k, pl.ds(h * SUBS, SUBS), :] = c_ref[
                pl.ds(h * SUBS * NNZ + k, SUBS, stride=NNZ), :
            ]
    lines = bo_ref.shape[1]
    for i in range(4):
        for h in range(lines // SUBS):
            rows = pl.ds(h * SUBS, SUBS)
            native = pl.ds(h * SUBS * 4 + i, SUBS, stride=4)
            b = b_ref[native, :]
            m = 1.0 / v_ref[pl.ds((i * lines + h * SUBS) * 4 + i, SUBS, stride=4), :]
            x = m * b
            bo_ref[i, rows, :] = b
            mo_ref[i, rows, :] = m
            x_ref[i, rows, :] = x
            for twice in range(2):
                pad_ref[pl.ds((twice * 4 + i) * lines + h * SUBS, SUBS), :] = x
    out_ref[...] = outgoing(
        lambda r: pad_ref[pl.ds(r, SUBS, stride=lines), :], lines, sends
    )


def fine_first(x_ref, b_ref, v_ref, c_ref, r_ref, vo_ref, line_ref):
    lines = x_ref.shape[1]

    def values(k, i, j, h):
        start = ((k * 4 + i) * lines + h * SUBS) * 4 + j
        tile = v_ref[pl.ds(start, SUBS, stride=4), :]
        vo_ref[k, i, j, pl.ds(h * SUBS, SUBS), :] = tile
        return tile

    fine_product(values, x_ref, b_ref, c_ref, r_ref, line_ref)


def fine_local(x_ref, b_ref, v_ref, c_ref, r_ref, line_ref):
    def values(k, i, j, h):
        return v_ref[k, i, j, pl.ds(h * SUBS, SUBS), :]

    fine_product(values, x_ref, b_ref, c_ref, r_ref, line_ref)


def fine_product(values, x_ref, b_ref, c_ref, r_ref, line_ref):
    lines = x_ref.shape[1]
    halves = lines // SUBS
    for j in range(4):
        for r in range(lines):
            line_ref[j, r] = wide(x_ref[j, pl.ds(r, 1), :])
    acc = []
    for h in range(halves):
        rows = pl.ds(h * SUBS, SUBS)
        for i in range(4):
            total = b_ref[i, rows, :]
            for j in range(4):
                total = total - values(0, i, j, h) * x_ref[j, rows, :]
            acc.append(total)

    def body(k, acc):
        acc = list(acc)
        for h in range(halves):
            rows = pl.ds(h * SUBS, SUBS)
            col = c_ref[k, rows, :]
            high, lane = col >> 7, col & (LANES - 1)
            for j in range(4):
                got = pick_lines([line_ref[j, r] for r in range(lines)], high, lane)
                for i in range(4):
                    acc[4 * h + i] = acc[4 * h + i] - values(k, i, j, h) * got
        return tuple(acc)

    acc = lax.fori_loop(1, NNZ, body, tuple(acc))
    for h in range(halves):
        for i in range(4):
            r_ref[i, pl.ds(h * SUBS, SUBS), :] = acc[4 * h + i]


def fine_remote(arrivals, r_ref, v_ref, c_ref, edge_ref, axis):
    lines = r_ref.shape[1]
    halves = lines // SUBS
    edge_lines(arrivals, edge_ref)
    edges = [wide(edge_ref[pl.ds(4 * axis + j, 1), :]) for j in range(4)]
    result = []
    for h in range(halves):
        rows = pl.ds(h * SUBS, SUBS)
        acc = [r_ref[i, rows, :] for i in range(4)]
        for k in range(1, NNZ):
            col = c_ref[k, rows, :]
            here, lane = (col >> 7) == lines + axis, col & (LANES - 1)
            for j in range(4):
                got = jnp.where(here, pick(edges[j], lane), 0.0)
                for i in range(4):
                    acc[i] = acc[i] - v_ref[k, i, j, rows, :] * got
        result.append(acc)
    return result


def fine_stream(*refs):
    r_ref, v_ref, c_ref, ro_ref, edge_ref = refs[3:]
    resid = fine_remote(refs[:3], r_ref, v_ref, c_ref, edge_ref, 0)
    for h, acc in enumerate(resid):
        for i in range(4):
            ro_ref[i, pl.ds(h * SUBS, SUBS), :] = acc[i]


def fine_step(factors, last, *refs):
    arrivals = refs[:3]
    r_ref, v_ref, c_ref, m_ref, x_ref, d_ref, s_ref, xo_ref, out_ref = refs[3:12]
    do_ref = refs[12] if last is False else None
    edge_ref, pad_ref = refs[-2:]
    keep, gain = factors
    lines = r_ref.shape[1]
    resid = fine_remote(arrivals, r_ref, v_ref, c_ref, edge_ref, 1)
    for h in range(lines // SUBS):
        rows = pl.ds(h * SUBS, SUBS)
        for i in range(4):
            d = gain * (m_ref[i, rows, :] * resid[h][i])
            if keep:
                d = keep * d_ref[i, rows, :] + d
            x = x_ref[i, rows, :] + d
            if not last:
                do_ref[i, rows, :] = d
            xo_ref[i, rows, :] = x
            for twice in range(2):
                pad_ref[pl.ds((twice * 4 + i) * lines + h * SUBS, SUBS), :] = x
    out_ref[...] = outgoing(
        lambda r: pad_ref[pl.ds(r, SUBS, stride=lines), :], lines, s_ref[...]
    )


def fine_finish(*refs):
    arrivals = refs[:3]
    r_ref, v_ref, c_ref, x_ref, so_ref, ro_ref, edge_ref = refs[3:]
    lines = r_ref.shape[1]
    resid = fine_remote(arrivals, r_ref, v_ref, c_ref, edge_ref, 1)
    for h in range(lines // SUBS):
        for i in range(4):
            native = pl.ds(h * SUBS * 4 + i, SUBS, stride=4)
            so_ref[native, :] = x_ref[i, pl.ds(h * SUBS, SUBS), :]
            ro_ref[native, :] = resid[h][i]


def fine_restrict(*refs):
    arrivals = refs[:3]
    (r_ref, v_ref, c_ref, w_ref, p_ref, m2_ref, s2_ref, b2_ref, x2_ref, out_ref, edge_ref, line_ref, pad_ref) = refs[3:]
    lines = r_ref.shape[1]
    resid = fine_remote(arrivals, r_ref, v_ref, c_ref, edge_ref, 1)
    for h in range(lines // SUBS):
        rows = pl.ds(h * SUBS, SUBS)
        for j in range(4):
            total = w_ref[0, j, rows, :] * resid[h][0]
            for i in range(1, 4):
                total = total + w_ref[i, j, rows, :] * resid[h][i]
            line_ref[j, rows, :] = total
    for j in range(4):
        total = None
        source = [wide(line_ref[j, pl.ds(r, 1), :]) for r in range(lines)]
        for part in range(2):
            place = p_ref[part]
            got = pick_lines(source, place >> 7, place & (LANES - 1))
            total = got if total is None else total + got
        b2 = duplicate(total)
        x2 = m2_ref[j] * b2
        b2_ref[j] = b2
        x2_ref[j] = x2
        middle_pad(pad_ref, j, x2)
    middle_out(out_ref, pad_ref, s2_ref)


def inverse_order(o_row, lines):
    count = lines * LANES
    high, lane = o_row >> 7, o_row & (LANES - 1)
    coarse = lax.broadcasted_iota(I32, (1, count), 1) >> 2
    here = lax.broadcasted_iota(I32, (lines, count), 0) == high
    upper = jnp.where(here, (coarse >> 4).astype(F32), 0.0)
    lower = jnp.where(here, (coarse & 15).astype(F32), 0.0)
    left = jnp.concatenate([upper, lower], axis=0).astype(jnp.bfloat16)
    right = jnp.where(
        lax.broadcasted_iota(I32, (LANES, count), 0) == lane, 1.0, 0.0
    ).astype(jnp.bfloat16)
    found = lax.dot_general(
        left, right, (((1,), (1,)), ((), ())), preferred_element_type=F32
    )
    return (found[:lines] * 16.0 + found[lines:]).astype(I32)


def pick_order(sources, unit):
    lane = tile_iota(1)
    place = 4 * (lane & 31) + unit
    result = jnp.zeros((SUBS, LANES), I32)
    for q, source in enumerate(sources):
        result = jnp.where((lane >> 5) == q, pick(source, place), result)
    return result


def fine_tables(w_ref, o_ref, v2_ref, _, wo_ref, place_ref, m2_ref):
    lines = o_ref.shape[0]
    for i in range(4):
        for j in range(4):
            for h in range(lines // SUBS):
                start = (i * lines + h * SUBS) * 4 + j
                wo_ref[i, j, pl.ds(h * SUBS, SUBS), :] = w_ref[pl.ds(start, SUBS, stride=4), :]
    sources = []
    for q in range(4):
        four = o_ref[pl.ds(q, 4, stride=4), :]
        sources.append(jnp.concatenate([four, four], axis=0))
    for part in range(2):
        place_ref[part] = pick_order(sources, (tile_iota(0) >> 2) + 2 * part)
    for i in range(4):
        four = 1.0 / v2_ref[pl.ds(i * 16 + i, 4, stride=4), :]
        m2_ref[i, pl.ds(0, 4), :] = four
        m2_ref[i, pl.ds(4, 4), :] = four


def fine_inverse(row_ref, _, agg_ref):
    agg_ref[...] = inverse_order(row_ref[...], agg_ref.shape[0])


def middle_blocks(v_ref, c_ref, _, vo_ref, co_ref):
    def body(ki, carry):
        k, i = ki // 4, ki % 4
        for j in range(4):
            for odd in range(2):
                start = ((2 * k + odd) * 4 + i) * 16 + j
                vo_ref[k, i, j, pl.ds(4 * odd, 4), :] = v_ref[pl.ds(start, 4, stride=4), :]
        return carry

    lax.fori_loop(0, NNZ // 2 * 4, body, 0)
    for k in range(NNZ // 2):
        for odd in range(2):
            co_ref[k, pl.ds(4 * odd, 4), :] = c_ref[pl.ds(2 * k + odd, 4, stride=NNZ), :]


def middle_tables(w_ref, row_ref, o_ref, _, wo_ref, agg_ref, place_ref):
    lines = o_ref.shape[0]
    for i in range(4):
        for j in range(4):
            four = w_ref[pl.ds(i * lines * 4 + j, 4, stride=4), :]
            wo_ref[i, j, pl.ds(0, 4), :] = four
            wo_ref[i, j, pl.ds(4, 4), :] = four
    agg = inverse_order(row_ref[...], lines)
    agg_ref[...] = jnp.concatenate([agg, agg], axis=0)
    sources = [wide(o_ref[pl.ds(q, 1), :]) for q in range(4)]
    place_ref[...] = pick_order(sources, tile_iota(0) & 3)


def middle_pad(pad_ref, j, x):
    for twice in range(2):
        pad_ref[pl.ds((twice * 4 + j) * SUBS, SUBS), :] = x


def middle_out(out_ref, pad_ref, s_ref):
    out_ref[...] = outgoing(
        lambda r: pad_ref[pl.ds(r, SUBS, stride=SUBS), :], 4, s_ref[...]
    )


def middle_local(x_ref, v_ref, c_ref, a_ref):
    acc = [jnp.zeros((SUBS, LANES), F32) for _ in range(4)]
    for j in range(4):
        source = [wide(x_ref[j, pl.ds(r, 1), :]) for r in range(4)]
        for kp in range(NNZ // 2):
            col = c_ref[kp]
            got = pick_lines(source, col >> 7, col & (LANES - 1))
            for i in range(4):
                acc[i] = acc[i] + v_ref[kp, i, j] * got
    for i in range(4):
        a_ref[i] = acc[i]


def middle_residual(arrivals, b_ref, a_ref, v_ref, c_ref, edge_ref):
    halo_lines(arrivals, edge_ref)
    acc = [a_ref[i] for i in range(4)]
    for j in range(4):
        source = [wide(edge_ref[pl.ds(4 * e + j, 1), :]) for e in range(2)]
        for kp in range(NNZ // 2):
            col = c_ref[kp]
            got = pick_lines(source, col >> 7, col & (LANES - 1), 4)
            for i in range(4):
                acc[i] = acc[i] + v_ref[kp, i, j] * got
    return [b_ref[i] - duplicate(acc[i]) for i in range(4)]


def middle_update(factors, resid, m_ref, x_ref, d_ref):
    keep, gain = factors
    xs, ds = [], []
    for i in range(4):
        d = gain * (m_ref[i] * resid[i])
        if keep:
            d = keep * d_ref[i] + d
        ds.append(d)
        xs.append(x_ref[i] + d)
    return xs, ds


def middle_step(factors, last, *refs):
    arrivals = refs[:5]
    b_ref, a_ref, m_ref, x_ref, d_ref, v_ref, c_ref, s_ref, xo_ref, out_ref = refs[5:15]
    do_ref = refs[15] if last is False else None
    edge_ref, pad_ref = refs[-2:]
    resid = middle_residual(arrivals, b_ref, a_ref, v_ref, c_ref, edge_ref)
    xs, ds = middle_update(factors, resid, m_ref, x_ref, d_ref)
    for i in range(4):
        xo_ref[i] = xs[i]
        if not last:
            do_ref[i] = ds[i]
        middle_pad(pad_ref, i, xs[i])
    middle_out(out_ref, pad_ref, s_ref)


def middle_restrict(*refs):
    arrivals = refs[:5]
    b_ref, a_ref, v_ref, c_ref, w_ref, p_ref, out_ref, edge_ref, line_ref = refs[5:]
    resid = middle_residual(arrivals, b_ref, a_ref, v_ref, c_ref, edge_ref)
    place = p_ref[...]
    high, lane = place >> 7, place & (LANES - 1)
    for j in range(4):
        total = w_ref[0, j] * resid[0]
        for i in range(1, 4):
            total = total + w_ref[i, j] * resid[i]
        line_ref[j] = total
        source = [wide(line_ref[j, pl.ds(r, 1), :]) for r in range(4)]
        got = pick_lines(source, high, lane)
        got = got + pltpu.roll(got, 2, 0)
        got = got + pltpu.roll(got, 1, 0)
        out_ref[pl.ds(j, 1), :] = got[0:1]
        out_ref[pl.ds(4 + j, 1), :] = got[0:1]


def middle_prolong(factors, *refs):
    arrivals = refs[:5]
    (b_ref, a_ref, m_ref, x_ref, d_ref, v_ref, c_ref, x1_ref, w_ref, agg_ref, s_ref, xo_ref, out_ref, edge_ref, line_ref, pad_ref) = refs[5:]
    lines = x1_ref.shape[1]
    resid = middle_residual(arrivals, b_ref, a_ref, v_ref, c_ref, edge_ref)
    xs, _ = middle_update(factors, resid, m_ref, x_ref, d_ref)
    for j in range(4):
        line_ref[j] = xs[j]
    for h in range(lines // SUBS):
        rows = pl.ds(h * SUBS, SUBS)
        agg = agg_ref[rows, :]
        high, lane = agg >> 7, agg & (LANES - 1)
        spread = [
            pick_lines([wide(line_ref[j, pl.ds(r, 1), :]) for r in range(4)], high, lane)
            for j in range(4)
        ]
        for i in range(4):
            placed = w_ref[i, 0, rows, :] * spread[0]
            for j in range(1, 4):
                placed = placed + w_ref[i, j, rows, :] * spread[j]
            x = x1_ref[i, rows, :] + placed
            xo_ref[i, rows, :] = x
            for twice in range(2):
                pad_ref[pl.ds((twice * 4 + i) * lines + h * SUBS, SUBS), :] = x
    out_ref[...] = outgoing(
        lambda r: pad_ref[pl.ds(r, SUBS, stride=lines), :], lines, s_ref[...]
    )


def coarse_tables(group, *refs):
    vo_ref, co_ref, mo_ref, pad_ref = refs[-4:]
    me = refs[0][0]
    for piece, places in zip(refs[1:-5], span_places(group)):
        for t, place in enumerate(places):
            pad_ref[place] = piece[t]
    for h in range(group // SUBS):
        rows = pl.ds(h * SUBS, SUBS)
        for ki in range(NNZ * 4):
            k, i = ki // 4, ki % 4
            for j in range(4):
                tile = pad_ref[rows, ki * 4 + j, :]
                vo_ref[k, i, j, rows, :] = tile
                if k == 0 and i == j:
                    mo_ref[i, rows, :] = 1.0 / tile
        for k in range(NNZ):
            col = pad_ref[rows, NNZ * 16 + k, :].astype(I32)
            co_ref[k, rows, :] = ((col >> 7) ^ me) * LANES + (col & (LANES - 1))


def coarse_solve(group, *refs):
    (v_ref, c_ref, m_ref, x2_ref, w_ref, agg_ref, s_ref, xo_ref, out_ref, b_ref, x_ref, d_ref, pad_ref) = refs[-13:]
    first = [0] + list(range(group - 1, 1, -2))
    for swapped, piece in enumerate(refs[:-13]):
        for t, place in enumerate([m ^ swapped for m in first]):
            for j in range(4):
                b_ref[j, pl.ds(place, 1), :] = piece[t, pl.ds(j, 1), :]
    blocks = group // SUBS
    for j in range(4):
        first = m_ref[j] * b_ref[j]
        x_ref[j] = first
        d_ref[j] = first
    for keep, gain in cheb_factors(KC)[1:]:
        resid = []
        for h in range(blocks):
            rows = pl.ds(h * SUBS, SUBS)
            acc = [b_ref[i, rows, :] for i in range(4)]
            for k in range(NNZ):
                col = c_ref[k, rows, :]
                high, lane = col >> 7, col & (LANES - 1)
                for j in range(4):
                    if k:
                        got = pick_lines(
                            [wide(x_ref[j, pl.ds(r, 1), :]) for r in range(group)], high, lane
                        )
                    else:
                        got = x_ref[j, rows, :]
                    for i in range(4):
                        acc[i] = acc[i] - v_ref[k, i, j, rows, :] * got
            resid.append(acc)
        for h in range(blocks):
            rows = pl.ds(h * SUBS, SUBS)
            for i in range(4):
                d = keep * d_ref[i, rows, :] + gain * (m_ref[i, rows, :] * resid[h][i])
                d_ref[i, rows, :] = d
                x_ref[i, rows, :] = x_ref[i, rows, :] + d
    lane = agg_ref[...]
    spread = [pick(wide(x_ref[j, pl.ds(0, 1), :]), lane) for j in range(4)]
    for i in range(4):
        x = x2_ref[i]
        for j in range(4):
            x = x + w_ref[i, j] * spread[j]
        xo_ref[i] = x
        middle_pad(pad_ref, i, x)
    middle_out(out_ref, pad_ref, s_ref)


def call(body, outs, args, scratch=(), free=(), smem=(), hbm=(), limit=16):
    specs = []
    for index in range(len(args)):
        if index in hbm:
            specs.append(pl.BlockSpec(memory_space=pltpu.HBM))
        elif index in free:
            specs.append(pl.BlockSpec(memory_space=pl.ANY))
        elif index in smem:
            specs.append(pl.BlockSpec(memory_space=pltpu.SMEM))
        else:
            specs.append(pl.BlockSpec(memory_space=pltpu.VMEM))
    single = not isinstance(outs, (list, tuple))
    shapes = [outs] if single else list(outs)
    result = pl.pallas_call(
        body,
        out_shape=shapes,
        in_specs=specs,
        out_specs=[pl.BlockSpec(memory_space=pltpu.VMEM) for _ in shapes],
        scratch_shapes=list(scratch),
        compiler_params=pltpu.CompilerParams(vmem_limit_bytes=limit * 2**20),
    )(*args)
    return result[0] if single else result


def shape(*dims, dtype=F32):
    return jax.ShapeDtypeStruct(dims, dtype)


def vmem(*dims, dtype=F32):
    return pltpu.VMEM(dims, dtype)


def native_rows(x):
    lines = x.shape[-1] // LANES
    split = x.reshape(x.shape[:-1] + (lines, LANES))
    return jnp.swapaxes(split, -2, -3).reshape(-1, LANES)


def from_native(rows, lines):
    return jnp.swapaxes(rows.reshape(lines, 4, LANES), 0, 1).reshape(4, lines * LANES)


def exchange(mesh, out, which):
    slabs, count = mesh.shape["stream"], mesh.shape["span"]

    def swap(partner):
        pairs = []
        for a in range(slabs):
            for b in range(count):
                to_a, to_b = partner(a, b)
                pairs.append((a * count + b, to_a * count + to_b))
        return lax.ppermute(out, AXES, pairs)

    def odd(index):
        return index + 1 if index % 2 else index - 1

    def span_odd(a, b):
        return (a, odd(b)) if 0 <= odd(b) < count else (a ^ 1, b)

    partners = [
        lambda a, b: (odd(a) % slabs, b),
        lambda a, b: (a ^ 1, b),
        span_odd,
        lambda a, b: (a, b ^ 1),
    ]
    return [swap(partner) for partner in partners] + [which]


def halo_choice(a, b, count):
    row, lane = (lax.broadcasted_iota(I32, (SUBS, LANES), d) for d in range(2))
    left = lane < LANES // 2
    index = jnp.where(row < 4, a, b)
    even = left == (index % 2 == 1)
    outside = (row >= 4) & jnp.where(left, b == 0, b == count - 1)
    return jnp.where(outside, 0, jnp.where(even, 1, 2)).astype(I32)


def span_places(group):
    places = [[0]]
    mask = group // 2
    while mask:
        places.append([(mask | 1) ^ m for piece in places for m in piece])
        mask //= 2
    return places


def span_swap(mesh, value, mask):
    slabs, count = mesh.shape["stream"], mesh.shape["span"]
    pairs = [
        (a * count + b, a * count + (b ^ mask)) for a in range(slabs) for b in range(count)
    ]
    return lax.ppermute(value, AXES, pairs)


def span_stage(mesh, held, out):
    held, _ = lax.optimization_barrier((held, out))
    return span_swap(mesh, held, mesh.shape["span"] // 2 // held.shape[0] | 1)


def join_kernel(*refs):
    place = 0
    for piece in refs[:-1]:
        for t in range(piece.shape[0]):
            refs[-1][place] = piece[t]
            place += 1


def join(pieces):
    count = sum(piece.shape[0] for piece in pieces)
    return call(join_kernel, shape(count, *pieces[0].shape[1:]), pieces)


def span_gather(mesh, value):
    masks = range(mesh.shape["span"] - 1, 1, -2)
    held = jnp.stack([value] + [span_swap(mesh, value, m) for m in masks])
    return [held, span_swap(mesh, held, 1)]


def per_device(mesh, right_side, fine_values, fine_columns, fine_sends, fine_order, fine_weights, middle_values, middle_columns, middle_sends, middle_order, middle_weights, coarsest_values, coarsest_columns):
    group = mesh.shape["span"]
    lines = right_side.shape[1] // LANES
    tile = shape(SUBS, LANES)
    vec1 = shape(4, lines, LANES)
    vec2 = shape(4, SUBS, LANES)
    edge = vmem(SUBS, LANES)
    pad1 = vmem(SUBS * lines, LANES)
    pad2 = vmem(SUBS * SUBS, LANES)
    factors = cheb_factors(KSM)
    me = lax.axis_index("span").astype(I32)
    choice = halo_choice(lax.axis_index("stream").astype(I32), me, group)
    values1 = native_rows(fine_values)
    values2 = native_rows(middle_values)

    starts = [
        values1,
        native_rows(right_side),
        fine_sends,
        middle_sends,
        native_columns(fine_columns),
        coarsest_values.reshape(NNZ * 16, LANES),
        coarsest_columns,
    ]
    int_tile = shape(SUBS, LANES, dtype=I32)
    b1, m1, x1, send1, send2, c1, own3, out = call(
        fine_start,
        [
            vec1,
            vec1,
            vec1,
            int_tile,
            int_tile,
            shape(NNZ, lines, LANES, dtype=I32),
            shape(1, NNZ * 17, LANES),
            tile,
        ],
        [pltpu.with_memory_space_constraint(x, pltpu.HBM) for x in starts],
        [pad1, vmem(16 * lines, LANES)]
        + [vmem(*x.shape, dtype=x.dtype) for x in starts[1:]]
        + [pltpu.SemaphoreType.DMA((len(starts),))],
        hbm=range(len(starts)),
    )
    d1 = x1

    arrived = exchange(mesh, out, choice)
    pieces3 = [own3, span_stage(mesh, own3, out)]
    resid, v1 = call(
        fine_first,
        [vec1, shape(NNZ, 4, 4, lines, LANES)],
        [x1, b1, values1, c1],
        [vmem(4, lines, SUBS, LANES)],
    )

    def fine_part(x):
        return call(fine_local, vec1, [x, b1, v1, c1], [vmem(4, lines, SUBS, LANES)])

    def fine_half(arrived, resid):
        return call(fine_stream, vec1, arrived[:2] + arrived[4:] + [resid, v1, c1], [edge])

    def fine_next(which, arrived, resid, x, d, after=()):
        args = arrived[2:] + [fine_half(arrived, resid), v1, c1, m1, x, d, send1]
        last = which == KSM - 1
        result = call(
            lambda *refs: fine_step(
                factors[which], last, *(refs[: len(args)] + refs[len(args) + len(after) :])
            ),
            [vec1, tile] + ([] if last else [vec1]),
            args + list(after),
            [edge, pad1],
            free=range(len(args), len(args) + len(after)),
        )
        return result[0], (None if last else result[2]), result[1]

    x1, d1, out = fine_next(1, arrived, resid, x1, d1)

    arrived = exchange(mesh, out, choice)
    resid = fine_part(x1)
    w1, place1, m2 = call(
        fine_tables,
        [
            shape(4, 4, lines, LANES),
            shape(2, SUBS, LANES, dtype=I32),
            vec2,
        ],
        [native_rows(fine_weights), fine_order.reshape(lines, LANES), values2, out],
        free=(3,),
    )
    x1, d1, out = fine_next(2, arrived, resid, x1, d1, [m2])

    arrived = exchange(mesh, out, choice)
    resid = fine_part(x1)
    held3 = join(pieces3)
    b2, x2, out = call(
        lambda *refs: fine_restrict(*(refs[:10] + refs[11:])),
        [vec2, vec2, tile],
        arrived[2:] + [fine_half(arrived, resid), v1, c1, w1, place1, m2, send2, held3],
        [edge, vmem(4, lines, LANES), pad2],
        free=(10,),
    )
    d2 = x2

    def middle_part(x):
        return call(middle_local, vec2, [x, v2, c2])

    def middle_next(which, arrived, x, d, after=()):
        args = arrived + [b2, middle_part(x), m2, x, d, v2, c2, send2]
        last = which == KSM - 1
        result = call(
            lambda *refs: middle_step(
                factors[which], last, *(refs[: len(args)] + refs[len(args) + len(after) :])
            ),
            [vec2, tile] + ([] if last else [vec2]),
            args + list(after),
            [edge, pad2],
            free=range(len(args), len(args) + len(after)),
        )
        return result[0], (None if last else result[2]), result[1]

    arrived = exchange(mesh, out, choice)
    for _ in range(len(span_places(group)) - 4):
        pieces3.append(span_stage(mesh, held3, out))
        held3 = join(pieces3)
    pieces3.append(span_stage(mesh, held3, out))
    v2, c2 = call(
        middle_blocks,
        [shape(NNZ // 2, 4, 4, SUBS, LANES), shape(NNZ // 2, SUBS, LANES, dtype=I32)],
        [values2, native_columns(middle_columns), out],
        free=(2,),
    )
    x2, d2, out = middle_next(1, arrived, x2, d2)

    arrived = exchange(mesh, out, choice)
    w2, agg2, place2 = call(
        middle_tables,
        [
            shape(4, 4, SUBS, LANES),
            shape(SUBS, LANES, dtype=I32),
            shape(SUBS, LANES, dtype=I32),
        ],
        [native_rows(middle_weights), middle_order, middle_order.reshape(-1, LANES), out],
        free=(3,),
    )
    x2, d2, out = middle_next(2, arrived, x2, d2, [agg2])

    arrived = exchange(mesh, out, choice)
    held3 = join(pieces3)
    agg1 = call(fine_inverse, shape(lines, LANES, dtype=I32), [fine_order, out], free=(1,))
    rhs3 = call(
        lambda *refs: middle_restrict(*(refs[:11] + refs[13:])),
        tile,
        arrived + [b2, middle_part(x2), v2, c2, w2, place2, agg1, held3],
        [edge, vmem(4, SUBS, LANES)],
        free=(11, 12),
    )
    pieces3.append(span_stage(mesh, held3, rhs3))
    v3, c3, m3 = call(
        lambda *refs: coarse_tables(group, *refs),
        [shape(NNZ, 4, 4, group, LANES), shape(NNZ, group, LANES, dtype=I32), shape(4, group, LANES)],
        [me.reshape(1)] + pieces3 + [rhs3],
        [vmem(group, NNZ * 17, LANES)],
        free=(1 + len(pieces3),),
        smem=(0,),
    )
    vec3 = vmem(4, group, LANES)
    x2, out = call(
        lambda *refs: coarse_solve(group, *refs),
        [vec2, tile],
        span_gather(mesh, rhs3) + [v3, c3, m3, x2, w2, agg2, send2],
        [vec3, vec3, vec3, pad2],
    )
    arrived = exchange(mesh, out, choice)
    x2, d2, out = middle_next(0, arrived, x2, x2)
    arrived = exchange(mesh, out, choice)
    x2, d2, out = middle_next(1, arrived, x2, d2)
    arrived = exchange(mesh, out, choice)
    x1, out = call(
        lambda *refs: middle_prolong(factors[2], *refs),
        [vec1, tile],
        arrived + [b2, middle_part(x2), m2, x2, d2, v2, c2, x1, w1, agg1, send1],
        [edge, vmem(4, SUBS, LANES), pad1],
    )
    d1 = x1
    for which in range(KSM):
        arrived = exchange(mesh, out, choice)
        resid = fine_part(x1)
        x1, d1, out = fine_next(which, arrived, resid, x1, d1)
    arrived = exchange(mesh, out, choice)
    resid = fine_part(x1)
    rows = shape(4 * lines, LANES)
    resid = fine_half(arrived, resid)
    solved, left = call(fine_finish, [rows, rows], arrived[2:] + [resid, v1, c1, x1], [edge])
    return from_native(solved, lines), from_native(left, lines)


def native_columns(columns):
    lines = columns.shape[1] // LANES
    return jnp.swapaxes(columns.reshape(NNZ, lines, LANES), 0, 1).reshape(-1, LANES)


def solution(mesh):
    both = ("stream", "span")
    in_specs = (
        P(None, both),
        P(None, None, None, both),
        P(None, both),
        P(None, both),
        P(both, None),
        P(None, None, both),
        P(None, None, None, both),
        P(None, both),
        P(None, both),
        P(both, None),
        P(None, None, both),
        P(None, None, None, both),
        P(None, both),
    )
    return jax.shard_map(
        lambda *args: per_device(mesh, *args),
        mesh=mesh,
        in_specs=in_specs,
        out_specs=(P(None, both), P(None, both)),
        check_vma=False,
    )
```

```python
import jax
import jax.numpy as jnp
from jax import lax
from jax.experimental import pallas as pl
from jax.experimental.pallas import tpu as pltpu
from jax.sharding import PartitionSpec as P

KSM = 3
KC = 4
NNZ = 8
LANES = 128
SUBS = 8

CHEB_CENTRE = 1.0
CHEB_RADIUS = 0.9
AXES = ("stream", "span")
F32 = jnp.float32
I32 = jnp.int32


def cheb_factors(degree):
    sigma = CHEB_CENTRE / CHEB_RADIUS
    rho = 1.0 / sigma
    factors = [(0.0, 1.0 / CHEB_CENTRE)]
    for _ in range(degree - 1):
        rho_next = 1.0 / (2.0 * sigma - rho)
        factors.append((rho_next * rho, 2.0 * rho_next / CHEB_RADIUS))
        rho = rho_next
    return factors


def tile_iota(dim):
    return lax.broadcasted_iota(I32, (SUBS, LANES), dim)


def pick(line, lane):
    return jnp.take_along_axis(line, lane, axis=1, mode="promise_in_bounds")


def wide(line):
    return jnp.broadcast_to(line, (SUBS, LANES))


def pick_lines(lines, high, lane, first=0):
    result = jnp.zeros((SUBS, LANES), F32)
    for r, line in enumerate(lines):
        result = jnp.where(high == first + r, pick(line, lane), result)
    return result


def halo_lines(arrivals, edge_ref):
    s_odd, s_even, p_odd, p_even, which = [r[...] for r in arrivals]
    upper = tile_iota(0) < 4
    even = jnp.where(upper, s_even, p_even)
    odd = jnp.where(upper, s_odd, p_odd)
    edge_ref[...] = jnp.where(which == 1, even, jnp.where(which == 2, odd, 0.0))


def edge_lines(arrivals, edge_ref):
    odd, even, which = [r[...] for r in arrivals]
    edge_ref[...] = jnp.where(which == 1, even, jnp.where(which == 2, odd, 0.0))


def outgoing(lines_of, count, sends):
    high, lane = sends >> 7, sends & (LANES - 1)
    return pick_lines([lines_of(r) for r in range(count)], high, lane)


def send_table(s_ref):
    stream = jnp.concatenate([s_ref[pl.ds(1, 1), :], s_ref[pl.ds(0, 1), :]], axis=1)
    span = jnp.concatenate([s_ref[pl.ds(3, 1), :], s_ref[pl.ds(2, 1), :]], axis=1)
    return jnp.where(tile_iota(0) < 4, stream, span)


def duplicate(x):
    return x + pltpu.roll(x, 4, 0)


def fine_start(*refs):
    sources = refs[:7]
    (bo_ref, mo_ref, x_ref, so_ref, s2o_ref, co_ref, o3_ref, out_ref, pad_ref) = refs[7:16]
    held, sems = refs[16:23], refs[23]
    copies = [
        pltpu.make_async_copy(source.at[pl.ds(0, there.shape[0]), :], there, sems.at[t])
        for t, (source, there) in enumerate(zip(sources, held))
    ]
    for copy in copies:
        copy.start()
    for copy in copies:
        copy.wait()
    v_ref, b_ref, s_ref, s2_ref, c_ref, v3_ref, c3_ref = held
    sends = send_table(s_ref)
    so_ref[...] = sends
    s2o_ref[...] = send_table(s2_ref)
    count = v3_ref.shape[0]
    o3_ref[0, pl.ds(0, count), :] = v3_ref[...]
    o3_ref[0, pl.ds(count, NNZ), :] = c3_ref[...].astype(F32)
    for k in range(NNZ):
        for h in range(co_ref.shape[1] // SUBS):
            co_ref[k, pl.ds(h * SUBS, SUBS), :] = c_ref[
                pl.ds(h * SUBS * NNZ + k, SUBS, stride=NNZ), :
            ]
    lines = bo_ref.shape[1]
    for i in range(4):
        for h in range(lines // SUBS):
            rows = pl.ds(h * SUBS, SUBS)
            native = pl.ds(h * SUBS * 4 + i, SUBS, stride=4)
            b = b_ref[native, :]
            m = 1.0 / v_ref[pl.ds((i * lines + h * SUBS) * 4 + i, SUBS, stride=4), :]
            x = m * b
            bo_ref[i, rows, :] = b
            mo_ref[i, rows, :] = m
            x_ref[i, rows, :] = x
            for twice in range(2):
                pad_ref[pl.ds((twice * 4 + i) * lines + h * SUBS, SUBS), :] = x
    out_ref[...] = outgoing(
        lambda r: pad_ref[pl.ds(r, SUBS, stride=lines), :], lines, sends
    )


def fine_first(x_ref, b_ref, v_ref, c_ref, r_ref, vo_ref, line_ref):
    lines = x_ref.shape[1]

    def values(k, i, j, h):
        start = ((k * 4 + i) * lines + h * SUBS) * 4 + j
        tile = v_ref[pl.ds(start, SUBS, stride=4), :]
        vo_ref[k, i, j, pl.ds(h * SUBS, SUBS), :] = tile
        return tile

    fine_product(values, x_ref, b_ref, c_ref, r_ref, line_ref)


def fine_local(x_ref, b_ref, v_ref, c_ref, r_ref, line_ref):
    def values(k, i, j, h):
        return v_ref[k, i, j, pl.ds(h * SUBS, SUBS), :]

    fine_product(values, x_ref, b_ref, c_ref, r_ref, line_ref)


def fine_product(values, x_ref, b_ref, c_ref, r_ref, line_ref):
    lines = x_ref.shape[1]
    halves = lines // SUBS
    for j in range(4):
        for r in range(lines):
            line_ref[j, r] = wide(x_ref[j, pl.ds(r, 1), :])
    acc = []
    for h in range(halves):
        rows = pl.ds(h * SUBS, SUBS)
        for i in range(4):
            total = b_ref[i, rows, :]
            for j in range(4):
                total = total - values(0, i, j, h) * x_ref[j, rows, :]
            acc.append(total)

    def body(k, acc):
        acc = list(acc)
        for h in range(halves):
            rows = pl.ds(h * SUBS, SUBS)
            col = c_ref[k, rows, :]
            high, lane = col >> 7, col & (LANES - 1)
            for j in range(4):
                got = pick_lines([line_ref[j, r] for r in range(lines)], high, lane)
                for i in range(4):
                    acc[4 * h + i] = acc[4 * h + i] - values(k, i, j, h) * got
        return tuple(acc)

    acc = lax.fori_loop(1, NNZ, body, tuple(acc))
    for h in range(halves):
        for i in range(4):
            r_ref[i, pl.ds(h * SUBS, SUBS), :] = acc[4 * h + i]


def fine_remote(arrivals, r_ref, v_ref, c_ref, edge_ref, axis):
    lines = r_ref.shape[1]
    halves = lines // SUBS
    edge_lines(arrivals, edge_ref)
    edges = [wide(edge_ref[pl.ds(4 * axis + j, 1), :]) for j in range(4)]
    result = []
    for h in range(halves):
        rows = pl.ds(h * SUBS, SUBS)
        acc = [r_ref[i, rows, :] for i in range(4)]
        for k in range(1, NNZ):
            col = c_ref[k, rows, :]
            here, lane = (col >> 7) == lines + axis, col & (LANES - 1)
            for j in range(4):
                got = jnp.where(here, pick(edges[j], lane), 0.0)
                for i in range(4):
                    acc[i] = acc[i] - v_ref[k, i, j, rows, :] * got
        result.append(acc)
    return result


def fine_stream(*refs):
    r_ref, v_ref, c_ref, ro_ref, edge_ref = refs[3:]
    resid = fine_remote(refs[:3], r_ref, v_ref, c_ref, edge_ref, 0)
    for h, acc in enumerate(resid):
        for i in range(4):
            ro_ref[i, pl.ds(h * SUBS, SUBS), :] = acc[i]


def fine_step(factors, last, *refs):
    arrivals = refs[:3]
    r_ref, v_ref, c_ref, m_ref, x_ref, d_ref, s_ref, xo_ref, out_ref = refs[3:12]
    do_ref = refs[12] if last is False else None
    edge_ref, pad_ref = refs[-2:]
    keep, gain = factors
    lines = r_ref.shape[1]
    resid = fine_remote(arrivals, r_ref, v_ref, c_ref, edge_ref, 1)
    for h in range(lines // SUBS):
        rows = pl.ds(h * SUBS, SUBS)
        for i in range(4):
            d = gain * (m_ref[i, rows, :] * resid[h][i])
            if keep:
                d = keep * d_ref[i, rows, :] + d
            x = x_ref[i, rows, :] + d
            if not last:
                do_ref[i, rows, :] = d
            xo_ref[i, rows, :] = x
            for twice in range(2):
                pad_ref[pl.ds((twice * 4 + i) * lines + h * SUBS, SUBS), :] = x
    out_ref[...] = outgoing(
        lambda r: pad_ref[pl.ds(r, SUBS, stride=lines), :], lines, s_ref[...]
    )


def fine_finish(*refs):
    arrivals = refs[:3]
    r_ref, v_ref, c_ref, x_ref, so_ref, ro_ref, edge_ref = refs[3:]
    lines = r_ref.shape[1]
    resid = fine_remote(arrivals, r_ref, v_ref, c_ref, edge_ref, 1)
    for h in range(lines // SUBS):
        for i in range(4):
            native = pl.ds(h * SUBS * 4 + i, SUBS, stride=4)
            so_ref[native, :] = x_ref[i, pl.ds(h * SUBS, SUBS), :]
            ro_ref[native, :] = resid[h][i]


def fine_restrict(*refs):
    arrivals = refs[:3]
    (r_ref, v_ref, c_ref, w_ref, p_ref, m2_ref, s2_ref, b2_ref, x2_ref, out_ref, edge_ref, line_ref, pad_ref) = refs[3:]
    lines = r_ref.shape[1]
    resid = fine_remote(arrivals, r_ref, v_ref, c_ref, edge_ref, 1)
    for h in range(lines // SUBS):
        rows = pl.ds(h * SUBS, SUBS)
        for j in range(4):
            total = w_ref[0, j, rows, :] * resid[h][0]
            for i in range(1, 4):
                total = total + w_ref[i, j, rows, :] * resid[h][i]
            line_ref[j, rows, :] = total
    for j in range(4):
        total = None
        source = [wide(line_ref[j, pl.ds(r, 1), :]) for r in range(lines)]
        for part in range(2):
            place = p_ref[part]
            got = pick_lines(source, place >> 7, place & (LANES - 1))
            total = got if total is None else total + got
        b2 = duplicate(total)
        x2 = m2_ref[j] * b2
        b2_ref[j] = b2
        x2_ref[j] = x2
        middle_pad(pad_ref, j, x2)
    middle_out(out_ref, pad_ref, s2_ref)


def inverse_order(o_row, lines):
    count = lines * LANES
    high, lane = o_row >> 7, o_row & (LANES - 1)
    coarse = lax.broadcasted_iota(I32, (1, count), 1) >> 2
    here = lax.broadcasted_iota(I32, (lines, count), 0) == high
    upper = jnp.where(here, (coarse >> 4).astype(F32), 0.0)
    lower = jnp.where(here, (coarse & 15).astype(F32), 0.0)
    left = jnp.concatenate([upper, lower], axis=0).astype(jnp.bfloat16)
    right = jnp.where(
        lax.broadcasted_iota(I32, (LANES, count), 0) == lane, 1.0, 0.0
    ).astype(jnp.bfloat16)
    found = lax.dot_general(
        left, right, (((1,), (1,)), ((), ())), preferred_element_type=F32
    )
    return (found[:lines] * 16.0 + found[lines:]).astype(I32)


def pick_order(sources, unit):
    lane = tile_iota(1)
    place = 4 * (lane & 31) + unit
    result = jnp.zeros((SUBS, LANES), I32)
    for q, source in enumerate(sources):
        result = jnp.where((lane >> 5) == q, pick(source, place), result)
    return result


def fine_tables(w_ref, o_ref, v2_ref, _, wo_ref, place_ref, m2_ref):
    lines = o_ref.shape[0]
    for i in range(4):
        for j in range(4):
            for h in range(lines // SUBS):
                start = (i * lines + h * SUBS) * 4 + j
                wo_ref[i, j, pl.ds(h * SUBS, SUBS), :] = w_ref[pl.ds(start, SUBS, stride=4), :]
    sources = []
    for q in range(4):
        four = o_ref[pl.ds(q, 4, stride=4), :]
        sources.append(jnp.concatenate([four, four], axis=0))
    for part in range(2):
        place_ref[part] = pick_order(sources, (tile_iota(0) >> 2) + 2 * part)
    for i in range(4):
        four = 1.0 / v2_ref[pl.ds(i * 16 + i, 4, stride=4), :]
        m2_ref[i, pl.ds(0, 4), :] = four
        m2_ref[i, pl.ds(4, 4), :] = four


def fine_inverse(row_ref, _, agg_ref):
    agg_ref[...] = inverse_order(row_ref[...], agg_ref.shape[0])


def middle_blocks(v_ref, c_ref, _, vo_ref, co_ref):
    def body(ki, carry):
        k, i = ki // 4, ki % 4
        for j in range(4):
            for odd in range(2):
                start = ((2 * k + odd) * 4 + i) * 16 + j
                vo_ref[k, i, j, pl.ds(4 * odd, 4), :] = v_ref[pl.ds(start, 4, stride=4), :]
        return carry

    lax.fori_loop(0, NNZ // 2 * 4, body, 0)
    for k in range(NNZ // 2):
        for odd in range(2):
            co_ref[k, pl.ds(4 * odd, 4), :] = c_ref[pl.ds(2 * k + odd, 4, stride=NNZ), :]


def middle_tables(w_ref, row_ref, o_ref, _, wo_ref, agg_ref, place_ref):
    lines = o_ref.shape[0]
    for i in range(4):
        for j in range(4):
            four = w_ref[pl.ds(i * lines * 4 + j, 4, stride=4), :]
            wo_ref[i, j, pl.ds(0, 4), :] = four
            wo_ref[i, j, pl.ds(4, 4), :] = four
    agg = inverse_order(row_ref[...], lines)
    agg_ref[...] = jnp.concatenate([agg, agg], axis=0)
    sources = [wide(o_ref[pl.ds(q, 1), :]) for q in range(4)]
    place_ref[...] = pick_order(sources, tile_iota(0) & 3)


def middle_pad(pad_ref, j, x):
    for twice in range(2):
        pad_ref[pl.ds((twice * 4 + j) * SUBS, SUBS), :] = x


def middle_out(out_ref, pad_ref, s_ref):
    out_ref[...] = outgoing(
        lambda r: pad_ref[pl.ds(r, SUBS, stride=SUBS), :], 4, s_ref[...]
    )


def middle_local(x_ref, v_ref, c_ref, a_ref):
    acc = [jnp.zeros((SUBS, LANES), F32) for _ in range(4)]
    for j in range(4):
        source = [wide(x_ref[j, pl.ds(r, 1), :]) for r in range(4)]
        for kp in range(NNZ // 2):
            col = c_ref[kp]
            got = pick_lines(source, col >> 7, col & (LANES - 1))
            for i in range(4):
                acc[i] = acc[i] + v_ref[kp, i, j] * got
    for i in range(4):
        a_ref[i] = acc[i]


def middle_residual(arrivals, b_ref, a_ref, v_ref, c_ref, edge_ref):
    halo_lines(arrivals, edge_ref)
    acc = [a_ref[i] for i in range(4)]
    for j in range(4):
        source = [wide(edge_ref[pl.ds(4 * e + j, 1), :]) for e in range(2)]
        for kp in range(NNZ // 2):
            col = c_ref[kp]
            got = pick_lines(source, col >> 7, col & (LANES - 1), 4)
            for i in range(4):
                acc[i] = acc[i] + v_ref[kp, i, j] * got
    return [b_ref[i] - duplicate(acc[i]) for i in range(4)]


def middle_update(factors, resid, m_ref, x_ref, d_ref):
    keep, gain = factors
    xs, ds = [], []
    for i in range(4):
        d = gain * (m_ref[i] * resid[i])
        if keep:
            d = keep * d_ref[i] + d
        ds.append(d)
        xs.append(x_ref[i] + d)
    return xs, ds


def middle_step(factors, last, *refs):
    arrivals = refs[:5]
    b_ref, a_ref, m_ref, x_ref, d_ref, v_ref, c_ref, s_ref, xo_ref, out_ref = refs[5:15]
    do_ref = refs[15] if last is False else None
    edge_ref, pad_ref = refs[-2:]
    resid = middle_residual(arrivals, b_ref, a_ref, v_ref, c_ref, edge_ref)
    xs, ds = middle_update(factors, resid, m_ref, x_ref, d_ref)
    for i in range(4):
        xo_ref[i] = xs[i]
        if not last:
            do_ref[i] = ds[i]
        middle_pad(pad_ref, i, xs[i])
    middle_out(out_ref, pad_ref, s_ref)


def middle_restrict(*refs):
    arrivals = refs[:5]
    b_ref, a_ref, v_ref, c_ref, w_ref, p_ref, out_ref, edge_ref, line_ref = refs[5:]
    resid = middle_residual(arrivals, b_ref, a_ref, v_ref, c_ref, edge_ref)
    place = p_ref[...]
    high, lane = place >> 7, place & (LANES - 1)
    for j in range(4):
        total = w_ref[0, j] * resid[0]
        for i in range(1, 4):
            total = total + w_ref[i, j] * resid[i]
        line_ref[j] = total
        source = [wide(line_ref[j, pl.ds(r, 1), :]) for r in range(4)]
        got = pick_lines(source, high, lane)
        got = got + pltpu.roll(got, 2, 0)
        got = got + pltpu.roll(got, 1, 0)
        out_ref[pl.ds(j, 1), :] = got[0:1]
        out_ref[pl.ds(4 + j, 1), :] = got[0:1]


def middle_prolong(factors, *refs):
    arrivals = refs[:5]
    (b_ref, a_ref, m_ref, x_ref, d_ref, v_ref, c_ref, x1_ref, w_ref, agg_ref, s_ref, xo_ref, out_ref, edge_ref, line_ref, pad_ref) = refs[5:]
    lines = x1_ref.shape[1]
    resid = middle_residual(arrivals, b_ref, a_ref, v_ref, c_ref, edge_ref)
    xs, _ = middle_update(factors, resid, m_ref, x_ref, d_ref)
    for j in range(4):
        line_ref[j] = xs[j]
    for h in range(lines // SUBS):
        rows = pl.ds(h * SUBS, SUBS)
        agg = agg_ref[rows, :]
        high, lane = agg >> 7, agg & (LANES - 1)
        spread = [
            pick_lines([wide(line_ref[j, pl.ds(r, 1), :]) for r in range(4)], high, lane)
            for j in range(4)
        ]
        for i in range(4):
            placed = w_ref[i, 0, rows, :] * spread[0]
            for j in range(1, 4):
                placed = placed + w_ref[i, j, rows, :] * spread[j]
            x = x1_ref[i, rows, :] + placed
            xo_ref[i, rows, :] = x
            for twice in range(2):
                pad_ref[pl.ds((twice * 4 + i) * lines + h * SUBS, SUBS), :] = x
    out_ref[...] = outgoing(
        lambda r: pad_ref[pl.ds(r, SUBS, stride=lines), :], lines, s_ref[...]
    )


def coarse_tables(group, *refs):
    vo_ref, co_ref, mo_ref, pad_ref = refs[-4:]
    me = refs[0][0]
    for piece, places in zip(refs[1:-5], span_places(group)):
        for t, place in enumerate(places):
            pad_ref[place] = piece[t]
    for h in range(group // SUBS):
        rows = pl.ds(h * SUBS, SUBS)
        for ki in range(NNZ * 4):
            k, i = ki // 4, ki % 4
            for j in range(4):
                tile = pad_ref[rows, ki * 4 + j, :]
                vo_ref[k, i, j, rows, :] = tile
                if k == 0 and i == j:
                    mo_ref[i, rows, :] = 1.0 / tile
        for k in range(NNZ):
            col = pad_ref[rows, NNZ * 16 + k, :].astype(I32)
            co_ref[k, rows, :] = ((col >> 7) ^ me) * LANES + (col & (LANES - 1))


def coarse_solve(group, *refs):
    (v_ref, c_ref, m_ref, x2_ref, w_ref, agg_ref, s_ref, xo_ref, out_ref, b_ref, x_ref, d_ref, pad_ref) = refs[-13:]
    first = [0] + list(range(group - 1, 1, -2))
    for swapped, piece in enumerate(refs[:-13]):
        for t, place in enumerate([m ^ swapped for m in first]):
            for j in range(4):
                b_ref[j, pl.ds(place, 1), :] = piece[t, pl.ds(j, 1), :]
    blocks = group // SUBS
    for j in range(4):
        first = m_ref[j] * b_ref[j]
        x_ref[j] = first
        d_ref[j] = first
    for keep, gain in cheb_factors(KC)[1:]:
        resid = []
        for h in range(blocks):
            rows = pl.ds(h * SUBS, SUBS)
            acc = [b_ref[i, rows, :] for i in range(4)]
            for k in range(NNZ):
                col = c_ref[k, rows, :]
                high, lane = col >> 7, col & (LANES - 1)
                for j in range(4):
                    if k:
                        got = pick_lines(
                            [wide(x_ref[j, pl.ds(r, 1), :]) for r in range(group)], high, lane
                        )
                    else:
                        got = x_ref[j, rows, :]
                    for i in range(4):
                        acc[i] = acc[i] - v_ref[k, i, j, rows, :] * got
            resid.append(acc)
        for h in range(blocks):
            rows = pl.ds(h * SUBS, SUBS)
            for i in range(4):
                d = keep * d_ref[i, rows, :] + gain * (m_ref[i, rows, :] * resid[h][i])
                d_ref[i, rows, :] = d
                x_ref[i, rows, :] = x_ref[i, rows, :] + d
    lane = agg_ref[...]
    spread = [pick(wide(x_ref[j, pl.ds(0, 1), :]), lane) for j in range(4)]
    for i in range(4):
        x = x2_ref[i]
        for j in range(4):
            x = x + w_ref[i, j] * spread[j]
        xo_ref[i] = x
        middle_pad(pad_ref, i, x)
    middle_out(out_ref, pad_ref, s_ref)


def call(body, outs, args, scratch=(), free=(), smem=(), hbm=(), limit=16):
    specs = []
    for index in range(len(args)):
        if index in hbm:
            specs.append(pl.BlockSpec(memory_space=pltpu.HBM))
        elif index in free:
            specs.append(pl.BlockSpec(memory_space=pl.ANY))
        elif index in smem:
            specs.append(pl.BlockSpec(memory_space=pltpu.SMEM))
        else:
            specs.append(pl.BlockSpec(memory_space=pltpu.VMEM))
    single = not isinstance(outs, (list, tuple))
    shapes = [outs] if single else list(outs)
    result = pl.pallas_call(
        body,
        out_shape=shapes,
        in_specs=specs,
        out_specs=[pl.BlockSpec(memory_space=pltpu.VMEM) for _ in shapes],
        scratch_shapes=list(scratch),
        compiler_params=pltpu.CompilerParams(vmem_limit_bytes=limit * 2**20),
    )(*args)
    return result[0] if single else result


def shape(*dims, dtype=F32):
    return jax.ShapeDtypeStruct(dims, dtype)


def vmem(*dims, dtype=F32):
    return pltpu.VMEM(dims, dtype)


def native_rows(x):
    lines = x.shape[-1] // LANES
    split = x.reshape(x.shape[:-1] + (lines, LANES))
    return jnp.swapaxes(split, -2, -3).reshape(-1, LANES)


def from_native(rows, lines):
    return jnp.swapaxes(rows.reshape(lines, 4, LANES), 0, 1).reshape(4, lines * LANES)


def exchange(mesh, out, which):
    slabs, count = mesh.shape["stream"], mesh.shape["span"]

    def swap(partner):
        pairs = []
        for a in range(slabs):
            for b in range(count):
                to_a, to_b = partner(a, b)
                pairs.append((a * count + b, to_a * count + to_b))
        return lax.ppermute(out, AXES, pairs)

    def odd(index):
        return index + 1 if index % 2 else index - 1

    def span_odd(a, b):
        return (a, odd(b)) if 0 <= odd(b) < count else (a ^ 1, b)

    partners = [
        lambda a, b: (odd(a) % slabs, b),
        lambda a, b: (a ^ 1, b),
        span_odd,
        lambda a, b: (a, b ^ 1),
    ]
    return [swap(partner) for partner in partners] + [which]


def halo_choice(a, b, count):
    row, lane = (lax.broadcasted_iota(I32, (SUBS, LANES), d) for d in range(2))
    left = lane < LANES // 2
    index = jnp.where(row < 4, a, b)
    even = left == (index % 2 == 1)
    outside = (row >= 4) & jnp.where(left, b == 0, b == count - 1)
    return jnp.where(outside, 0, jnp.where(even, 1, 2)).astype(I32)


def span_places(group):
    places = [[0]]
    mask = group // 2
    while mask:
        places.append([(mask | 1) ^ m for piece in places for m in piece])
        mask //= 2
    return places


def span_swap(mesh, value, mask):
    slabs, count = mesh.shape["stream"], mesh.shape["span"]
    pairs = [
        (a * count + b, a * count + (b ^ mask)) for a in range(slabs) for b in range(count)
    ]
    return lax.ppermute(value, AXES, pairs)


def span_stage(mesh, held, out):
    held, _ = lax.optimization_barrier((held, out))
    return span_swap(mesh, held, mesh.shape["span"] // 2 // held.shape[0] | 1)


def join_kernel(*refs):
    place = 0
    for piece in refs[:-1]:
        for t in range(piece.shape[0]):
            refs[-1][place] = piece[t]
            place += 1


def join(pieces):
    count = sum(piece.shape[0] for piece in pieces)
    return call(join_kernel, shape(count, *pieces[0].shape[1:]), pieces)


def span_gather(mesh, value):
    masks = range(mesh.shape["span"] - 1, 1, -2)
    held = jnp.stack([value] + [span_swap(mesh, value, m) for m in masks])
    return [held, span_swap(mesh, held, 1)]


def per_device(mesh, right_side, fine_values, fine_columns, fine_sends, fine_order, fine_weights, middle_values, middle_columns, middle_sends, middle_order, middle_weights, coarsest_values, coarsest_columns):
    group = mesh.shape["span"]
    lines = right_side.shape[1] // LANES
    tile = shape(SUBS, LANES)
    vec1 = shape(4, lines, LANES)
    vec2 = shape(4, SUBS, LANES)
    edge = vmem(SUBS, LANES)
    pad1 = vmem(SUBS * lines, LANES)
    pad2 = vmem(SUBS * SUBS, LANES)
    factors = cheb_factors(KSM)
    me = lax.axis_index("span").astype(I32)
    choice = halo_choice(lax.axis_index("stream").astype(I32), me, group)
    values1 = native_rows(fine_values)
    values2 = native_rows(middle_values)

    starts = [
        values1,
        native_rows(right_side),
        fine_sends,
        middle_sends,
        native_columns(fine_columns),
        coarsest_values.reshape(NNZ * 16, LANES),
        coarsest_columns,
    ]
    int_tile = shape(SUBS, LANES, dtype=I32)
    b1, m1, x1, send1, send2, c1, own3, out = call(
        fine_start,
        [
            vec1,
            vec1,
            vec1,
            int_tile,
            int_tile,
            shape(NNZ, lines, LANES, dtype=I32),
            shape(1, NNZ * 17, LANES),
            tile,
        ],
        [pltpu.with_memory_space_constraint(x, pltpu.HBM) for x in starts],
        [pad1, vmem(16 * lines, LANES)]
        + [vmem(*x.shape, dtype=x.dtype) for x in starts[1:]]
        + [pltpu.SemaphoreType.DMA((len(starts),))],
        hbm=range(len(starts)),
    )
    d1 = x1

    arrived = exchange(mesh, out, choice)
    pieces3 = [own3, span_stage(mesh, own3, out)]
    resid, v1 = call(
        fine_first,
        [vec1, shape(NNZ, 4, 4, lines, LANES)],
        [x1, b1, values1, c1],
        [vmem(4, lines, SUBS, LANES)],
    )

    def fine_part(x):
        return call(fine_local, vec1, [x, b1, v1, c1], [vmem(4, lines, SUBS, LANES)])

    def fine_half(arrived, resid):
        args = [arrived[0], arrived[3], arrived[1], arrived[4], resid, v1, c1]
        return call(
            lambda *refs: fine_stream(*(refs[:1] + refs[2:])), vec1, args, [edge], free=(1,)
        )

    def fine_next(which, arrived, resid, x, d, after=()):
        args = arrived[2:] + [fine_half(arrived, resid), v1, c1, m1, x, d, send1]
        last = which == KSM - 1
        result = call(
            lambda *refs: fine_step(
                factors[which], last, *(refs[: len(args)] + refs[len(args) + len(after) :])
            ),
            [vec1, tile] + ([] if last else [vec1]),
            args + list(after),
            [edge, pad1],
            free=range(len(args), len(args) + len(after)),
        )
        return result[0], (None if last else result[2]), result[1]

    x1, d1, out = fine_next(1, arrived, resid, x1, d1)

    arrived = exchange(mesh, out, choice)
    resid = fine_part(x1)
    w1, place1, m2 = call(
        fine_tables,
        [
            shape(4, 4, lines, LANES),
            shape(2, SUBS, LANES, dtype=I32),
            vec2,
        ],
        [native_rows(fine_weights), fine_order.reshape(lines, LANES), values2, out],
        free=(3,),
    )
    x1, d1, out = fine_next(2, arrived, resid, x1, d1, [m2])

    arrived = exchange(mesh, out, choice)
    resid = fine_part(x1)
    held3 = join(pieces3)
    b2, x2, out = call(
        lambda *refs: fine_restrict(*(refs[:10] + refs[11:])),
        [vec2, vec2, tile],
        arrived[2:] + [fine_half(arrived, resid), v1, c1, w1, place1, m2, send2, held3],
        [edge, vmem(4, lines, LANES), pad2],
        free=(10,),
    )
    d2 = x2

    def middle_part(x):
        return call(middle_local, vec2, [x, v2, c2])

    def middle_next(which, arrived, x, d, after=()):
        args = arrived + [b2, middle_part(x), m2, x, d, v2, c2, send2]
        last = which == KSM - 1
        result = call(
            lambda *refs: middle_step(
                factors[which], last, *(refs[: len(args)] + refs[len(args) + len(after) :])
            ),
            [vec2, tile] + ([] if last else [vec2]),
            args + list(after),
            [edge, pad2],
            free=range(len(args), len(args) + len(after)),
        )
        return result[0], (None if last else result[2]), result[1]

    arrived = exchange(mesh, out, choice)
    for _ in range(len(span_places(group)) - 4):
        pieces3.append(span_stage(mesh, held3, out))
        held3 = join(pieces3)
    pieces3.append(span_stage(mesh, held3, out))
    v2, c2 = call(
        middle_blocks,
        [shape(NNZ // 2, 4, 4, SUBS, LANES), shape(NNZ // 2, SUBS, LANES, dtype=I32)],
        [values2, native_columns(middle_columns), out],
        free=(2,),
    )
    x2, d2, out = middle_next(1, arrived, x2, d2)

    arrived = exchange(mesh, out, choice)
    w2, agg2, place2 = call(
        middle_tables,
        [
            shape(4, 4, SUBS, LANES),
            shape(SUBS, LANES, dtype=I32),
            shape(SUBS, LANES, dtype=I32),
        ],
        [native_rows(middle_weights), middle_order, middle_order.reshape(-1, LANES), out],
        free=(3,),
    )
    x2, d2, out = middle_next(2, arrived, x2, d2, [agg2])

    arrived = exchange(mesh, out, choice)
    held3 = join(pieces3)
    agg1 = call(fine_inverse, shape(lines, LANES, dtype=I32), [fine_order, out], free=(1,))
    rhs3 = call(
        lambda *refs: middle_restrict(*(refs[:11] + refs[13:])),
        tile,
        arrived + [b2, middle_part(x2), v2, c2, w2, place2, agg1, held3],
        [edge, vmem(4, SUBS, LANES)],
        free=(11, 12),
    )
    pieces3.append(span_stage(mesh, held3, rhs3))
    v3, c3, m3 = call(
        lambda *refs: coarse_tables(group, *refs),
        [shape(NNZ, 4, 4, group, LANES), shape(NNZ, group, LANES, dtype=I32), shape(4, group, LANES)],
        [me.reshape(1)] + pieces3 + [rhs3],
        [vmem(group, NNZ * 17, LANES)],
        free=(1 + len(pieces3),),
        smem=(0,),
    )
    vec3 = vmem(4, group, LANES)
    x2, out = call(
        lambda *refs: coarse_solve(group, *refs),
        [vec2, tile],
        span_gather(mesh, rhs3) + [v3, c3, m3, x2, w2, agg2, send2],
        [vec3, vec3, vec3, pad2],
    )
    arrived = exchange(mesh, out, choice)
    x2, d2, out = middle_next(0, arrived, x2, x2)
    arrived = exchange(mesh, out, choice)
    x2, d2, out = middle_next(1, arrived, x2, d2)
    arrived = exchange(mesh, out, choice)
    x1, out = call(
        lambda *refs: middle_prolong(factors[2], *refs),
        [vec1, tile],
        arrived + [b2, middle_part(x2), m2, x2, d2, v2, c2, x1, w1, agg1, send1],
        [edge, vmem(4, SUBS, LANES), pad1],
    )
    d1 = x1
    for which in range(KSM):
        arrived = exchange(mesh, out, choice)
        resid = fine_part(x1)
        x1, d1, out = fine_next(which, arrived, resid, x1, d1)
    arrived = exchange(mesh, out, choice)
    resid = fine_part(x1)
    rows = shape(4 * lines, LANES)
    resid = fine_half(arrived, resid)
    solved, left = call(fine_finish, [rows, rows], arrived[2:] + [resid, v1, c1, x1], [edge])
    return from_native(solved, lines), from_native(left, lines)


def native_columns(columns):
    lines = columns.shape[1] // LANES
    return jnp.swapaxes(columns.reshape(NNZ, lines, LANES), 0, 1).reshape(-1, LANES)


def solution(mesh):
    both = ("stream", "span")
    in_specs = (
        P(None, both),
        P(None, None, None, both),
        P(None, both),
        P(None, both),
        P(both, None),
        P(None, None, both),
        P(None, None, None, both),
        P(None, both),
        P(None, both),
        P(both, None),
        P(None, None, both),
        P(None, None, None, both),
        P(None, both),
    )
    return jax.shard_map(
        lambda *args: per_device(mesh, *args),
        mesh=mesh,
        in_specs=in_specs,
        out_specs=(P(None, both), P(None, both)),
        check_vma=False,
    )
```
